32 devices in a mesh: ty: 2 (over x), tx: 4 (over y, core), items: 4 (over z).
Axes of the slice: x: 2, y: 2, z: 4, core: 2. Of those that a mesh axis runs over, the one named last changes fastest.
Arguments:
- inputs: float32 [128, 32, 3072], P('items', 'ty', 'tx'), may hold values from -300 to 300
- regions: int32 [128, 32, 32], P('items', 'ty', 'tx'), may hold values from 0 to 8, as said below
- lead_step_index: int32 [128], P('items'), may hold values from 0 to 13
- running_channel_mean: float32 [96], replicated, may hold values from -3 to 3
- running_channel_variance: float32 [96], replicated, may hold values from 0.5 to 4
- query_key_value_weight: float32 [96, 288], replicated, may hold values from -0.625 to 0.625
- query_value_bias: float32 [2, 96], replicated, may hold values from -3 to 3
- log_cosine_scale: float32 [3], replicated, may hold values from 1.8 to 2.6
- bias_net_weight1: float32 [2, 512], replicated, may hold values from -4 to 4
- bias_net_bias1: float32 [512], replicated, may hold values from -3 to 3
- bias_net_weight2: float32 [512, 3], replicated, may hold values from -0.125 to 0.125
- output_weight: float32 [96, 96], replicated, may hold values from -0.625 to 0.625
- projection_bias: float32 [96], replicated, may hold values from -3 to 3
- up_weight: float32 [96, 384], replicated, may hold values from -0.625 to 0.625
- up_bias: float32 [384], replicated, may hold values from -3 to 3
- down_weight: float32 [96, 384], replicated, may hold values from -0.3125 to 0.3125
- down_bias: float32 [96], replicated, may hold values from -3 to 3
- conditioned_norm_values: float32 [2, 4, 96], replicated, may hold values from -2 to 2
- cotangent: float32 [128, 32, 3072], P('items', 'ty', 'tx'), may hold values from -6 to 6
Outputs:
- outputs: float32 [128, 32, 3072], P('items', 'ty', 'tx')
- grad_inputs: float32 [128, 32, 3072], P('items', 'ty', 'tx')
- grad_w_qkv: float32 [96, 288], replicated
- grad_qv_bias: float32 [2, 96], replicated
- grad_logit_scale: float32 [3], replicated
- grad_cpb_w1: float32 [2, 512], replicated
- grad_cpb_b1: float32 [512], replicated
- grad_cpb_w2: float32 [512, 3], replicated
- grad_w_out: float32 [96, 96], replicated
- grad_b_out: float32 [96], replicated
- grad_w_up: float32 [96, 384], replicated
- grad_b_up: float32 [384], replicated
- grad_w_down: float32 [96, 384], replicated
- grad_b_down: float32 [96], replicated
- grad_norm_params: float32 [2, 4, 96], replicated
- new_mean: float32 [96], replicated
- new_var: float32 [96], replicated
The draws below stay inside these ranges and needn't reach their ends.
Inputs may be any that keep to these rules, and one draw needn't show every extreme that they name: regions[b, r, c] = 3 * p + q. Along rows, an item is either wrapped (p = 0 for all rows) or cut (p = 0 for r < 24, 1 for r < 28, 2 for the rest); q likewise along columns with 32. Each item chooses for each dimension; some item is cut along both.
All inputs are finite; a program needn't handle non-finite values.
Results may differ from the reference program's by a relative error of at most 0.0003.
Values sent between devices are 32-bit elements; how exact they have to be, the bound alone decides.
No kernel may reach another device: no remote copies, remote signals or barrier semaphores. Data moves between devices by JAX's collectives and lax.ppermute only.
A program may use at most 128 MiB of HBM per device.

```python
import math
import jax
import jax.numpy as jnp
from jax import lax

ATTENTION_HEADS = 3
HEAD_DIM = 32
MLP_HIDDEN = 384
BIAS_NET_UNITS = 512
WINDOW = 8
SHIFT = 4
LEAD_STEPS = 14
WIDTH = 96
GRID_R = 32
GRID_C = 32
ITEMS = 128


def draw_inputs(key, part):
    key = jax.random.fold_in(key, 11)
    key_mean, key_scale, key_noise = jax.random.split(key, 3)
    chan_mean = 2.0 * jax.random.truncated_normal(key_mean, -3.0, 3.0, (WIDTH,), jnp.float32)
    chan_scale = jnp.exp(jax.random.uniform(key_scale, (WIDTH,), jnp.float32, 0.0, math.log(10.0)))
    rising = 3.0
    noise = jax.random.truncated_normal(key_noise, -3.0, 3.0, (ITEMS, GRID_R, GRID_C, WIDTH), jnp.float32)
    ladder = jnp.arange(ITEMS, dtype=jnp.float32) / max(ITEMS - 1, 1)
    item_scale = jnp.exp(math.log(rising) * ladder)
    field = chan_mean + item_scale[:, None, None, None] * chan_scale * noise
    return field.reshape(ITEMS, GRID_R, GRID_C * WIDTH)


def draw_regions(key, part):
    key = jax.random.fold_in(key, 23)
    key_flags, key_pick = jax.random.split(key)
    flags = jax.random.randint(key_flags, (ITEMS, 2), 0, 2)
    picked = jax.random.randint(key_pick, (), 0, ITEMS)
    open_edges = jnp.where(jnp.arange(ITEMS)[:, None] == picked, 1, 1 - flags).astype(jnp.int32)
    row_index = jnp.arange(GRID_R, dtype=jnp.int32)
    col_index = jnp.arange(GRID_C, dtype=jnp.int32)
    row_band = (row_index >= GRID_R - WINDOW).astype(jnp.int32) + (row_index >= GRID_R - SHIFT).astype(jnp.int32)
    col_band = (col_index >= GRID_C - WINDOW).astype(jnp.int32) + (col_index >= GRID_C - SHIFT).astype(jnp.int32)
    row_part = row_band[None, :, None] * open_edges[:, 0, None, None]
    col_part = col_band[None, None, :] * open_edges[:, 1, None, None]
    return (3 * row_part + col_part).astype(jnp.int32)


def set_ends(values, stream_key, low, high):
    spot = [jax.random.randint(jax.random.fold_in(stream_key, axis), (), 0, length) for axis, length in enumerate(values.shape)]
    widest = values.shape.index(max(values.shape))
    neighbour = spot[:widest] + [(spot[widest] + 1) % values.shape[widest]] + spot[widest + 1:]
    return values.at[tuple(spot)].set(low).at[tuple(neighbour)].set(high)


def steps_of(stream_key, dims, cuts, low, high):
    def one(position, shards_of):
        steps = jax.random.uniform(jax.random.fold_in(jax.random.fold_in(stream_key, 6), position), (shards_of,), jnp.float32, low / len(cuts), high / len(cuts))
        return jnp.repeat(jnp.exp(steps), dims[position] // shards_of).reshape((-1,) + (1,) * (len(dims) - position - 1))

    level = one(*cuts[0])
    for cut in cuts[1:]:
        level = level * one(*cut)
    return level


def scatter_about(rng, extent, scale, most, pieces=(), kind=jnp.bfloat16):
    loudness = steps_of(rng, extent, pieces, -0.22, 0.18) if pieces else 1.0
    entries = jax.random.normal(rng, extent, jnp.float32) * scale * loudness
    return jnp.minimum(jnp.maximum(entries, -most), most).astype(kind)


def setup_inputs(seed: int = 0) -> dict:
    arg_keys = jax.random.split(jax.random.key(seed), 20)
    return {
        "inputs": draw_inputs(jax.random.fold_in(arg_keys[19], 71), 0),
        "regions": draw_regions(jax.random.fold_in(arg_keys[19], 71), 0),
        "lead_step_index": set_ends(jax.random.randint(arg_keys[2], (ITEMS,), 0, LEAD_STEPS), jax.random.fold_in(arg_keys[2], 1), 0, LEAD_STEPS - 1).astype(jnp.int32),
        "running_channel_mean": scatter_about(arg_keys[3], (WIDTH,), 0.5, 3.0, (), jnp.float32),
        "running_channel_variance": jnp.clip(jnp.exp(jax.random.uniform(arg_keys[4], (WIDTH,), jnp.float32, math.log(0.5), math.log(4.0))), 0.5, 4.0),
        "query_key_value_weight": scatter_about(arg_keys[5], (WIDTH, 3 * WIDTH), WIDTH ** -0.5, 0.625, (), jnp.float32),
        "query_value_bias": scatter_about(arg_keys[6], (2, WIDTH), 0.5, 3.0, (), jnp.float32),
        "log_cosine_scale": jnp.clip(jax.random.uniform(arg_keys[7], (ATTENTION_HEADS,), jnp.float32, 1.8, 2.6), 1.8, 2.6),
        "bias_net_weight1": scatter_about(arg_keys[8], (2, BIAS_NET_UNITS), 1.0, 4.0, (), jnp.float32),
        "bias_net_bias1": scatter_about(arg_keys[9], (BIAS_NET_UNITS,), 0.5, 3.0, (), jnp.float32),
        "bias_net_weight2": scatter_about(arg_keys[10], (BIAS_NET_UNITS, ATTENTION_HEADS), (4 * BIAS_NET_UNITS) ** -0.5, 0.125, (), jnp.float32),
        "output_weight": scatter_about(arg_keys[11], (WIDTH, WIDTH), WIDTH ** -0.5, 0.625, (), jnp.float32),
        "projection_bias": scatter_about(arg_keys[12], (WIDTH,), 0.5, 3.0, (), jnp.float32),
        "up_weight": scatter_about(arg_keys[13], (WIDTH, MLP_HIDDEN), WIDTH ** -0.5, 0.625, (), jnp.float32),
        "up_bias": scatter_about(arg_keys[14], (MLP_HIDDEN,), 0.5, 3.0, (), jnp.float32),
        "down_weight": scatter_about(arg_keys[15], (WIDTH, MLP_HIDDEN), MLP_HIDDEN ** -0.5, 0.3125, (), jnp.float32),
        "down_bias": scatter_about(arg_keys[16], (WIDTH,), 0.5, 3.0, (), jnp.float32),
        "conditioned_norm_values": scatter_about(arg_keys[17], (2, 4, WIDTH), 0.3, 2.0, (), jnp.float32),
        "cotangent": scatter_about(arg_keys[18], (ITEMS, GRID_R, GRID_C * WIDTH), 1.0, 6.0, ((0, 4), (1, 2), (2, 4)), jnp.float32),
    }


precise_product = lax.Precision.HIGHEST
masked_score = -1000000000.0
norm_eps = 1e-05
unit_eps = 1e-06
momentum = 0.1

@jax.custom_vjp
def low(v):
    return lax.optimization_barrier(v.astype(jnp.bfloat16)).astype(jnp.float32)

@jax.custom_vjp
def low_back(v):
    return v

def low_keep(v):
    return (low(v), None)

def low_pass(kept, grad):
    return (grad,)

def back_keep(v):
    return (v, None)

def back_low(kept, grad):
    return (low(grad),)
low.defvjp(low_keep, low_pass)
low_back.defvjp(back_keep, back_low)

def windows_of(grid_field):
    batch_items, tile_rows, tile_cols = grid_field.shape[:3]
    trailing = grid_field.shape[3:]
    blocks = grid_field.reshape((batch_items, tile_rows // WINDOW, WINDOW, tile_cols // WINDOW, WINDOW) + trailing)
    return jnp.moveaxis(blocks, 3, 2).reshape((-1, WINDOW * WINDOW) + trailing)

def grid_of(window_field, batch_items, tile_rows, tile_cols):
    trailing = window_field.shape[2:]
    blocks = window_field.reshape((batch_items, tile_rows // WINDOW, tile_cols // WINDOW, WINDOW, WINDOW) + trailing)
    return jnp.moveaxis(blocks, 3, 2).reshape((batch_items, tile_rows, tile_cols) + trailing)

def relative_index():
    places = jnp.arange(WINDOW * WINDOW, dtype=jnp.int32)
    place_row = places // WINDOW
    place_col = places % WINDOW
    offset_row = place_row[:, None] - place_row[None, :] + WINDOW - 1
    offset_col = place_col[:, None] - place_col[None, :] + WINDOW - 1
    return (offset_row * (2 * WINDOW - 1) + offset_col).astype(jnp.int32)

def coordinate_table():
    offsets = jnp.arange((2 * WINDOW - 1) ** 2, dtype=jnp.int32)
    along_rows = (offsets // (2 * WINDOW - 1) - (WINDOW - 1)).astype(jnp.float32)
    along_cols = (offsets % (2 * WINDOW - 1) - (WINDOW - 1)).astype(jnp.float32)
    stacked = jnp.stack([along_rows, along_cols], -1) * (8.0 / (WINDOW - 1))
    return jnp.sign(stacked) * jnp.log2(jnp.abs(stacked) + 1.0) / 3.0

def position_bias_table(bias_net_weight1, bias_net_bias1, bias_net_weight2):
    hidden_units = jax.nn.gelu(jnp.dot(coordinate_table(), bias_net_weight1, precision=precise_product) + bias_net_bias1, approximate=False)
    bias_table = 16.0 * jax.nn.sigmoid(jnp.dot(hidden_units, bias_net_weight2, precision=precise_product))
    return jnp.transpose(bias_table[relative_index()], (2, 0, 1))

def unit_rows(field):
    return field * lax.rsqrt(lax.optimization_barrier(jnp.sum(field * field, -1, keepdims=True)) + unit_eps)

def heads_of(field):
    return field.reshape(field.shape[:-1] + (ATTENTION_HEADS, HEAD_DIM))

def project_heads(windowed, query_key_value_weight, query_value_bias):
    feature_count = windowed.shape[-1]
    joined = jnp.einsum('wtc,ce->wte', windowed, query_key_value_weight, precision=precise_product)
    queries = joined[..., :feature_count] + query_value_bias[0]
    keys_raw = joined[..., feature_count:2 * feature_count]
    values = joined[..., 2 * feature_count:] + query_value_bias[1]
    return (unit_rows(heads_of(queries)), unit_rows(heads_of(keys_raw)), heads_of(values))

def score_block(query_dir, key_dir, scale_head, relative_bias, same_region):
    cosine = jnp.einsum('wihd,wjhd->whij', query_dir, key_dir, precision=precise_product)
    scores = jnp.where(same_region, cosine * scale_head[None, :, None, None] + relative_bias[None], masked_score)
    return (cosine, scores)

def cond_norm(field, lead_time_value, params):
    centre = lax.optimization_barrier(jnp.mean(field, -1, keepdims=True))
    centred = field - centre
    spread = lax.optimization_barrier(jnp.mean(centred * centred, -1, keepdims=True))
    gain = 1.0 + params[0] + lead_time_value * params[1]
    return centred * lax.rsqrt(spread + norm_eps) * gain + params[2] + lead_time_value * params[3]

def post_block(back_rolled, normed, output_weight, projection_bias, up_weight, up_bias, down_weight, down_bias, conditioned_norm_values, lead_time_value):
    attn_out = jnp.einsum('brcd,de->brce', back_rolled, output_weight, precision=precise_product) + projection_bias
    first_sum = normed + cond_norm(attn_out, lead_time_value, conditioned_norm_values[0])
    hidden_units = jax.nn.gelu(jnp.einsum('brcd,de->brce', first_sum, up_weight, precision=precise_product) + up_bias, approximate=False)
    branch = jnp.einsum('brce,de->brcd', hidden_units, down_weight, precision=precise_product) + down_bias
    return first_sum + cond_norm(branch, lead_time_value, conditioned_norm_values[1])

def forward_block(inputs, query_key_value_weight, query_value_bias, log_cosine_scale, bias_net_weight1, bias_net_bias1, bias_net_weight2, output_weight, projection_bias, up_weight, up_bias, down_weight, down_bias, conditioned_norm_values, regions, lead_time_value):
    chan_mean = lax.optimization_barrier(jnp.mean(inputs, (0, 1, 2)))
    chan_var = lax.optimization_barrier(jnp.mean(jnp.square(inputs - chan_mean), (0, 1, 2)))
    normed = (inputs - chan_mean) * lax.rsqrt(chan_var + norm_eps)
    shifted = jnp.roll(normed, (-SHIFT, -SHIFT), (1, 2))
    batch_items, grid_rows, grid_cols = inputs.shape[:3]
    query_dir, key_dir, values = project_heads(windows_of(shifted), query_key_value_weight, query_value_bias)
    region_win = windows_of(regions)
    same_region = region_win[:, None, :, None] == region_win[:, None, None, :]
    relative_bias = position_bias_table(bias_net_weight1, bias_net_bias1, bias_net_weight2)
    cosine, scores = score_block(query_dir, key_dir, jnp.exp(log_cosine_scale), relative_bias, same_region)
    row_top = lax.optimization_barrier(jnp.max(scores, -1, keepdims=True))
    expo = jnp.exp(scores - row_top)
    attn_probs = expo / lax.optimization_barrier(jnp.sum(expo, -1, keepdims=True))
    mixed_win = jnp.einsum('whij,wjhd->wihd', attn_probs, values, precision=precise_product)
    mixed_win = mixed_win.reshape(mixed_win.shape[0], WINDOW * WINDOW, ATTENTION_HEADS * HEAD_DIM)
    mixed_out = grid_of(mixed_win, batch_items, grid_rows, grid_cols)
    back_rolled = jnp.roll(mixed_out, (SHIFT, SHIFT), (1, 2))
    outputs = post_block(back_rolled, normed, output_weight, projection_bias, up_weight, up_bias, down_weight, down_bias, conditioned_norm_values, lead_time_value)
    return (outputs, (chan_mean, chan_var))

def reference(inputs, regions, lead_step_index, running_channel_mean, running_channel_variance, query_key_value_weight, query_value_bias, log_cosine_scale, bias_net_weight1, bias_net_bias1, bias_net_weight2, output_weight, projection_bias, up_weight, up_bias, down_weight, down_bias, conditioned_norm_values, cotangent):
    lead_time_value = ((lead_step_index + 1).astype(jnp.float32) / LEAD_STEPS).reshape(-1, 1, 1, 1)
    flat_shape = inputs.shape
    feature_count = query_key_value_weight.shape[0]
    grid_shape = (flat_shape[0], flat_shape[1], flat_shape[2] // feature_count, feature_count)
    inputs = inputs.reshape(grid_shape)
    cotangent = cotangent.reshape(grid_shape)

    def wrapped_function(inputs, query_key_value_weight, query_value_bias, log_cosine_scale, bias_net_weight1, bias_net_bias1, bias_net_weight2, output_weight, projection_bias, up_weight, up_bias, down_weight, down_bias, conditioned_norm_values):
        return forward_block(inputs, query_key_value_weight, query_value_bias, log_cosine_scale, bias_net_weight1, bias_net_bias1, bias_net_weight2, output_weight, projection_bias, up_weight, up_bias, down_weight, down_bias, conditioned_norm_values, regions, lead_time_value)
    outputs, pullback_function, batch_statistics = jax.vjp(wrapped_function, inputs, query_key_value_weight, query_value_bias, log_cosine_scale, bias_net_weight1, bias_net_bias1, bias_net_weight2, output_weight, projection_bias, up_weight, up_bias, down_weight, down_bias, conditioned_norm_values, has_aux=True)
    grads = pullback_function(cotangent)
    chan_mean, chan_var = batch_statistics
    token_count = inputs.shape[0] * inputs.shape[1] * inputs.shape[2]
    new_mean = (1.0 - momentum) * running_channel_mean + momentum * chan_mean
    new_var = (1.0 - momentum) * running_channel_variance + momentum * chan_var * (token_count / (token_count - 1.0))
    return (outputs.reshape(flat_shape), grads[0].reshape(flat_shape), grads[1], grads[2], grads[3], grads[4], grads[5], grads[6], grads[7], grads[8], grads[9], grads[10], grads[11], grads[12], grads[13], new_mean, new_var)
```

```python
from functools import partial

import jax
import jax.numpy as jnp
from jax import lax
from jax.experimental import pallas as pl
from jax.experimental.pallas import tpu as pltpu
from jax.sharding import PartitionSpec as P

HEADS = 3
HEAD_DIM = 32
WIDTH = 96
HIDDEN = 384
WINDOW = 8
SHIFT = 4
LEAD_STEPS = 14
PLACES = WINDOW * WINDOW
SPAN = 2 * WINDOW - 1
PAIR = 2 * PLACES
LANES = 128

masked_score = -1000000000.0
norm_eps = 1e-05
unit_eps = 1e-06
momentum = 0.1
axes_all = ("ty", "tx", "items")

f32 = jnp.float32
bf16 = jnp.bfloat16

normal_slope = 0.28
normal_poly = (
    0.11652074430372011,
    0.06749697235753221,
    0.26890961436457633,
    -0.23699279280357777,
    0.389873590681989,
    -0.10580813816203069,
)


def dot(a, b):
    return lax.dot_general(a, b, (((1,), (0,)), ((), ())), preferred_element_type=f32)


def dot_rows(a, b):
    return lax.dot_general(a, b, (((1,), (1,)), ((), ())), preferred_element_type=f32)


def split(x):
    hi = x.astype(bf16)
    return hi, (x - hi.astype(f32)).astype(bf16)


def normal_parts(u):
    a = jnp.abs(u)
    t = 1.0 / (1.0 + normal_slope * a)
    bell = jnp.exp(-0.5 * u * u)
    poly = normal_poly[-1] * t + normal_poly[-2]
    for c in normal_poly[-3::-1]:
        poly = poly * t + c
    tail = poly * t * bell
    return jnp.where(u < 0, tail, 1.0 - tail), bell * 0.3989422804014327


def stats_kernel(x_ref, out_ref):
    items, rows, flat = x_ref.shape
    cols = flat // WIDTH
    count = items * rows * cols

    def fold(v):
        total = v[:, :WIDTH]
        for j in range(1, cols):
            total = total + v[:, j * WIDTH : (j + 1) * WIDTH]
        return jnp.sum(total, 0, keepdims=True)

    def add(i, acc):
        return acc + x_ref[i, 0:8, :] + x_ref[i, 8:16, :]

    zero = jnp.zeros((8, flat), f32)
    mean = fold(lax.fori_loop(0, items, add, zero)) * (1.0 / count)
    spread = jnp.concatenate([mean] * cols, 1)

    def add_square(i, acc):
        lo = x_ref[i, 0:8, :] - spread
        hi = x_ref[i, 8:16, :] - spread
        return acc + lo * lo + hi * hi

    square = fold(lax.fori_loop(0, items, add_square, zero))
    out_ref[...] = jnp.concatenate(
        [mean, square, jnp.zeros((6, WIDTH), f32)], 0
    )


def local_stats(x):
    return pl.pallas_call(
        stats_kernel,
        out_shape=jax.ShapeDtypeStruct((8, WIDTH), f32),
        compiler_params=pltpu.CompilerParams(vmem_limit_bytes=32 * 1024 * 1024),
    )(x)


def stack_rows(hi, lo):
    return jnp.concatenate([hi, lo], 0)


def block_kernel(
    step_items,
    flags_ref,
    lead_ref,
    x_own,
    x_right,
    x_down,
    x_corner,
    ct_own,
    ct_right,
    ct_down,
    ct_corner,
    affine_ref,
    w_qkv_ref,
    w_out_ref,
    w_up_ref,
    w_down_ref,
    cols_ref,
    up_bias_ref,
    scale_ref,
    bias_ref,
    out_lo,
    out_ld,
    out_ro,
    out_rd,
    dn_lo,
    dn_ld,
    dn_ro,
    dn_rd,
    g_qkv_ref,
    g_out_ref,
    g_up_ref,
    g_down_ref,
    sums_ref,
    dpos_ref,
    dcos_ref,
    qkv_f,
    out_f,
    up_f,
    down_f,
    down_b,
    up_b,
    out_b,
    qkv_b,
    down_f_hi,
    up_b_hi,
    qkv_b_hi,
):
    step = pl.program_id(0)
    last = pl.num_programs(0) - 1

    def packed(w):
        hi, lo = split(w)
        return jnp.concatenate(
            [jnp.concatenate([hi, hi], 1), jnp.concatenate([lo, jnp.zeros_like(lo)], 1)], 0
        )

    @pl.when(step == 0)
    def _():
        w = w_qkv_ref[...]
        qkv_f[...] = packed(w.T)
        hi, lo = split(w)
        qkv_b[...] = stack_rows(hi, lo)
        qkv_b_hi[...] = hi
        w = w_out_ref[...]
        out_f[...] = packed(w.T)
        out_b[...] = packed(w)
        w = w_up_ref[...]
        up_f[...] = packed(w.T)
        hi, lo = split(w)
        up_b[...] = stack_rows(hi, lo)
        up_b_hi[...] = hi
        w = w_down_ref[...]
        down_b[...] = packed(w.T)
        hi, lo = split(w)
        down_f[...] = stack_rows(hi, lo)
        down_f_hi[...] = hi
        g_qkv_ref[...] = jnp.zeros_like(g_qkv_ref)
        g_out_ref[...] = jnp.zeros_like(g_out_ref)
        g_up_ref[...] = jnp.zeros_like(g_up_ref)
        g_down_ref[...] = jnp.zeros_like(g_down_ref)
        sums_ref[...] = jnp.zeros_like(sums_ref)
        dpos_ref[...] = jnp.zeros_like(dpos_ref)
        dcos_ref[...] = jnp.zeros_like(dcos_ref)

    first_half = lax.broadcasted_iota(jnp.int32, (1, PAIR), 1) < PLACES

    def narrow(weight, x_hi, x_lo):
        r = dot(weight, stack_rows(x_hi, x_lo))
        m = weight.shape[0] // 2
        return r[:m] + r[m:]

    def wide(weight, weight_hi, x_hi, x_lo):
        r = dot(weight, x_hi)
        m = weight_hi.shape[0]
        return (r[:m] + r[m:]) + dot(weight_hi, x_lo)

    def halves(v):
        m = v.shape[0] // 2
        return jnp.where(first_half, v[:m], v[m:])

    def col(i):
        return cols_ref[i]

    def per_item(fn):
        return jnp.concatenate([fn(m) for m in range(step_items)], 1)

    def spread_cols(i):
        c = col(i)
        return jnp.concatenate([c] * step_items, 1)

    def gather(own, right, down, corner, m):
        top_l = own[m, SHIFT : SHIFT + WINDOW, HIDDEN:]
        top_r = right[m, 0:WINDOW, :]
        low_l = jnp.concatenate([own[m, SHIFT + WINDOW :, HIDDEN:], down[m]], 0)
        low_r = jnp.concatenate([right[m, WINDOW:, :], corner[m]], 0)
        tiles = [
            part[:, j * WIDTH : (j + 1) * WIDTH]
            for part in (top_l, top_r, low_l, low_r)
            for j in range(4)
        ]
        return jnp.concatenate(tiles, 0).T

    def scatter(value, lo, ld, ro, rd, m):
        rows = value.T
        parts = [
            jnp.concatenate([rows[(4 * s + j) * 8 : (4 * s + j + 1) * 8] for j in range(4)], 1)
            for s in range(4)
        ]
        lo[m, 0:WINDOW] = parts[0]
        ro[m, 0:WINDOW] = parts[1]
        lo[m, WINDOW:] = parts[2][:SHIFT]
        ro[m, WINDOW:] = parts[3][:SHIFT]
        ld[m] = parts[2][SHIFT:]
        rd[m] = parts[3][SHIFT:]

    def mean_rows(v):
        return jnp.sum(v, 0, keepdims=True) * (1.0 / WIDTH)

    def layer_norm(v):
        centred = v - mean_rows(v)
        rstd = lax.rsqrt(mean_rows(centred * centred) + norm_eps)
        return centred * rstd, rstd

    items = [step * step_items + m for m in range(step_items)]
    leads = [lead_ref[i] for i in items]
    raw = per_item(lambda m: gather(x_own, x_right, x_down, x_corner, m))
    mean = jnp.concatenate([affine_ref[0]] * step_items, 1)
    inv_std = jnp.concatenate([affine_ref[1]] * step_items, 1)
    normed = (raw - mean) * inv_std
    n_hi, n_lo = split(normed)

    joined = narrow(qkv_f[...], n_hi, n_lo)
    query = joined[:WIDTH] + spread_cols(0)
    key = joined[WIDTH : 2 * WIDTH]
    value = joined[2 * WIDTH :] + spread_cols(1)

    def unit(v):
        rows, inverses = [], []
        for h in range(HEADS):
            part = v[h * HEAD_DIM : (h + 1) * HEAD_DIM]
            inverse = lax.rsqrt(jnp.sum(part * part, 0, keepdims=True) + unit_eps)
            rows.append(part * inverse)
            inverses.append(inverse)
        return rows, inverses

    q_rows, q_inv = unit(query)
    k_rows, k_inv = unit(key)
    v_rows = [value[h * HEAD_DIM : (h + 1) * HEAD_DIM] for h in range(HEADS)]

    def of_item(v, m):
        return v[:, m * PAIR : (m + 1) * PAIR]

    def three(a_hi, a_lo, b_hi, b_lo):
        left = jnp.concatenate([a_hi, a_lo, a_hi], 0)
        right = jnp.concatenate([b_hi, b_hi, b_lo], 0)
        return halves(dot(left.T, right))

    def side_by_side(v):
        other = pltpu.roll(v, PLACES, 1)
        v_hi, v_lo = split(v)
        o_hi, o_lo = split(other)
        top = jnp.concatenate([jnp.where(first_half, v_hi, o_lo), v_hi], 1)
        low = jnp.concatenate([jnp.where(first_half, o_hi, v_lo), o_hi], 1)
        return jnp.concatenate([top, low], 0)[:, : 3 * PLACES]

    def over_keys(both, e_hi, e_lo):
        return halves(dot(both, jnp.concatenate([e_hi, e_hi, e_lo], 0)))

    def over_queries(v_hi, v_lo, e_hi, e_lo):
        zero = jnp.zeros_like(v_hi)

        def apart(x):
            return jnp.concatenate(
                [jnp.where(first_half, x, zero), jnp.where(first_half, zero, x)], 0
            )

        a_hi, a_lo = apart(v_hi), apart(v_lo)
        left = jnp.concatenate(
            [
                jnp.concatenate([a_hi, a_hi], 1),
                jnp.concatenate([a_lo, jnp.zeros_like(a_lo)], 1),
            ],
            0,
        )
        weights = jnp.concatenate([e_hi, e_lo], 1)
        r = dot_rows(left, jnp.concatenate([weights, weights], 0))
        return halves(r[:PLACES] + r[PLACES:])

    kept = []
    mixed_items = []
    for m in range(step_items):
        mixed_heads = []
        for h in range(HEADS):
            q_hi, q_lo = split(of_item(q_rows[h], m))
            k_hi, k_lo = split(of_item(k_rows[h], m))
            cosine = three(k_hi, k_lo, q_hi, q_lo)
            flag0 = flags_ref[2 * items[m]]
            flag1 = flags_ref[2 * items[m] + 1]
            offset = jnp.where(first_half, bias_ref[flag0, h], bias_ref[flag1, h])
            expo = jnp.exp(cosine * scale_ref[h] + offset)
            inverse = 1.0 / jnp.sum(expo, 0, keepdims=True)
            e_hi, e_lo = split(expo)
            mixed = over_keys(side_by_side(of_item(v_rows[h], m)), e_hi, e_lo) * inverse
            mixed_heads.append(mixed)
            kept.append((q_hi, q_lo, k_hi, k_lo, cosine, expo, e_hi, e_lo, inverse, mixed))
        mixed_items.append(jnp.concatenate(mixed_heads, 0))
    mixed = jnp.concatenate(mixed_items, 1)

    o_hi, o_lo = split(mixed)
    attn_hat, attn_rstd = layer_norm(narrow(out_f[...], o_hi, o_lo) + spread_cols(2))

    def gain(base):
        return per_item(lambda m: 1.0 + col(base) + leads[m] * col(base + 1))

    def shift(base):
        return per_item(lambda m: col(base + 2) + leads[m] * col(base + 3))

    gain0 = gain(4)
    first = normed + attn_hat * gain0 + shift(4)
    f_hi, f_lo = split(first)

    up_bias = jnp.concatenate([up_bias_ref[...]] * step_items, 1)
    u = narrow(up_f[...], f_hi, f_lo) + up_bias
    phi, bell = normal_parts(u)
    hidden = u * phi
    slope = phi + u * bell
    h_hi, h_lo = split(hidden)
    branch = wide(down_f[...], down_f_hi[...], h_hi, h_lo) + spread_cols(3)
    hat, rstd = layer_norm(branch)
    gain1 = gain(8)
    out = first + hat * gain1 + shift(8)
    for m in range(step_items):
        scatter(of_item(out, m), out_lo, out_ld, out_ro, out_rd, m)

    def norm_back(g, hat, rstd, gain, base):
        weighted = g * hat
        for m in range(step_items):
            a, b = of_item(weighted, m), of_item(g, m)
            sums_ref[base] += a
            sums_ref[base + 1] += leads[m] * a
            sums_ref[base + 2] += b
            sums_ref[base + 3] += leads[m] * b
        e = g * gain
        return (e - mean_rows(e) - hat * mean_rows(e * hat)) * rstd

    def add_items(v):
        total = of_item(v, 0)
        for m in range(1, step_items):
            total = total + of_item(v, m)
        return total

    ones_rows = jnp.where(
        lax.broadcasted_iota(jnp.int32, (LANES - WIDTH, step_items * PAIR), 0) == 0, 1.0, 0.0
    ).astype(bf16)
    zero_rows = jnp.zeros((LANES - WIDTH, step_items * PAIR), bf16)

    def outer(a_hi, a_lo, b_hi, b_lo):
        right = jnp.concatenate([b_hi, ones_rows, b_lo, zero_rows], 0)
        r = dot_rows(stack_rows(a_hi, a_lo), right)
        m = a_hi.shape[0]
        return (r[:m, :LANES] + r[m:, :LANES]) + r[:m, LANES:]

    cot = per_item(lambda m: gather(ct_own, ct_right, ct_down, ct_corner, m))
    d_branch = norm_back(cot, hat, rstd, gain1, 4)
    sums_ref[8] += add_items(d_branch)
    z_hi, z_lo = split(d_branch)
    g_down_ref[...] += outer(h_hi, h_lo, z_hi, z_lo)
    d_pre = narrow(down_b[...], z_hi, z_lo) * slope
    p_hi, p_lo = split(d_pre)
    g_up_ref[...] += outer(p_hi, p_lo, f_hi, f_lo)
    d_first = cot + wide(up_b[...], up_b_hi[...], p_hi, p_lo)
    d_attn = norm_back(d_first, attn_hat, attn_rstd, gain0, 0)
    a_hi, a_lo = split(d_attn)
    g_out_ref[...] += outer(a_hi, a_lo, o_hi, o_lo)
    d_mixed = narrow(out_b[...], a_hi, a_lo)

    d_items = []
    for m in range(step_items):
        dq_rows, dk_rows, dv_rows = [], [], []
        for h in range(HEADS):
            q_hi, q_lo, k_hi, k_lo, cosine, expo, e_hi, e_lo, inverse, mixed_h = kept[m * HEADS + h]
            q_dir, k_dir = of_item(q_rows[h], m), of_item(k_rows[h], m)
            v_hi, v_lo = split(of_item(v_rows[h], m))
            d_out = of_item(d_mixed, m)[h * HEAD_DIM : (h + 1) * HEAD_DIM] * inverse
            d_hi, d_lo = split(d_out)
            delta = jnp.sum(d_out * mixed_h, 0, keepdims=True)
            d_scores = expo * (three(v_hi, v_lo, d_hi, d_lo) - delta)
            dpos_ref[h] += d_scores
            folded = d_scores * cosine
            total = folded[0:8]
            for i in range(1, PLACES // 8):
                total = total + folded[8 * i : 8 * i + 8]
            dcos_ref[h] += total
            s_hi, s_lo = split(d_scores)
            dv = over_queries(d_hi, d_lo, e_hi, e_lo)
            dk = over_queries(q_hi, q_lo, s_hi, s_lo) * scale_ref[h]
            dq = over_keys(side_by_side(k_dir), s_hi, s_lo) * scale_ref[h]
            dq = (dq - q_dir * jnp.sum(q_dir * dq, 0, keepdims=True)) * of_item(q_inv[h], m)
            dk = (dk - k_dir * jnp.sum(k_dir * dk, 0, keepdims=True)) * of_item(k_inv[h], m)
            dq_rows.append(dq)
            dk_rows.append(dk)
            dv_rows.append(dv)
        d_items.append(jnp.concatenate(dq_rows + dk_rows + dv_rows, 0))
    d_joined = jnp.concatenate(d_items, 1)
    j_hi, j_lo = split(d_joined)
    g_qkv_ref[...] += outer(j_hi, j_lo, n_hi, n_lo)
    d_normed = d_first + wide(qkv_b[...], qkv_b_hi[...], j_hi, j_lo)
    sums_ref[9] += add_items(d_normed)
    sums_ref[10] += add_items(d_normed * normed)
    for m in range(step_items):
        scatter(of_item(d_normed, m), dn_lo, dn_ld, dn_ro, dn_rd, m)


def run_block(flags, lead, x_parts, ct_parts, affine, weights, cols, up_bias, scale, bias):
    items = x_parts[0].shape[0]
    step_items = 2
    steps = items // step_items
    half = HIDDEN

    def rows(n, width):
        return pl.BlockSpec((step_items, n, width), lambda i: (i, 0, 0))

    def whole(shape):
        return pl.BlockSpec(shape, lambda i: (0,) * len(shape))

    smem = pl.BlockSpec(memory_space=pltpu.SMEM)
    part_specs = [
        rows(16, 2 * half),
        rows(12, half),
        rows(4, half),
        rows(4, half),
    ]
    side_shapes = [(12, half), (4, half), (12, half), (4, half)]
    side_out = [jax.ShapeDtypeStruct((items,) + s, f32) for s in side_shapes]
    side_specs = [rows(*s) for s in side_shapes]
    acc_shapes = [
        (3 * WIDTH, LANES),
        (WIDTH, LANES),
        (HIDDEN, LANES),
        (HIDDEN, LANES),
        (11, WIDTH, LANES),
        (HEADS, PLACES, LANES),
        (HEADS, 8, LANES),
    ]
    w_qkv, w_out, w_up, w_down = weights
    return pl.pallas_call(
        partial(block_kernel, step_items),
        grid=(steps,),
        in_specs=[smem, smem]
        + part_specs
        + part_specs
        + [whole(affine.shape)]
        + [whole(w.shape) for w in weights]
        + [whole(cols.shape), whole(up_bias.shape), smem, whole(bias.shape)],
        out_specs=side_specs + side_specs + [whole(s) for s in acc_shapes],
        out_shape=side_out + side_out + [jax.ShapeDtypeStruct(s, f32) for s in acc_shapes],
        scratch_shapes=[
            pltpu.VMEM((6 * WIDTH, 2 * WIDTH), bf16),
            pltpu.VMEM((2 * WIDTH, 2 * WIDTH), bf16),
            pltpu.VMEM((2 * HIDDEN, 2 * WIDTH), bf16),
            pltpu.VMEM((2 * WIDTH, HIDDEN), bf16),
            pltpu.VMEM((2 * HIDDEN, 2 * WIDTH), bf16),
            pltpu.VMEM((2 * WIDTH, HIDDEN), bf16),
            pltpu.VMEM((2 * WIDTH, 2 * WIDTH), bf16),
            pltpu.VMEM((2 * WIDTH, 3 * WIDTH), bf16),
            pltpu.VMEM((WIDTH, HIDDEN), bf16),
            pltpu.VMEM((WIDTH, HIDDEN), bf16),
            pltpu.VMEM((WIDTH, 3 * WIDTH), bf16),
        ],
        compiler_params=pltpu.CompilerParams(
            dimension_semantics=("arbitrary",), vmem_limit_bytes=56 * 1024 * 1024
        ),
    )(
        flags,
        lead,
        *x_parts,
        *ct_parts,
        affine,
        w_qkv,
        w_out,
        w_up,
        w_down,
        cols,
        up_bias,
        scale,
        bias,
    )


def input_grad_kernel(x_ref, own_ref, right_ref, down_ref, corner_ref, c_ref, out_ref):
    inv_std = c_ref[0:1]
    a = c_ref[1:2]
    b = c_ref[2:3]
    mean = c_ref[3:4]
    half = HIDDEN
    for m in range(x_ref.shape[0]):
        for rows, left, right in (
            (slice(0, SHIFT), corner_ref[m], down_ref[m]),
            (slice(SHIFT, 16), right_ref[m], own_ref[m]),
        ):
            for lanes, d in ((slice(0, half), left), (slice(half, 2 * half), right)):
                x = x_ref[m, rows, lanes]
                out_ref[m, rows, lanes] = (
                    inv_std[:, lanes] * d - a[:, lanes] - (x - mean[:, lanes]) * b[:, lanes]
                )


def input_grad(x, own, right, down, corner, coefficients):
    items, rows, flat = x.shape
    step_items = 8 if items % 8 == 0 else 1
    half = HIDDEN

    def spec(n, width):
        return pl.BlockSpec((step_items, n, width), lambda i: (i, 0, 0))

    return pl.pallas_call(
        input_grad_kernel,
        grid=(items // step_items,),
        in_specs=[
            spec(rows, flat),
            spec(12, half),
            spec(12, half),
            spec(4, half),
            spec(4, half),
            pl.BlockSpec(coefficients.shape, lambda i: (0, 0)),
        ],
        out_specs=spec(rows, flat),
        out_shape=jax.ShapeDtypeStruct(x.shape, f32),
    )(x, own, right, down, corner, coefficients)


def place_coordinates():
    places = jnp.arange(PLACES, dtype=jnp.int32)
    return places % WINDOW, places // WINDOW


def coordinate_table():
    offsets = jnp.arange(SPAN * SPAN, dtype=jnp.int32)
    along_rows = (offsets // SPAN - (WINDOW - 1)).astype(f32)
    along_cols = (offsets % SPAN - (WINDOW - 1)).astype(f32)
    stacked = jnp.stack([along_rows, along_cols], -1) * (8.0 / (WINDOW - 1))
    return jnp.sign(stacked) * jnp.log2(jnp.abs(stacked) + 1.0) / 3.0


def position_bias(weight1, bias1, weight2):
    precise = lax.Precision.HIGHEST
    hidden_units = jax.nn.gelu(
        jnp.dot(coordinate_table(), weight1, precision=precise) + bias1, approximate=False
    )
    table = 16.0 * jax.nn.sigmoid(jnp.dot(hidden_units, weight2, precision=precise))
    row, col = place_coordinates()
    index = (row[None, :] - row[:, None] + WINDOW - 1) * SPAN + (
        col[None, :] - col[:, None] + WINDOW - 1
    )
    offset_ids = jnp.arange(SPAN * SPAN, dtype=jnp.int32)
    one_hot = (index.reshape(-1)[:, None] == offset_ids[None, :]).astype(f32)
    spread_out = lax.dot_general(
        table, one_hot, (((0,), (1,)), ((), ())), precision=precise
    )
    return spread_out.reshape(HEADS, PLACES, PLACES)


def mask_tables():
    row, col = place_coordinates()
    apart_r = (row[None, :] < SHIFT) != (row[:, None] < SHIFT)
    apart_c = (col[None, :] < SHIFT) != (col[:, None] < SHIFT)
    none = jnp.zeros_like(apart_r)
    return jnp.stack([none, apart_c, apart_r, apart_r | apart_c])


def take_from(block, dy, dx):
    rows, cols = lax.axis_size("ty"), lax.axis_size("tx")
    route = []
    for i in range(rows * cols):
        y, x = divmod(i, cols)
        route.append((((y + dy) % rows) * cols + (x + dx) % cols, i))
    return lax.ppermute(block, ("ty", "tx"), route)


def reduce_all(v):
    n = lax.axis_size(axes_all)
    step = 1
    while step < n:
        v = v + lax.ppermute(v, axes_all, [(i, i ^ step) for i in range(n)])
        step *= 2
    return v


def shards(
    inputs,
    regions,
    lead_step_index,
    running_channel_mean,
    running_channel_variance,
    query_key_value_weight,
    query_value_bias,
    log_cosine_scale,
    bias_net_weight1,
    bias_net_bias1,
    bias_net_weight2,
    output_weight,
    projection_bias,
    up_weight,
    up_bias,
    down_weight,
    down_bias,
    conditioned_norm_values,
    cotangent,
):
    items, tile_rows, flat = inputs.shape
    tile_cols = flat // WIDTH
    half = flat // 2
    devices = lax.axis_size(axes_all)
    local_count = items * tile_rows * tile_cols
    token_count = local_count * devices

    def halo(field):
        return (
            field,
            take_from(field[:, SHIFT:, :half], 0, 1),
            take_from(field[:, :SHIFT, half:], 1, 0),
            take_from(field[:, :SHIFT, :half], 1, 1),
        )

    stats = local_stats(inputs)
    x_parts = halo(inputs)
    ct_parts = halo(cotangent)
    mine = jnp.broadcast_to(stats[None, :2], (devices, 2, WIDTH))
    every = lax.all_to_all(mine, axes_all, 0, 0, tiled=True)
    chan_mean = jnp.mean(every[:, 0], 0)
    apart = every[:, 0] - chan_mean
    chan_var = (
        jnp.sum(every[:, 1], 0) + local_count * jnp.sum(apart * apart, 0)
    ) / token_count
    inv_std = lax.rsqrt(chan_var + norm_eps)

    row_cut = regions[:, ::WINDOW, 0] != regions[:, WINDOW - 1 :: WINDOW, 0]
    col_cut = regions[:, ::WINDOW, 0] != regions[:, ::WINDOW, WINDOW - 1]
    flags = (2 * row_cut.astype(jnp.int32) + col_cut.astype(jnp.int32)).reshape(-1)
    lead = (lead_step_index + 1).astype(f32) / LEAD_STEPS

    scale = jnp.exp(log_cosine_scale)
    pos_bias, bias_pull = jax.vjp(
        position_bias, bias_net_weight1, bias_net_bias1, bias_net_weight2
    )
    ceiling = (scale + 16.0)[:, None, None]
    tables = jnp.where(mask_tables()[:, None], masked_score, pos_bias[None] - ceiling[None])
    tables = jnp.concatenate([tables, tables], -1)

    def spread(rows):
        return jnp.broadcast_to(rows[..., None], rows.shape + (LANES,))

    cols = spread(
        jnp.concatenate(
            [
                query_value_bias,
                projection_bias[None],
                down_bias[None],
                conditioned_norm_values.reshape(8, WIDTH),
            ],
            0,
        )
    )
    affine = spread(jnp.stack([chan_mean, inv_std]))
    results = run_block(
        flags,
        lead,
        x_parts,
        ct_parts,
        affine,
        (query_key_value_weight, output_weight, up_weight, down_weight),
        cols,
        spread(up_bias),
        scale,
        tables,
    )
    out_parts, dn_parts = results[:4], results[4:8]
    g_qkv, g_out, g_up, g_down, sums, d_pos, d_cos = results[8:]

    def home(parts):
        own, down, right, corner = parts
        return (own, take_from(right, 0, -1), take_from(down, -1, 0), take_from(corner, -1, -1))

    dn_own, dn_right, dn_down, dn_corner = home(dn_parts)
    out_own, out_right, out_down, out_corner = home(out_parts)
    outputs = jnp.concatenate(
        [
            jnp.concatenate([out_corner, out_down], 2),
            jnp.concatenate([out_right, out_own], 2),
        ],
        1,
    )

    d_pos = d_pos[:, :, :PLACES] + d_pos[:, :, PLACES:]
    g_w1, g_b1, g_w2 = bias_pull(d_pos)
    sums = jnp.sum(sums, -1)
    pieces = [
        g_qkv,
        g_out,
        g_up,
        g_down,
        sums,
        jnp.sum(d_cos, (1, 2)) * scale,
        g_w1,
        g_b1,
        g_w2,
    ]
    sizes = [p.size for p in pieces]
    total = sum(sizes)
    padded = -(-total // 1024) * 1024
    flat_sum = jnp.concatenate([p.reshape(-1) for p in pieces] + [jnp.zeros(padded - total, f32)])
    flat_sum = reduce_all(flat_sum.reshape(-1, LANES)).reshape(-1)
    back, at = [], 0
    for p in pieces:
        back.append(flat_sum[at : at + p.size].reshape(p.shape))
        at += p.size
    g_qkv, g_out, g_up, g_down, sums, g_scale, g_w1, g_b1, g_w2 = back

    sum_grad = sums[9] / token_count
    sum_cross = sums[10] / token_count
    coefficients = jnp.stack(
        [inv_std, inv_std * sum_grad, inv_std * inv_std * sum_cross, chan_mean]
    )
    coefficients = jnp.tile(coefficients, (1, tile_cols))
    grad_inputs = input_grad(inputs, dn_own, dn_right, dn_down, dn_corner, coefficients)
    new_mean = (1.0 - momentum) * running_channel_mean + momentum * chan_mean
    new_var = (1.0 - momentum) * running_channel_variance + momentum * chan_var * (
        token_count / (token_count - 1.0)
    )
    return (
        outputs,
        grad_inputs,
        g_qkv[:, :WIDTH].T,
        jnp.stack([g_qkv[:WIDTH, WIDTH], g_qkv[2 * WIDTH :, WIDTH]]),
        g_scale,
        g_w1,
        g_b1,
        g_w2,
        g_out[:, :WIDTH].T,
        g_out[:, WIDTH],
        g_up[:, :WIDTH].T,
        g_up[:, WIDTH],
        g_down[:, :WIDTH].T,
        sums[8],
        sums[:8].reshape(2, 4, WIDTH),
        new_mean,
        new_var,
    )


def solution(mesh):
    tiled = P("items", "ty", "tx")
    placed = (tiled, tiled, P("items")) + (P(),) * 15 + (tiled,)
    return jax.shard_map(
        shards,
        mesh=mesh,
        in_specs=placed,
        out_specs=(tiled, tiled) + (P(),) * 15,
        check_vma=False,
    )
```

```python
from functools import partial

import jax
import jax.numpy as jnp
import numpy as np
from jax import lax
from jax.experimental import pallas as pl
from jax.experimental.pallas import tpu as pltpu
from jax.sharding import PartitionSpec as P

HEADS = 3
HEAD_DIM = 32
WIDTH = 96
HIDDEN = 384
WINDOW = 8
SHIFT = 4
LEAD_STEPS = 14
PLACES = WINDOW * WINDOW
SPAN = 2 * WINDOW - 1
PAIR = 2 * PLACES
LANES = 128
OFFSETS = 256
PAYLOAD = 903

masked_score = -1000000000.0
norm_eps = 1e-05
unit_eps = 1e-06
momentum = 0.1
axes_all = ("ty", "tx", "items")

f32 = jnp.float32
bf16 = jnp.bfloat16

in_order = pltpu.CompilerParams(
    dimension_semantics=("arbitrary",), vmem_limit_bytes=60 * 1024 * 1024
)


def block_of(items):
    return next(n for n in (8, 4, 2, 1) if items % n == 0)


def whole(a):
    return pl.BlockSpec(a.shape, lambda i: (0,) * len(a.shape))


normal_slope = 0.28
normal_poly = (
    0.11652074430372011,
    0.06749697235753221,
    0.26890961436457633,
    -0.23699279280357777,
    0.389873590681989,
    -0.10580813816203069,
)


def dot(a, b):
    return lax.dot_general(a, b, (((1,), (0,)), ((), ())), preferred_element_type=f32)


def dot_rows(a, b):
    return lax.dot_general(a, b, (((1,), (1,)), ((), ())), preferred_element_type=f32)


def split(x):
    hi = x.astype(bf16)
    return hi, (x - hi.astype(f32)).astype(bf16)


def normal_parts(u):
    a = jnp.abs(u)
    t = 1.0 / (1.0 + normal_slope * a)
    bell = jnp.exp(-0.5 * u * u)
    poly = normal_poly[-1] * t + normal_poly[-2]
    for c in normal_poly[-3::-1]:
        poly = poly * t + c
    tail = poly * t * bell
    return jnp.where(u < 0, tail, 1.0 - tail), bell * 0.3989422804014327


def pack_kernel(items, x_ref, ct_ref, stats_ref, right_ref, down_ref, corner_ref, sums_ref):
    step = pl.program_id(0)
    step_items, rows, flat = x_ref.shape
    cols = flat // WIDTH
    half = flat // 2

    for part, ref in enumerate((x_ref, ct_ref)):
        right_ref[:, 12 * part : 12 * part + 12, :] = ref[:, SHIFT:, :half]
        down_ref[:, 4 * part : 4 * part + 4, :] = ref[:, :SHIFT, half:]
        corner_ref[:, 4 * part : 4 * part + 4, :] = ref[:, :SHIFT, :half]

    def fold(v):
        total = v[:, :WIDTH]
        for j in range(1, cols):
            total = total + v[:, j * WIDTH : (j + 1) * WIDTH]
        return jnp.sum(total, 0, keepdims=True)

    def total(fn):
        acc = jnp.zeros((8, flat), f32)
        for i in range(step_items):
            acc = acc + fn(x_ref[i, 0:8, :]) + fn(x_ref[i, 8:16, :])
        return acc

    @pl.when(step == 0)
    def _():
        pivot = fold(total(lambda v: v)) * (1.0 / (step_items * rows * cols))
        sums_ref[0] = jnp.broadcast_to(jnp.concatenate([pivot] * cols, 1), (8, flat))
        sums_ref[1] = jnp.zeros((8, flat), f32)
        sums_ref[2] = jnp.zeros((8, flat), f32)

    pivot = sums_ref[0]
    sums_ref[1] += total(lambda v: v - pivot)
    sums_ref[2] += total(lambda v: (v - pivot) * (v - pivot))

    @pl.when(step == pl.num_programs(0) - 1)
    def _():
        count = items * rows * cols
        offset = fold(sums_ref[1]) * (1.0 / count)
        square = fold(sums_ref[2]) - count * offset * offset
        pad = jnp.zeros((1, LANES - WIDTH), f32)
        row = jnp.concatenate([sums_ref[0, 0:1, :WIDTH] + offset, pad, square, pad], 1)
        stats_ref[...] = jnp.broadcast_to(row[None], stats_ref.shape)


def pack(x, ct, devices):
    items, rows, flat = x.shape
    half = flat // 2
    step_items = block_of(items)

    def spec(n, width):
        return pl.BlockSpec((step_items, n, width), lambda i: (i, 0, 0))

    return pl.pallas_call(
        partial(pack_kernel, items),
        grid=(items // step_items,),
        in_specs=[spec(rows, flat)] * 2,
        out_specs=[
            pl.BlockSpec((devices, 1, 2 * LANES), lambda i: (0, 0, 0)),
            spec(24, half),
            spec(8, half),
            spec(8, half),
        ],
        out_shape=[
            jax.ShapeDtypeStruct((devices, 1, 2 * LANES), f32),
            jax.ShapeDtypeStruct((items, 24, half), f32),
            jax.ShapeDtypeStruct((items, 8, half), f32),
            jax.ShapeDtypeStruct((items, 8, half), f32),
        ],
        scratch_shapes=[pltpu.VMEM((3, 8, flat), f32)],
        compiler_params=in_order,
    )(x, ct)


def offset_constants():
    coords = np.zeros((8, OFFSETS), np.float32)
    o = np.arange(SPAN * SPAN)
    for k, along in enumerate((o // SPAN - (WINDOW - 1), o % SPAN - (WINDOW - 1))):
        u = along.astype(np.float32) * np.float32(8.0 / (WINDOW - 1))
        coords[k, : SPAN * SPAN] = np.sign(u) * np.log2(np.abs(u) + np.float32(1.0)) / np.float32(3.0)
    coords[2, : SPAN * SPAN] = 1.0
    key_row, lane = np.divmod(np.arange(WINDOW * LANES), LANES)
    across, row = np.divmod(lane, WINDOW)
    target = (row - key_row + WINDOW - 1) * SPAN + across
    target = np.where(across < SPAN, target, -1).astype(np.int32)
    return jnp.asarray(coords), jnp.asarray(np.broadcast_to(target, (8, target.size)).copy())


def exact(a, b, dims):
    return lax.dot_general(
        a, b, (dims, ((), ())), preferred_element_type=f32, precision=lax.Precision.HIGHEST
    )


def bias_net(net, coords):
    units = net.shape[1]
    columns = jnp.concatenate([net, jnp.zeros((LANES - 8, units), f32)], 0).T

    def column(i):
        return jnp.broadcast_to(columns[:, i : i + 1], (units, OFFSETS))

    u = column(0) * coords[0:1] + column(1) * coords[1:2] + column(2)
    phi, bell = normal_parts(u)
    return column, u * phi, phi + u * bell


def head_rows(net):
    return jnp.concatenate([net[3:6], jnp.zeros((5, net.shape[1]), f32)], 0)


def one_hot(target):
    rows = lax.broadcasted_iota(jnp.int32, (OFFSETS, WINDOW * LANES), 0)
    return jnp.where(rows == target[0:1], 1.0, 0.0)


def prepare_kernel(
    w_qkv_ref,
    w_out_ref,
    w_up_ref,
    w_down_ref,
    rows_ref,
    up_bias_ref,
    log_scale_ref,
    net_ref,
    coords_ref,
    target_ref,
    qkv_f,
    out_f,
    up_f,
    down_f,
    down_b,
    up_b,
    out_b,
    qkv_b,
    cols_ref,
    up_cols_ref,
    scale_ref,
    bias_ref,
):
    def packed(w):
        hi, lo = split(w)
        return jnp.concatenate(
            [jnp.concatenate([hi, hi], 1), jnp.concatenate([lo, jnp.zeros_like(lo)], 1)], 0
        )

    def stacked(w):
        hi, lo = split(w)
        return jnp.concatenate([hi, lo], 0)

    qkv_f[...] = packed(w_qkv_ref[...].T)
    qkv_b[...] = stacked(w_qkv_ref[...])
    out_f[...] = packed(w_out_ref[...].T)
    out_b[...] = packed(w_out_ref[...])
    up_f[...] = packed(w_up_ref[...].T)
    up_b[...] = stacked(w_up_ref[...])
    down_b[...] = packed(w_down_ref[...].T)
    down_f[...] = stacked(w_down_ref[...])

    for i in range(cols_ref.shape[0]):
        cols_ref[i] = jnp.broadcast_to(rows_ref[i : i + 1], (LANES, WIDTH)).T
    up_cols_ref[...] = jnp.broadcast_to(up_bias_ref[...], (LANES, HIDDEN)).T

    lanes = lax.broadcasted_iota(jnp.int32, (1, LANES), 1)
    net = net_ref[...]
    _, hidden, _ = bias_net(net, coords_ref[...])
    table = 16.0 / (1.0 + jnp.exp(-exact(head_rows(net), hidden, ((1,), (0,)))))
    tiles = exact(table, one_hot(target_ref[...]), ((1,), (0,)))
    place = lax.broadcasted_iota(jnp.int32, (PLACES, LANES), 0)
    other = lax.broadcasted_iota(jnp.int32, (PLACES, LANES), 1) % PLACES
    apart_r = (place % WINDOW < SHIFT) != (other % WINDOW < SHIFT)
    apart_c = (place // WINDOW < SHIFT) != (other // WINDOW < SHIFT)
    for h in range(HEADS):
        scale = jnp.exp(jnp.full((1, LANES), log_scale_ref[h], f32))
        scale_ref[h : h + 1, :] = scale
        tile = jnp.concatenate(
            [tiles[h : h + 1, r * LANES : (r + 1) * LANES] for r in range(WINDOW)], 0
        )
        columns = []
        for j in range(WINDOW):
            turned = pltpu.roll(tile, (72 + 8 * j) % LANES, 1)
            columns.append(jnp.where(lanes < PLACES, turned, pltpu.roll(turned, PLACES, 1)))
        bias = jnp.concatenate(columns, 0) - (scale + 16.0)
        bias_ref[0, h] = bias
        bias_ref[1, h] = jnp.where(apart_c, masked_score, bias)
        bias_ref[2, h] = jnp.where(apart_r, masked_score, bias)
        bias_ref[3, h] = jnp.where(apart_r | apart_c, masked_score, bias)


def prepare(weights, rows, up_bias, log_scale, net, coords, target):
    smem = pl.BlockSpec(memory_space=pltpu.SMEM)
    shapes = [
        ((6 * WIDTH, 2 * WIDTH), bf16),
        ((2 * WIDTH, 2 * WIDTH), bf16),
        ((2 * HIDDEN, 2 * WIDTH), bf16),
        ((2 * WIDTH, HIDDEN), bf16),
        ((2 * HIDDEN, 2 * WIDTH), bf16),
        ((2 * WIDTH, HIDDEN), bf16),
        ((2 * WIDTH, 2 * WIDTH), bf16),
        ((2 * WIDTH, 3 * WIDTH), bf16),
        ((rows.shape[0], WIDTH, LANES), f32),
        ((HIDDEN, LANES), f32),
        ((8, LANES), f32),
        ((4, HEADS, PLACES, LANES), f32),
    ]
    shapes = [jax.ShapeDtypeStruct(s, t) for s, t in shapes]
    return pl.pallas_call(
        prepare_kernel,
        grid=(1,),
        in_specs=[whole(a) for a in (*weights, rows, up_bias)]
        + [smem]
        + [whole(a) for a in (net, coords, target)],
        out_specs=[whole(a) for a in shapes],
        out_shape=shapes,
        compiler_params=in_order,
    )(*weights, rows, up_bias, log_scale, net, coords, target)


def stack_rows(hi, lo):
    return jnp.concatenate([hi, lo], 0)


def block_kernel(
    step_items,
    token_count,
    flags_ref,
    lead_ref,
    x_own,
    x_right,
    x_down,
    x_corner,
    ct_own,
    stats_ref,
    running_ref,
    qkv_f,
    out_f,
    up_f,
    down_f,
    down_b,
    up_b,
    out_b,
    qkv_b,
    cols_ref,
    up_cols_ref,
    scale_ref,
    bias_ref,
    net_ref,
    coords_ref,
    target_ref,
    out_keep,
    dn_keep,
    send_right,
    send_down,
    send_corner,
    grads_ref,
    norm_ref,
    affine_ref,
    g_qkv_ref,
    g_out_ref,
    g_up_ref,
    g_down_ref,
    sums_ref,
    dpos_ref,
    dcos_ref,
    flat_ref,
):
    step = pl.program_id(0)

    @pl.when(step == 0)
    def _():
        every = stats_ref[...]
        devices = every.shape[0]
        means, squares = every[:, 0, :LANES], every[:, 0, LANES:]
        mean = jnp.sum(means, 0, keepdims=True) * (1.0 / devices)
        apart = means - mean
        var = (
            jnp.sum(squares, 0, keepdims=True) * (1.0 / token_count)
            + jnp.sum(apart * apart, 0, keepdims=True) * (1.0 / devices)
        )
        inv_std = lax.rsqrt(var + norm_eps)
        affine_ref[0] = jnp.broadcast_to(mean, (LANES, LANES)).T[:WIDTH]
        affine_ref[1] = jnp.broadcast_to(inv_std, (LANES, LANES)).T[:WIDTH]
        pad = jnp.zeros((1, LANES - WIDTH), f32)
        running = jnp.concatenate([running_ref[...], jnp.concatenate([pad, pad], 0)], 1)
        norm_ref[0:1] = mean
        norm_ref[1:2] = inv_std
        norm_ref[2:3] = (1.0 - momentum) * running[0:1] + momentum * mean
        norm_ref[3:4] = (1.0 - momentum) * running[1:2] + momentum * var * (
            token_count / (token_count - 1.0)
        )
        norm_ref[4:8] = jnp.zeros((4, LANES), f32)
        g_qkv_ref[...] = jnp.zeros_like(g_qkv_ref)
        g_out_ref[...] = jnp.zeros_like(g_out_ref)
        g_up_ref[...] = jnp.zeros_like(g_up_ref)
        g_down_ref[...] = jnp.zeros_like(g_down_ref)
        sums_ref[...] = jnp.zeros_like(sums_ref)
        dpos_ref[...] = jnp.zeros_like(dpos_ref)
        dcos_ref[...] = jnp.zeros_like(dcos_ref)

    first_half = lax.broadcasted_iota(jnp.int32, (1, PAIR), 1) < PLACES

    def narrow(weight, x_hi, x_lo):
        r = dot(weight, stack_rows(x_hi, x_lo))
        m = weight.shape[0] // 2
        return r[:m] + r[m:]

    def wide(weight, x_hi, x_lo):
        r = dot(weight[...], x_hi)
        m = weight.shape[0] // 2
        return (r[:m] + r[m:]) + dot(weight[:m], x_lo)

    def halves(v):
        m = v.shape[0] // 2
        return jnp.where(first_half, v[:m], v[m:])

    def col(i):
        return cols_ref[i]

    def per_item(fn):
        return jnp.concatenate([fn(m) for m in range(step_items)], 1)

    def spread_cols(i):
        c = col(i)
        return jnp.concatenate([c] * step_items, 1)

    def gather(own, part, m):
        right, down = 12 * part, 4 * part
        top_l = own[m, SHIFT : SHIFT + WINDOW, :]
        top_r = x_right[m, right : right + WINDOW, :]
        low_l = jnp.concatenate([own[m, SHIFT + WINDOW :, :], x_down[m, down : down + SHIFT, :]], 0)
        low_r = jnp.concatenate(
            [x_right[m, right + WINDOW : right + 12, :], x_corner[m, down : down + SHIFT, :]], 0
        )
        tiles = [
            side[:, j * WIDTH : (j + 1) * WIDTH]
            for side in (top_l, top_r, low_l, low_r)
            for j in range(4)
        ]
        return jnp.concatenate(tiles, 0).T

    def scatter(value, keep, part, m):
        rows = value.T
        sides = [
            jnp.concatenate([rows[(4 * s + j) * 8 : (4 * s + j + 1) * 8] for j in range(4)], 1)
            for s in range(4)
        ]
        right, down = 12 * part, 4 * part
        keep[m, 0:WINDOW, :] = sides[0]
        keep[m, WINDOW:, :] = sides[2][:SHIFT]
        send_right[m, right : right + WINDOW, :] = sides[1]
        send_right[m, right + WINDOW : right + 12, :] = sides[3][:SHIFT]
        send_down[m, down : down + SHIFT, :] = sides[2][SHIFT:]
        send_corner[m, down : down + SHIFT, :] = sides[3][SHIFT:]

    def mean_rows(v):
        return jnp.sum(v, 0, keepdims=True) * (1.0 / WIDTH)

    def layer_norm(v):
        centred = v - mean_rows(v)
        rstd = lax.rsqrt(mean_rows(centred * centred) + norm_eps)
        return centred * rstd, rstd

    items = [step * step_items + m for m in range(step_items)]
    leads = [(lead_ref[i] + 1).astype(f32) * (1.0 / LEAD_STEPS) for i in items]
    raw = per_item(lambda m: gather(x_own, 0, m))
    mean = jnp.concatenate([affine_ref[0]] * step_items, 1)
    inv_std = jnp.concatenate([affine_ref[1]] * step_items, 1)
    normed = (raw - mean) * inv_std
    n_hi, n_lo = split(normed)

    joined = narrow(qkv_f[...], n_hi, n_lo)
    query = joined[:WIDTH] + spread_cols(0)
    key = joined[WIDTH : 2 * WIDTH]
    value = joined[2 * WIDTH :] + spread_cols(1)

    def unit(v):
        rows, inverses = [], []
        for h in range(HEADS):
            part = v[h * HEAD_DIM : (h + 1) * HEAD_DIM]
            inverse = lax.rsqrt(jnp.sum(part * part, 0, keepdims=True) + unit_eps)
            rows.append(part * inverse)
            inverses.append(inverse)
        return rows, inverses

    q_rows, q_inv = unit(query)
    k_rows, k_inv = unit(key)
    v_rows = [value[h * HEAD_DIM : (h + 1) * HEAD_DIM] for h in range(HEADS)]

    def of_item(v, m):
        return v[:, m * PAIR : (m + 1) * PAIR]

    def three(a_hi, a_lo, b_hi, b_lo):
        left = jnp.concatenate([a_hi, a_lo, a_hi], 0)
        right = jnp.concatenate([b_hi, b_hi, b_lo], 0)
        return halves(dot(left.T, right))

    def side_by_side(v):
        other = pltpu.roll(v, PLACES, 1)
        v_hi, v_lo = split(v)
        o_hi, o_lo = split(other)
        top = jnp.concatenate([jnp.where(first_half, v_hi, o_lo), v_hi], 1)
        low = jnp.concatenate([jnp.where(first_half, o_hi, v_lo), o_hi], 1)
        return jnp.concatenate([top, low], 0)[:, : 3 * PLACES]

    def over_keys(both, e_hi, e_lo):
        return halves(dot(both, jnp.concatenate([e_hi, e_hi, e_lo], 0)))

    def over_queries(v_hi, v_lo, e_hi, e_lo):
        zero = jnp.zeros_like(v_hi)

        def apart(x):
            return jnp.concatenate(
                [jnp.where(first_half, x, zero), jnp.where(first_half, zero, x)], 0
            )

        a_hi, a_lo = apart(v_hi), apart(v_lo)
        left = jnp.concatenate(
            [
                jnp.concatenate([a_hi, a_hi], 1),
                jnp.concatenate([a_lo, jnp.zeros_like(a_lo)], 1),
            ],
            0,
        )
        weights = jnp.concatenate([e_hi, e_lo], 1)
        r = dot_rows(left, jnp.concatenate([weights, weights], 0))
        return halves(r[:PLACES] + r[PLACES:])

    pairs = [(m, h) for m in range(step_items) for h in range(HEADS)]
    q_parts = [split(of_item(q_rows[h], m)) for m, h in pairs]
    k_parts = [split(of_item(k_rows[h], m)) for m, h in pairs]
    cosines = [three(*k, *q) for k, q in zip(k_parts, q_parts)]
    expos, inverses = [], []
    for (m, h), cosine in zip(pairs, cosines):
        flag0 = flags_ref[2 * items[m]]
        flag1 = flags_ref[2 * items[m] + 1]
        offset = jnp.where(first_half, bias_ref[flag0, h], bias_ref[flag1, h])
        expo = jnp.exp(cosine * scale_ref[h : h + 1, :] + offset)
        expos.append(expo)
        inverses.append(1.0 / jnp.sum(expo, 0, keepdims=True))
    e_parts = [split(e) for e in expos]
    mixes = [
        over_keys(side_by_side(of_item(v_rows[h], m)), *e) * inverse
        for (m, h), e, inverse in zip(pairs, e_parts, inverses)
    ]
    mixed = jnp.concatenate(
        [jnp.concatenate(mixes[HEADS * m : HEADS * (m + 1)], 0) for m in range(step_items)], 1
    )

    o_hi, o_lo = split(mixed)
    attn_hat, attn_rstd = layer_norm(narrow(out_f[...], o_hi, o_lo) + spread_cols(2))

    def gain(base):
        return per_item(lambda m: 1.0 + col(base) + leads[m] * col(base + 1))

    def shift(base):
        return per_item(lambda m: col(base + 2) + leads[m] * col(base + 3))

    gain0 = gain(4)
    first = normed + attn_hat * gain0 + shift(4)
    f_hi, f_lo = split(first)

    up_bias = jnp.concatenate([up_cols_ref[...]] * step_items, 1)
    u = narrow(up_f[...], f_hi, f_lo) + up_bias
    phi, bell = normal_parts(u)
    hidden = u * phi
    slope = phi + u * bell
    h_hi, h_lo = split(hidden)
    branch = wide(down_f, h_hi, h_lo) + spread_cols(3)
    hat, rstd = layer_norm(branch)
    gain1 = gain(8)
    out = first + hat * gain1 + shift(8)
    for m in range(step_items):
        scatter(of_item(out, m), out_keep, 0, m)

    def norm_back(g, hat, rstd, gain, base):
        weighted = g * hat
        for m in range(step_items):
            a, b = of_item(weighted, m), of_item(g, m)
            sums_ref[base] += a
            sums_ref[base + 1] += leads[m] * a
            sums_ref[base + 2] += b
            sums_ref[base + 3] += leads[m] * b
        e = g * gain
        return (e - mean_rows(e) - hat * mean_rows(e * hat)) * rstd

    def add_items(v):
        total = of_item(v, 0)
        for m in range(1, step_items):
            total = total + of_item(v, m)
        return total

    ones_rows = jnp.where(
        lax.broadcasted_iota(jnp.int32, (LANES - WIDTH, step_items * PAIR), 0) == 0, 1.0, 0.0
    ).astype(bf16)
    zero_rows = jnp.zeros((LANES - WIDTH, step_items * PAIR), bf16)

    def outer(a_hi, a_lo, b_hi, b_lo):
        right = jnp.concatenate([b_hi, ones_rows, b_lo, zero_rows], 0)
        r = dot_rows(stack_rows(a_hi, a_lo), right)
        m = a_hi.shape[0]
        return (r[:m, :LANES] + r[m:, :LANES]) + r[:m, LANES:]

    cot = per_item(lambda m: gather(ct_own, 1, m))
    d_branch = norm_back(cot, hat, rstd, gain1, 4)
    sums_ref[8] += add_items(d_branch)
    z_hi, z_lo = split(d_branch)
    g_down_ref[...] += outer(h_hi, h_lo, z_hi, z_lo)
    d_pre = narrow(down_b[...], z_hi, z_lo) * slope
    p_hi, p_lo = split(d_pre)
    g_up_ref[...] += outer(p_hi, p_lo, f_hi, f_lo)
    d_first = cot + wide(up_b, p_hi, p_lo)
    d_attn = norm_back(d_first, attn_hat, attn_rstd, gain0, 0)
    a_hi, a_lo = split(d_attn)
    g_out_ref[...] += outer(a_hi, a_lo, o_hi, o_lo)
    d_mixed = narrow(out_b[...], a_hi, a_lo)

    d_outs = [
        of_item(d_mixed, m)[h * HEAD_DIM : (h + 1) * HEAD_DIM] * inverse
        for (m, h), inverse in zip(pairs, inverses)
    ]
    d_parts = [split(d) for d in d_outs]
    d_probs = [
        three(*split(of_item(v_rows[h], m)), *d) for (m, h), d in zip(pairs, d_parts)
    ]
    s_parts = []
    for n, (m, h) in enumerate(pairs):
        delta = jnp.sum(d_outs[n] * mixes[n], 0, keepdims=True)
        d_scores = expos[n] * (d_probs[n] - delta)
        dpos_ref[h] += d_scores
        folded = d_scores * cosines[n]
        total = folded[0:8]
        for i in range(1, PLACES // 8):
            total = total + folded[8 * i : 8 * i + 8]
        dcos_ref[h] += total
        s_parts.append(split(d_scores))
    dv_rows = [over_queries(*d, *e) for d, e in zip(d_parts, e_parts)]
    dk_rows = [over_queries(*q, *d) for q, d in zip(q_parts, s_parts)]
    dq_rows = [
        over_keys(side_by_side(of_item(k_rows[h], m)), *d) for (m, h), d in zip(pairs, s_parts)
    ]

    def unit_back(grads, rows, inverse):
        out = []
        for n, (m, h) in enumerate(pairs):
            d = grads[n] * scale_ref[h : h + 1, :]
            row = of_item(rows[h], m)
            d = d - row * jnp.sum(row * d, 0, keepdims=True)
            out.append(d * of_item(inverse[h], m))
        return out

    dq_rows = unit_back(dq_rows, q_rows, q_inv)
    dk_rows = unit_back(dk_rows, k_rows, k_inv)
    d_joined = jnp.concatenate(
        [
            jnp.concatenate(
                [d for rows in (dq_rows, dk_rows, dv_rows) for d in rows[HEADS * m : HEADS * (m + 1)]], 0
            )
            for m in range(step_items)
        ],
        1,
    )
    j_hi, j_lo = split(d_joined)
    g_qkv_ref[...] += outer(j_hi, j_lo, n_hi, n_lo)
    d_normed = d_first + wide(qkv_b, j_hi, j_lo)
    sums_ref[9] += add_items(d_normed)
    sums_ref[10] += add_items(d_normed * normed)
    for m in range(step_items):
        scatter(of_item(d_normed, m), dn_keep, 1, m)

    @pl.when(step == pl.num_programs(0) - 1)
    def _():
        def lane_sums(v):
            return jnp.sum(v.T, 0, keepdims=True)

        flat_ref[...] = jnp.zeros_like(flat_ref)
        g = g_qkv_ref[...].T
        flat_ref[0:96, :] = g[:WIDTH, :LANES]
        flat_ref[96:192, :] = g[:WIDTH, LANES : 2 * LANES]
        qv = g[WIDTH : WIDTH + 1]
        g_out = g_out_ref[...].T
        flat_ref[192:288, :] = jnp.concatenate([g_out[:WIDTH], g[:WIDTH, 2 * LANES :]], 1)
        g_up = g_up_ref[...].T
        g_down = g_down_ref[...].T
        for k in range(3):
            lanes = slice(k * LANES, (k + 1) * LANES)
            flat_ref[288 + 96 * k : 384 + 96 * k, :] = g_up[:WIDTH, lanes]
            flat_ref[576 + 96 * k : 672 + 96 * k, :] = g_down[:WIDTH, lanes]
            flat_ref[876 + k : 877 + k, :] = g_up[WIDTH : WIDTH + 1, lanes]
        totals = [lane_sums(sums_ref[i]) for i in range(11)]
        for i in range(8):
            flat_ref[864 + i : 865 + i, :WIDTH] = totals[i]
        flat_ref[872:873, :WIDTH] = totals[8]
        flat_ref[873:874, :WIDTH] = g_out[WIDTH : WIDTH + 1]
        flat_ref[874:875, :WIDTH] = qv[:, :WIDTH]
        flat_ref[875:876, :WIDTH] = qv[:, 2 * WIDTH :]
        lane = lax.broadcasted_iota(jnp.int32, (1, LANES), 1)
        scales = jnp.zeros((1, LANES), f32)
        for h in range(HEADS):
            total = jnp.sum(jnp.sum(dcos_ref[h], 0, keepdims=True), 1, keepdims=True)
            scales = jnp.where(lane == WIDTH + h, total * scale_ref[h : h + 1, :], scales)
        flat_ref[864:865, :] = flat_ref[864:865, :] + scales

        rows = []
        for h in range(HEADS):
            d = dpos_ref[h]
            d = jnp.where(first_half, d + pltpu.roll(d, PLACES, 1), 0.0)
            tile = jnp.zeros((WINDOW, LANES), f32)
            for j in range(WINDOW):
                tile = tile + pltpu.roll(d[8 * j : 8 * j + 8], 56 - 8 * j, 1)
            rows.append(jnp.concatenate([tile[r : r + 1] for r in range(WINDOW)], 1))
        rows.append(jnp.zeros((8 - HEADS, WINDOW * LANES), f32))
        d_table = exact(jnp.concatenate(rows, 0), one_hot(target_ref[...]), ((1,), (1,)))
        net, coords = net_ref[...], coords_ref[...]
        column, hidden, slope = bias_net(net, coords)
        gate = 1.0 / (1.0 + jnp.exp(-exact(head_rows(net), hidden, ((1,), (0,)))))
        d_logit = d_table * (16.0 * gate * (1.0 - gate))
        g_w2 = exact(d_logit, hidden, ((1,), (1,)))
        d_hidden = column(3) * d_logit[0:1] + column(4) * d_logit[1:2] + column(5) * d_logit[2:3]
        g_first = exact(coords, d_hidden * slope, ((1,), (1,)))
        for i, row in enumerate(
            [g_first[0:1], g_first[1:2], g_first[2:3], g_w2[0:1], g_w2[1:2], g_w2[2:3]]
        ):
            for k in range(4):
                at = 879 + 4 * i + k
                flat_ref[at : at + 1, :] = row[:, k * LANES : (k + 1) * LANES]

        slots, slot_rows, _ = grads_ref.shape
        share = slot_rows - 2
        for j in range(slots):
            grads_ref[j, 0:share, :] = flat_ref[share * j : share * (j + 1), :]
        for i in range(2):
            grads_ref[:, share + i : share + i + 1, :WIDTH] = jnp.broadcast_to(
                totals[9 + i][None], (slots, 1, WIDTH)
            )
            grads_ref[:, share + i : share + i + 1, WIDTH:] = jnp.zeros(
                (slots, 1, LANES - WIDTH), f32
            )


def run_block(flags, lead, x, ct, halo, stats, running, prepared, net, coords, target, token_count):
    items, tile_rows, flat = x.shape
    half = flat // 2
    step_items = block_of(items)

    def own(i):
        return (i, 0, 1)

    def rows(n):
        return pl.BlockSpec((step_items, n, half), lambda i: (i, 0, 0))

    smem = pl.BlockSpec(memory_space=pltpu.SMEM)
    field = pl.BlockSpec((step_items, tile_rows, half), own)
    out_rows = (12, 12, 24, 8, 8)
    slots = stats.shape[0]
    slot_rows = -(-PAYLOAD // slots)
    slot_rows = -(-(slot_rows + 2) // 8) * 8
    tail = [
        jax.ShapeDtypeStruct((slots, slot_rows, LANES), f32),
        jax.ShapeDtypeStruct((8, LANES), f32),
    ]
    return pl.pallas_call(
        partial(block_kernel, step_items, float(token_count)),
        grid=(items // step_items,),
        in_specs=[smem, smem, field, rows(24), rows(8), rows(8), field]
        + [whole(a) for a in (stats, running, *prepared, net, coords, target)],
        out_specs=[rows(n) for n in out_rows] + [whole(a) for a in tail],
        out_shape=[jax.ShapeDtypeStruct((items, n, half), f32) for n in out_rows] + tail,
        scratch_shapes=[
            pltpu.VMEM((2, WIDTH, LANES), f32),
            pltpu.VMEM((3 * WIDTH, LANES), f32),
            pltpu.VMEM((WIDTH, LANES), f32),
            pltpu.VMEM((HIDDEN, LANES), f32),
            pltpu.VMEM((HIDDEN, LANES), f32),
            pltpu.VMEM((11, WIDTH, LANES), f32),
            pltpu.VMEM((HEADS, PLACES, LANES), f32),
            pltpu.VMEM((HEADS, 8, LANES), f32),
            pltpu.VMEM((slots * (slot_rows - 2), LANES), f32),
        ],
        compiler_params=in_order,
    )(flags, lead, x, *halo, ct, stats, running, *prepared, net, coords, target)


def place(ref_out, m, keep, right, down, corner, part, fn):
    half = keep.shape[2]
    at, low = 12 * part, 4 * part
    for rows, left, own in (
        (slice(0, SHIFT), corner[m, low : low + SHIFT, :], down[m, low : low + SHIFT, :]),
        (slice(SHIFT, 16), right[m, at : at + 12, :], keep[m]),
    ):
        for lanes, value in ((slice(0, half), left), (slice(half, 2 * half), own)):
            ref_out[m, rows, lanes] = fn(value, rows, lanes)


def outputs_kernel(keep_ref, right_ref, down_ref, corner_ref, out_ref):
    for m in range(out_ref.shape[0]):
        place(out_ref, m, keep_ref, right_ref, down_ref, corner_ref, 0, lambda v, r, l: v)


def input_grad_kernel(
    token_count, x_ref, keep_ref, right_ref, down_ref, corner_ref, norm_ref, sums_ref, out_ref
):
    cols = x_ref.shape[2] // WIDTH

    def wide(row):
        return jnp.concatenate([row[:, :WIDTH]] * cols, 1)

    mean, inv_std = norm_ref[0:1], norm_ref[1:2]
    at = sums_ref.shape[0] - 2
    mean_grad = sums_ref[at : at + 1] * (1.0 / token_count)
    mean_cross = sums_ref[at + 1 : at + 2] * (1.0 / token_count)
    factor, centre = wide(inv_std), wide(mean)
    offset, slope = wide(inv_std * mean_grad), wide(inv_std * inv_std * mean_cross)
    for m in range(x_ref.shape[0]):

        def grad(v, rows, lanes):
            x = x_ref[m, rows, lanes] - centre[:, lanes]
            return factor[:, lanes] * v - offset[:, lanes] - x * slope[:, lanes]

        place(out_ref, m, keep_ref, right_ref, down_ref, corner_ref, 1, grad)


def final_specs(x_shape):
    items, rows, flat = x_shape
    step_items = block_of(items)

    def spec(n):
        return pl.BlockSpec((step_items, n, flat // 2), lambda i: (i, 0, 0))

    field = pl.BlockSpec((step_items, rows, flat), lambda i: (i, 0, 0))
    return (items // step_items,), field, [spec(12), spec(24), spec(8), spec(8)]


def place_outputs(x_shape, parts):
    grid, field, specs = final_specs(x_shape)
    return pl.pallas_call(
        outputs_kernel,
        grid=grid,
        in_specs=specs,
        out_specs=field,
        out_shape=jax.ShapeDtypeStruct(x_shape, f32),
        compiler_params=in_order,
    )(*parts)


def input_grad(x, parts, norm, sums, token_count):
    grid, field, specs = final_specs(x.shape)
    return pl.pallas_call(
        partial(input_grad_kernel, float(token_count)),
        grid=grid,
        in_specs=[field]
        + specs
        + [pl.BlockSpec(a.shape, lambda i: (0, 0)) for a in (norm, sums)],
        out_specs=field,
        out_shape=jax.ShapeDtypeStruct(x.shape, f32),
        compiler_params=in_order,
    )(x, *parts, norm, sums)


def unpack_kernel(
    all_ref,
    qkv_ref,
    qv_ref,
    scale_ref,
    w1_ref,
    b1_ref,
    w2_ref,
    out_ref,
    b_out_ref,
    up_ref,
    b_up_ref,
    down_ref,
    b_down_ref,
    norm_ref,
    flat_ref,
):
    slots, slot_rows, _ = all_ref.shape
    share = slot_rows - 2
    for j in range(slots):
        flat_ref[share * j : share * (j + 1), :] = all_ref[j, 0:share, :]
    qkv_ref[:, 0:LANES] = flat_ref[0:96, :]
    qkv_ref[:, LANES : 2 * LANES] = flat_ref[96:192, :]
    qkv_ref[:, 2 * LANES :] = flat_ref[192:288, WIDTH:]
    out_ref[...] = flat_ref[192:288, :WIDTH]
    for k in range(3):
        lanes = slice(k * LANES, (k + 1) * LANES)
        up_ref[:, lanes] = flat_ref[288 + 96 * k : 384 + 96 * k, :]
        down_ref[:, lanes] = flat_ref[576 + 96 * k : 672 + 96 * k, :]
        b_up_ref[:, lanes] = flat_ref[876 + k : 877 + k, :]
    norm_ref[...] = flat_ref[864:872, :WIDTH]
    scale_ref[...] = flat_ref[864:865, WIDTH : WIDTH + HEADS]
    b_down_ref[...] = flat_ref[872:873, :WIDTH]
    b_out_ref[...] = flat_ref[873:874, :WIDTH]
    qv_ref[...] = flat_ref[874:876, :WIDTH]
    for k in range(4):
        lanes = slice(k * LANES, (k + 1) * LANES)
        for i in range(2):
            w1_ref[i : i + 1, lanes] = flat_ref[879 + 4 * i + k : 880 + 4 * i + k, :]
        b1_ref[:, lanes] = flat_ref[887 + k : 888 + k, :]
        for i in range(3):
            w2_ref[i : i + 1, lanes] = flat_ref[891 + 4 * i + k : 892 + 4 * i + k, :]


def unpack(everything):
    slots, slot_rows, _ = everything.shape
    shapes = [
        (WIDTH, 3 * WIDTH),
        (2, WIDTH),
        (1, HEADS),
        (2, 512),
        (1, 512),
        (HEADS, 512),
        (WIDTH, WIDTH),
        (1, WIDTH),
        (WIDTH, HIDDEN),
        (1, HIDDEN),
        (WIDTH, HIDDEN),
        (1, WIDTH),
        (8, WIDTH),
    ]
    shapes = [jax.ShapeDtypeStruct(s, f32) for s in shapes]
    return pl.pallas_call(
        unpack_kernel,
        grid=(1,),
        in_specs=[whole(everything)],
        out_specs=[whole(a) for a in shapes],
        out_shape=shapes,
        compiler_params=in_order,
        scratch_shapes=[pltpu.VMEM((slots * (slot_rows - 2), LANES), f32)],
    )(everything)


def take_from(block, dy, dx):
    rows, cols = lax.axis_size("ty"), lax.axis_size("tx")
    route = []
    for i in range(rows * cols):
        y, x = divmod(i, cols)
        route.append((((y + dy) % rows) * cols + (x + dx) % cols, i))
    return lax.ppermute(block, ("ty", "tx"), route)


def exchange(slots):
    return lax.all_to_all(slots, axes_all, 0, 0, tiled=True)


def shards(
    inputs,
    regions,
    lead_step_index,
    running_channel_mean,
    running_channel_variance,
    query_key_value_weight,
    query_value_bias,
    log_cosine_scale,
    bias_net_weight1,
    bias_net_bias1,
    bias_net_weight2,
    output_weight,
    projection_bias,
    up_weight,
    up_bias,
    down_weight,
    down_bias,
    conditioned_norm_values,
    cotangent,
):
    items, tile_rows, flat = inputs.shape
    devices = lax.axis_size(axes_all)
    token_count = items * tile_rows * (flat // WIDTH) * devices

    stats, right, down, corner = pack(inputs, cotangent, devices)
    halo = (take_from(right, 0, 1), take_from(down, 1, 0), take_from(corner, 1, 1))
    stats = exchange(stats)

    row_cut = regions[:, ::WINDOW, 0] != regions[:, WINDOW - 1 :: WINDOW, 0]
    col_cut = regions[:, ::WINDOW, 0] != regions[:, ::WINDOW, WINDOW - 1]
    flags = (2 * row_cut.astype(jnp.int32) + col_cut.astype(jnp.int32)).reshape(-1)
    rows = jnp.concatenate(
        [
            query_value_bias,
            projection_bias[None],
            down_bias[None],
            conditioned_norm_values.reshape(8, WIDTH),
        ],
        0,
    )
    net = jnp.concatenate(
        [
            bias_net_weight1,
            bias_net_bias1[None],
            bias_net_weight2.T,
            jnp.zeros((2, bias_net_bias1.shape[0]), f32),
        ],
        0,
    )
    coords, target = offset_constants()
    weights = (query_key_value_weight, output_weight, up_weight, down_weight)
    prepared = prepare(weights, rows, up_bias[None], log_cosine_scale, net, coords, target)
    running = jnp.stack([running_channel_mean, running_channel_variance])
    out_keep, dn_keep, right, down, corner, grads, norm = run_block(
        flags,
        lead_step_index,
        inputs,
        cotangent,
        halo,
        stats,
        running,
        prepared,
        net,
        coords,
        target,
        token_count,
    )
    halo = (take_from(right, 0, -1), take_from(down, -1, 0), take_from(corner, -1, -1))
    share = jnp.sum(exchange(grads), 0)
    share, halo = lax.optimization_barrier((share, halo))
    outputs = place_outputs(inputs.shape, (out_keep,) + halo)
    grad_inputs = input_grad(inputs, (dn_keep,) + halo, norm, share, token_count)
    everything = exchange(jnp.broadcast_to(share[None], grads.shape))
    (
        g_qkv,
        g_qv,
        g_scale,
        g_w1,
        g_b1,
        g_w2,
        g_out,
        g_b_out,
        g_up,
        g_b_up,
        g_down,
        g_b_down,
        g_norm,
    ) = unpack(everything)
    return (
        outputs,
        grad_inputs,
        g_qkv,
        g_qv,
        g_scale.reshape(-1),
        g_w1,
        g_b1.reshape(-1),
        g_w2.T,
        g_out,
        g_b_out.reshape(-1),
        g_up,
        g_b_up.reshape(-1),
        g_down,
        g_b_down.reshape(-1),
        g_norm.reshape(2, 4, WIDTH),
        norm[2, :WIDTH],
        norm[3, :WIDTH],
    )


def solution(mesh):
    tiled = P("items", "ty", "tx")
    placed = (tiled, tiled, P("items")) + (P(),) * 15 + (tiled,)
    return jax.shard_map(
        shards,
        mesh=mesh,
        in_specs=placed,
        out_specs=(tiled, tiled) + (P(),) * 15,
        check_vma=False,
    )
```

```python
from functools import partial

import jax
import jax.numpy as jnp
import numpy as np
from jax import lax
from jax.experimental import pallas as pl
from jax.experimental.pallas import tpu as pltpu
from jax.sharding import PartitionSpec as P

HEADS = 3
HEAD_DIM = 32
WIDTH = 96
HIDDEN = 384
WINDOW = 8
SHIFT = 4
LEAD_STEPS = 14
PLACES = WINDOW * WINDOW
SPAN = 2 * WINDOW - 1
PAIR = 2 * PLACES
LANES = 128
OFFSETS = 256
PAYLOAD = 903
PARTS = 2

masked_score = -1000000000.0
norm_eps = 1e-05
unit_eps = 1e-06
momentum = 0.1
axes_all = ("ty", "tx", "items")

f32 = jnp.float32
bf16 = jnp.bfloat16

in_order = pltpu.CompilerParams(
    dimension_semantics=("arbitrary",), vmem_limit_bytes=60 * 1024 * 1024
)


def about(microseconds):
    return pl.CostEstimate(flops=microseconds * 10**9, bytes_accessed=10**6, transcendentals=0)


def block_of(items, most=8):
    return max(n for n in range(1, most + 1) if items % n == 0)


def whole(a):
    return pl.BlockSpec(a.shape, lambda i: (0,) * len(a.shape))


def dot(a, b):
    return lax.dot_general(a, b, (((1,), (0,)), ((), ())), preferred_element_type=f32)


def dot_rows(a, b):
    return lax.dot_general(a, b, (((1,), (1,)), ((), ())), preferred_element_type=f32)


def split(x):
    hi = x.astype(bf16)
    return hi, (x - hi.astype(f32)).astype(bf16)


def normal_parts(u):
    phi = 0.5 + 0.5 * lax.erf(u * 0.7071067811865476)
    return phi, (u * 0.3989422804014327) * jnp.exp(-0.5 * (u * u))


def pack_kernel(items, part_steps, x_ref, ct_ref, ct_top_ref, stats_ref, *refs):
    step = pl.program_id(0)
    step_items, rows, flat = x_ref.shape
    cols = flat // WIDTH
    half = flat // 2

    sums_ref = refs[-1]

    def send(right_ref, down_ref, corner_ref):
        for part, ref in enumerate((x_ref, ct_ref)):
            right_ref[:, 12 * part : 12 * part + 12, :] = ref[:, SHIFT:, :half]
            corner_ref[:, 4 * part : 4 * part + 4, :] = ref[:, :SHIFT, :half]
        down_ref[:, 0:4, :] = x_ref[:, :SHIFT, half:]
        down_ref[:, 4:8, :] = ct_top_ref[:, :SHIFT, :]

    for n in range(PARTS):
        pl.when(step // part_steps == n)(partial(send, *refs[3 * n : 3 * n + 3]))

    def fold(v):
        total = v[:, :WIDTH]
        for j in range(1, cols):
            total = total + v[:, j * WIDTH : (j + 1) * WIDTH]
        return jnp.sum(total, 0, keepdims=True)

    def total(fn):
        acc = jnp.zeros((8, flat), f32)
        for i in range(step_items):
            acc = acc + fn(x_ref[i, 0:8, :]) + fn(x_ref[i, 8:16, :])
        return acc

    @pl.when(step == 0)
    def _():
        pivot = fold(total(lambda v: v)) * (1.0 / (step_items * rows * cols))
        sums_ref[0] = jnp.broadcast_to(jnp.concatenate([pivot] * cols, 1), (8, flat))
        sums_ref[1] = jnp.zeros((8, flat), f32)
        sums_ref[2] = jnp.zeros((8, flat), f32)

    pivot = sums_ref[0]
    sums_ref[1] += total(lambda v: v - pivot)
    sums_ref[2] += total(lambda v: (v - pivot) * (v - pivot))

    @pl.when(step == pl.num_programs(0) - 1)
    def _():
        count = items * rows * cols
        offset = fold(sums_ref[1]) * (1.0 / count)
        square = fold(sums_ref[2]) - count * offset * offset
        pad = jnp.zeros((1, LANES - WIDTH), f32)
        row = jnp.concatenate([sums_ref[0, 0:1, :WIDTH] + offset, pad, square, pad], 1)
        stats_ref[...] = jnp.broadcast_to(row[None], stats_ref.shape)


def spread_kernel(row_ref, out_ref):
    out_ref[...] = jnp.broadcast_to(row_ref[0:1][None], out_ref.shape)


def pack(x, ct, devices):
    items, rows, flat = x.shape
    half = flat // 2
    part_items = items // PARTS
    step_items = block_of(part_items, 16)
    part_steps = part_items // step_items

    def spec(n, width):
        return pl.BlockSpec((step_items, n, width), lambda i: (i, 0, 0))

    def of_part(n, count):
        return pl.BlockSpec(
            (step_items, count, half),
            lambda i: (jnp.clip(i - n * part_steps, 0, part_steps - 1), 0, 0),
        )

    stats = jax.ShapeDtypeStruct((devices, 1, 2 * LANES), f32)
    counts = (24, 8, 8)
    outs = pl.pallas_call(
        partial(pack_kernel, items, part_steps),
        grid=(items // step_items,),
        in_specs=[
            spec(rows, flat),
            spec(rows, half),
            pl.BlockSpec((step_items, 8, half), lambda i: (i, 0, 1)),
        ],
        out_specs=[whole(stats)] + [of_part(n, c) for n in range(PARTS) for c in counts],
        out_shape=[stats]
        + [jax.ShapeDtypeStruct((part_items, c, half), f32) for _ in range(PARTS) for c in counts],
        scratch_shapes=[pltpu.VMEM((3, 8, flat), f32)],
        cost_estimate=about(4),
        compiler_params=in_order,
    )(x, ct, ct)
    stats = outs[0]
    return stats, [outs[1 + 3 * n : 4 + 3 * n] for n in range(PARTS)]


def offset_constants():
    coords = np.zeros((8, OFFSETS), np.float32)
    o = np.arange(SPAN * SPAN)
    for k, along in enumerate((o // SPAN - (WINDOW - 1), o % SPAN - (WINDOW - 1))):
        u = along.astype(np.float32) * np.float32(8.0 / (WINDOW - 1))
        coords[k, : SPAN * SPAN] = np.sign(u) * np.log2(np.abs(u) + np.float32(1.0)) / np.float32(3.0)
    coords[2, : SPAN * SPAN] = 1.0
    key_row, lane = np.divmod(np.arange(WINDOW * LANES), LANES)
    across, row = np.divmod(lane, WINDOW)
    target = (row - key_row + WINDOW - 1) * SPAN + across
    target = np.where(across < SPAN, target, -1).astype(np.int32)
    return jnp.asarray(coords), jnp.asarray(np.broadcast_to(target, (8, target.size)).copy())


def exact(a, b):
    return jnp.dot(a, b, preferred_element_type=f32, precision=lax.Precision.HIGHEST)


def net_columns(net):
    columns = jnp.concatenate([net, jnp.zeros((LANES - 8, net.shape[1]), f32)], 0).T

    def column(i):
        return jnp.broadcast_to(columns[:, i : i + 1], (net.shape[1], OFFSETS))

    return column


def bias_net(net, coords):
    column = net_columns(net)
    u = column(0) * coords[0:1] + column(1) * coords[1:2] + column(2)
    phi, bell = normal_parts(u)
    return u * phi, phi + bell


def head_rows(net):
    return jnp.concatenate([net[3:6], jnp.zeros((5, net.shape[1]), f32)], 0)


def one_hot(target):
    rows = lax.broadcasted_iota(jnp.int32, (OFFSETS, WINDOW * LANES), 0)
    return jnp.where(rows == target[0:1], 1.0, 0.0).astype(bf16)


def three_parts(v):
    hi, lo = split(v)
    rest = v - hi.astype(f32) - lo.astype(f32)
    return jnp.concatenate([hi.astype(f32), lo.astype(f32), rest], 0).astype(bf16)


def add_parts(v):
    return v[:8] + v[8:16] + v[16:]


def prepare_kernel(
    log_scale_ref,
    qv_ref,
    proj_ref,
    down_ref,
    norms_ref,
    up_ref,
    mean_ref,
    var_ref,
    w1_ref,
    b1_ref,
    w2_ref,
    coords_ref,
    target_ref,
    scale_ref,
    bias_ref,
    vec_ref,
    net_ref,
    gate_ref,
):
    def row(ref):
        return ref[...].reshape(1, ref.shape[0])

    vec_ref[...] = jnp.zeros_like(vec_ref)
    vec_ref[0:2, :WIDTH] = qv_ref[...]
    vec_ref[2:3, :WIDTH] = row(proj_ref)
    vec_ref[3:4, :WIDTH] = row(down_ref)
    vec_ref[4:8, :WIDTH] = norms_ref[0]
    vec_ref[8:12, :WIDTH] = norms_ref[1]
    vec_ref[12:13, :HIDDEN] = row(up_ref)
    vec_ref[13:14, :WIDTH] = row(mean_ref)
    vec_ref[14:15, :WIDTH] = row(var_ref)
    units = w1_ref.shape[1]
    net = jnp.concatenate([w1_ref[...], row(b1_ref), w2_ref[...], jnp.zeros((2, units), f32)], 0)
    vec_ref[16:24, :] = net
    lanes = lax.broadcasted_iota(jnp.int32, (1, LANES), 1)
    hidden, slope = bias_net(net, coords_ref[...])
    gate = 1.0 / (1.0 + jnp.exp(-exact(head_rows(net), hidden)))
    net_ref[0] = hidden
    net_ref[1] = slope
    gate_ref[...] = 16.0 * gate * (1.0 - gate)
    spots = one_hot(target_ref[...])
    tiles = add_parts(dot(three_parts(16.0 * gate), spots))
    scale_ref[...] = jnp.zeros_like(scale_ref)
    for h in range(HEADS):
        scale = jnp.exp(jnp.full((1, LANES), log_scale_ref[h], f32))
        scale_ref[h : h + 1, :] = scale
        tile = jnp.concatenate(
            [tiles[h : h + 1, r * LANES : (r + 1) * LANES] for r in range(WINDOW)], 0
        )
        columns = []
        for j in range(WINDOW):
            turned = pltpu.roll(tile, (72 + 8 * j) % LANES, 1)
            columns.append(jnp.where(lanes < PLACES, turned, pltpu.roll(turned, PLACES, 1)))
        bias_ref[h] = jnp.concatenate(columns, 0) - (scale + 16.0)


def prepare(log_scale, vectors, coords, target):
    units = vectors[-1].shape[1]
    shapes = [
        (8, LANES),
        (HEADS, PLACES, LANES),
        (24, units),
        (2, units, OFFSETS),
        (8, OFFSETS),
    ]
    shapes = [jax.ShapeDtypeStruct(a, f32) for a in shapes]
    inputs = (*vectors, coords, target)
    return pl.pallas_call(
        prepare_kernel,
        grid=(1,),
        in_specs=[pl.BlockSpec(memory_space=pltpu.SMEM)] + [whole(a) for a in inputs],
        out_specs=[whole(a) for a in shapes],
        out_shape=shapes,
        cost_estimate=about(0),
        compiler_params=in_order,
    )(log_scale, *inputs)


def packed(w):
    hi, lo = split(w)
    return jnp.concatenate([hi, lo, hi], 1)


def stack_rows(hi, lo):
    return jnp.concatenate([hi, lo], 0)


def block_kernel(
    step_items,
    first_item,
    token_count,
    is_first,
    is_last,
    flags_ref,
    lead_ref,
    x_own,
    x_right,
    x_down,
    x_corner,
    ct_own,
    stats_ref,
    w_qkv_ref,
    w_out_ref,
    w_up_ref,
    w_down_ref,
    scale_ref,
    base_ref,
    vec_ref,
    *refs,
):
    step = pl.program_id(0)
    if is_last:
        (net_ref, gate_ref, coords_ref, target_ref), refs = refs[:4], refs[4:]
    refs, scratch = refs[:-11], refs[-11:]
    qkv_f, out_f, up_f, down_f, down_b, up_b, out_b, qkv_b, cols_ref, up_cols_ref, bias_ref = scratch
    count = len(totals_shapes)
    so_far, refs = (refs[:0], refs) if is_first else (refs[:count], refs[count:])
    out_keep, dn_keep, send_right, send_down, send_corner = refs[:5]
    refs = refs[5:]
    if is_last:
        grads_ref, norm_ref, affine_ref, flat_ref = refs[:4]
        refs = refs[4:]
    else:
        affine_ref, refs = refs[-1], refs[:-1]
    g_qkv_ref, g_out_ref, g_up_ref, g_down_ref, sums_ref, dpos_ref, dcos_ref = refs

    @pl.when(step == 0)
    def _():
        every = stats_ref[...]
        devices = every.shape[0]
        means, squares = every[:, 0, :LANES], every[:, 0, LANES:]
        mean = jnp.sum(means, 0, keepdims=True) * (1.0 / devices)
        apart = means - mean
        var = (
            jnp.sum(squares, 0, keepdims=True) * (1.0 / token_count)
            + jnp.sum(apart * apart, 0, keepdims=True) * (1.0 / devices)
        )
        inv_std = lax.rsqrt(var + norm_eps)
        affine_ref[0] = jnp.broadcast_to(mean, (LANES, LANES)).T[:WIDTH]
        affine_ref[1] = jnp.broadcast_to(inv_std, (LANES, LANES)).T[:WIDTH]
        if is_last:
            pad = jnp.zeros((2, LANES - WIDTH), f32)
            running = jnp.concatenate([vec_ref[13:15, :WIDTH], pad], 1)
            norm_ref[0:1] = mean
            norm_ref[1:2] = inv_std
            norm_ref[2:3] = (1.0 - momentum) * running[0:1] + momentum * mean
            norm_ref[3:4] = (1.0 - momentum) * running[1:2] + momentum * var * (
                token_count / (token_count - 1.0)
            )
            norm_ref[4:8] = jnp.zeros((4, LANES), f32)
        for n, ref in enumerate(refs):
            ref[...] = jnp.zeros_like(ref) if is_first else so_far[n][...]
        qkv_f[...] = packed(w_qkv_ref[...].T)
        qkv_b[...] = packed(w_qkv_ref[...])
        out_f[...] = packed(w_out_ref[...].T)
        out_b[...] = packed(w_out_ref[...])
        up_f[...] = packed(w_up_ref[...].T)
        up_b[...] = packed(w_up_ref[...])
        down_b[...] = packed(w_down_ref[...].T)
        down_f[...] = packed(w_down_ref[...])
        for i in range(cols_ref.shape[0]):
            cols_ref[i] = jnp.broadcast_to(vec_ref[i : i + 1, :WIDTH], (LANES, WIDTH)).T
        up_cols_ref[...] = jnp.broadcast_to(vec_ref[12:13, :HIDDEN], (LANES, HIDDEN)).T
        place = lax.broadcasted_iota(jnp.int32, (PLACES, LANES), 0)
        other = lax.broadcasted_iota(jnp.int32, (PLACES, LANES), 1) % PLACES
        apart_r = (place % WINDOW < SHIFT) != (other % WINDOW < SHIFT)
        apart_c = (place // WINDOW < SHIFT) != (other // WINDOW < SHIFT)
        for h in range(HEADS):
            bias = base_ref[h]
            bias_ref[0, h] = bias
            bias_ref[1, h] = jnp.where(apart_c, masked_score, bias)
            bias_ref[2, h] = jnp.where(apart_r, masked_score, bias)
            bias_ref[3, h] = jnp.where(apart_r | apart_c, masked_score, bias)

    first_half = lax.broadcasted_iota(jnp.int32, (1, PAIR), 1) < PLACES

    def product(weight, x_hi, x_lo):
        return dot(weight[...], jnp.concatenate([x_hi, x_hi, x_lo], 0))

    def halves(v):
        m = v.shape[0] // 2
        return jnp.where(first_half, v[:m], v[m:])

    def col(i):
        return cols_ref[i]

    def per_item(fn):
        return jnp.concatenate([fn(m) for m in range(step_items)], 1)

    def spread_cols(i):
        c = col(i)
        return jnp.concatenate([c] * step_items, 1)

    def gather(own, part, m):
        right, down = 12 * part, 4 * part
        top_l = own[m, SHIFT : SHIFT + WINDOW, :]
        top_r = x_right[m, right : right + WINDOW, :]
        low_l = jnp.concatenate([own[m, SHIFT + WINDOW :, :], x_down[m, down : down + SHIFT, :]], 0)
        low_r = jnp.concatenate(
            [x_right[m, right + WINDOW : right + 12, :], x_corner[m, down : down + SHIFT, :]], 0
        )
        tiles = [
            side[:, j * WIDTH : (j + 1) * WIDTH]
            for side in (top_l, top_r, low_l, low_r)
            for j in range(4)
        ]
        return jnp.concatenate(tiles, 0).T

    def scatter(value, keep, part, m):
        rows = value.T
        sides = [
            jnp.concatenate([rows[(4 * s + j) * 8 : (4 * s + j + 1) * 8] for j in range(4)], 1)
            for s in range(4)
        ]
        right, down = 12 * part, 4 * part
        keep[m, 0:WINDOW, :] = sides[0]
        keep[m, WINDOW:, :] = sides[2][:SHIFT]
        send_right[m, right : right + WINDOW, :] = sides[1]
        send_right[m, right + WINDOW : right + 12, :] = sides[3][:SHIFT]
        send_down[m, down : down + SHIFT, :] = sides[2][SHIFT:]
        send_corner[m, down : down + SHIFT, :] = sides[3][SHIFT:]

    def mean_rows(v):
        return jnp.sum(v, 0, keepdims=True) * (1.0 / WIDTH)

    def layer_norm(v):
        centred = v - mean_rows(v)
        rstd = lax.rsqrt(mean_rows(centred * centred) + norm_eps)
        return centred * rstd, rstd

    items = [first_item + step * step_items + m for m in range(step_items)]
    leads = [(lead_ref[i] + 1).astype(f32) * (1.0 / LEAD_STEPS) for i in items]
    raw = per_item(lambda m: gather(x_own, 0, m))
    mean = jnp.concatenate([affine_ref[0]] * step_items, 1)
    inv_std = jnp.concatenate([affine_ref[1]] * step_items, 1)
    normed = (raw - mean) * inv_std
    n_hi, n_lo = split(normed)

    joined = product(qkv_f, n_hi, n_lo)
    query = joined[:WIDTH] + spread_cols(0)
    key = joined[WIDTH : 2 * WIDTH]
    value = joined[2 * WIDTH :] + spread_cols(1)

    def unit(v):
        rows, inverses = [], []
        for h in range(HEADS):
            part = v[h * HEAD_DIM : (h + 1) * HEAD_DIM]
            inverse = lax.rsqrt(jnp.sum(part * part, 0, keepdims=True) + unit_eps)
            rows.append(part * inverse)
            inverses.append(inverse)
        return rows, inverses

    q_rows, q_inv = unit(query)
    k_rows, k_inv = unit(key)
    v_rows = [value[h * HEAD_DIM : (h + 1) * HEAD_DIM] for h in range(HEADS)]

    def of_item(v, m):
        return v[:, m * PAIR : (m + 1) * PAIR]

    def three(a_hi, a_lo, b_hi, b_lo):
        left = jnp.concatenate([a_hi, a_lo, a_hi], 0)
        right = jnp.concatenate([b_hi, b_hi, b_lo], 0)
        return halves(dot(left.T, right))

    def apart(x):
        zero = jnp.zeros_like(x)
        return jnp.concatenate(
            [jnp.where(first_half, x, zero), jnp.where(first_half, zero, x)], 0
        )

    def two_rows(v_hi, v_lo):
        return jnp.concatenate(
            [
                jnp.concatenate([v_hi, v_hi], 1),
                jnp.concatenate([v_lo, jnp.zeros_like(v_lo)], 1),
            ],
            0,
        )

    def over_keys(v_hi, v_lo, e_hi, e_lo):
        r = dot(two_rows(v_hi, v_lo), stack_rows(apart(e_hi), apart(e_lo)))
        return r[:HEAD_DIM] + r[HEAD_DIM:]

    def over_queries(v_hi, v_lo, e_hi, e_lo):
        weights = jnp.concatenate([e_hi, e_lo], 1)
        r = dot_rows(two_rows(apart(v_hi), apart(v_lo)), stack_rows(weights, weights))
        return halves(r[:PLACES] + r[PLACES:])

    pairs = [(m, h) for m in range(step_items) for h in range(HEADS)]
    q_parts = [split(of_item(q_rows[h], m)) for m, h in pairs]
    k_parts = [split(of_item(k_rows[h], m)) for m, h in pairs]
    v_parts = [split(of_item(v_rows[h], m)) for m, h in pairs]
    cosines = [three(*k, *q) for k, q in zip(k_parts, q_parts)]
    expos, inverses = [], []
    for (m, h), cosine in zip(pairs, cosines):
        flag0, flag1 = flags_ref[0, items[m]], flags_ref[1, items[m]]
        offset = jnp.where(first_half, bias_ref[flag0, h], bias_ref[flag1, h])
        expo = jnp.exp(cosine * scale_ref[h : h + 1, :] + offset)
        expos.append(expo)
        inverses.append(1.0 / jnp.sum(expo, 0, keepdims=True))
    e_parts = [split(e) for e in expos]
    mixes = [
        over_keys(*v, *e) * inverse for v, e, inverse in zip(v_parts, e_parts, inverses)
    ]
    mixed = jnp.concatenate(
        [jnp.concatenate(mixes[HEADS * m : HEADS * (m + 1)], 0) for m in range(step_items)], 1
    )

    o_hi, o_lo = split(mixed)
    attn_hat, attn_rstd = layer_norm(product(out_f, o_hi, o_lo) + spread_cols(2))

    def gain(base):
        return per_item(lambda m: 1.0 + col(base) + leads[m] * col(base + 1))

    def shift(base):
        return per_item(lambda m: col(base + 2) + leads[m] * col(base + 3))

    gain0 = gain(4)
    first = normed + attn_hat * gain0 + shift(4)
    f_hi, f_lo = split(first)

    up_bias = jnp.concatenate([up_cols_ref[...]] * step_items, 1)
    u = product(up_f, f_hi, f_lo) + up_bias
    phi, bell = normal_parts(u)
    hidden = u * phi
    slope = phi + bell
    h_hi, h_lo = split(hidden)
    branch = product(down_f, h_hi, h_lo) + spread_cols(3)
    hat, rstd = layer_norm(branch)
    gain1 = gain(8)
    out = first + hat * gain1 + shift(8)
    for m in range(step_items):
        scatter(of_item(out, m), out_keep, 0, m)

    def norm_back(g, hat, rstd, gain, base):
        weighted = g * hat
        for m in range(step_items):
            a, b = of_item(weighted, m), of_item(g, m)
            sums_ref[base] += a
            sums_ref[base + 1] += leads[m] * a
            sums_ref[base + 2] += b
            sums_ref[base + 3] += leads[m] * b
        e = g * gain
        return (e - mean_rows(e) - hat * mean_rows(e * hat)) * rstd

    def add_items(v):
        total = of_item(v, 0)
        for m in range(1, step_items):
            total = total + of_item(v, m)
        return total

    ones_rows = jnp.where(
        lax.broadcasted_iota(jnp.int32, (LANES - WIDTH, step_items * PAIR), 0) == 0, 1.0, 0.0
    ).astype(bf16)
    zero_rows = jnp.zeros((LANES - WIDTH, step_items * PAIR), bf16)

    def outer(a_hi, a_lo, b_hi, b_lo):
        right = jnp.concatenate([b_hi, ones_rows, b_lo, zero_rows], 0)
        r = dot_rows(stack_rows(a_hi, a_lo), right)
        m = a_hi.shape[0]
        return (r[:m, :LANES] + r[m:, :LANES]) + r[:m, LANES:]

    cot = per_item(lambda m: gather(ct_own, 1, m))
    d_branch = norm_back(cot, hat, rstd, gain1, 4)
    sums_ref[8] += add_items(d_branch)
    z_hi, z_lo = split(d_branch)
    g_down_ref[...] += outer(h_hi, h_lo, z_hi, z_lo)
    d_pre = product(down_b, z_hi, z_lo) * slope
    p_hi, p_lo = split(d_pre)
    g_up_ref[...] += outer(p_hi, p_lo, f_hi, f_lo)
    d_first = cot + product(up_b, p_hi, p_lo)
    d_attn = norm_back(d_first, attn_hat, attn_rstd, gain0, 0)
    a_hi, a_lo = split(d_attn)
    g_out_ref[...] += outer(a_hi, a_lo, o_hi, o_lo)
    d_mixed = product(out_b, a_hi, a_lo)

    d_outs = [
        of_item(d_mixed, m)[h * HEAD_DIM : (h + 1) * HEAD_DIM] * inverse
        for (m, h), inverse in zip(pairs, inverses)
    ]
    d_parts = [split(d) for d in d_outs]
    d_probs = [three(*v, *d) for v, d in zip(v_parts, d_parts)]
    s_parts = []
    for n, (m, h) in enumerate(pairs):
        delta = jnp.sum(d_outs[n] * mixes[n], 0, keepdims=True)
        d_scores = expos[n] * (d_probs[n] - delta)
        dpos_ref[h] += d_scores
        folded = d_scores * cosines[n]
        total = folded[0:8]
        for i in range(1, PLACES // 8):
            total = total + folded[8 * i : 8 * i + 8]
        dcos_ref[h] += total
        s_parts.append(split(d_scores))
    dv_rows = [over_queries(*d, *e) for d, e in zip(d_parts, e_parts)]
    dk_rows = [over_queries(*q, *d) for q, d in zip(q_parts, s_parts)]
    dq_rows = [over_keys(*k, *d) for k, d in zip(k_parts, s_parts)]

    def unit_back(grads, rows, inverse):
        out = []
        for n, (m, h) in enumerate(pairs):
            d = grads[n] * scale_ref[h : h + 1, :]
            row = of_item(rows[h], m)
            d = d - row * jnp.sum(row * d, 0, keepdims=True)
            out.append(d * of_item(inverse[h], m))
        return out

    dq_rows = unit_back(dq_rows, q_rows, q_inv)
    dk_rows = unit_back(dk_rows, k_rows, k_inv)
    d_joined = jnp.concatenate(
        [
            jnp.concatenate(
                [d for rows in (dq_rows, dk_rows, dv_rows) for d in rows[HEADS * m : HEADS * (m + 1)]], 0
            )
            for m in range(step_items)
        ],
        1,
    )
    j_hi, j_lo = split(d_joined)
    g_qkv_ref[...] += outer(j_hi, j_lo, n_hi, n_lo)
    d_normed = d_first + product(qkv_b, j_hi, j_lo)
    sums_ref[9] += add_items(d_normed)
    sums_ref[10] += add_items(d_normed * normed)
    for m in range(step_items):
        scatter(of_item(d_normed, m), dn_keep, 1, m)

    def finish():
        def lane_sums(v):
            return jnp.sum(v.T, 0, keepdims=True)

        flat_ref[...] = jnp.zeros_like(flat_ref)
        g = g_qkv_ref[...].T
        flat_ref[0:96, :] = g[:WIDTH, :LANES]
        flat_ref[96:192, :] = g[:WIDTH, LANES : 2 * LANES]
        qv = g[WIDTH : WIDTH + 1]
        g_out = g_out_ref[...].T
        flat_ref[192:288, :] = jnp.concatenate([g_out[:WIDTH], g[:WIDTH, 2 * LANES :]], 1)
        g_up = g_up_ref[...].T
        g_down = g_down_ref[...].T
        for k in range(3):
            lanes = slice(k * LANES, (k + 1) * LANES)
            flat_ref[288 + 96 * k : 384 + 96 * k, :] = g_up[:WIDTH, lanes]
            flat_ref[576 + 96 * k : 672 + 96 * k, :] = g_down[:WIDTH, lanes]
            flat_ref[876 + k : 877 + k, :] = g_up[WIDTH : WIDTH + 1, lanes]
        totals = [lane_sums(sums_ref[i]) for i in range(11)]
        for i in range(8):
            flat_ref[864 + i : 865 + i, :WIDTH] = totals[i]
        flat_ref[872:873, :WIDTH] = totals[8]
        flat_ref[873:874, :WIDTH] = g_out[WIDTH : WIDTH + 1]
        flat_ref[874:875, :WIDTH] = qv[:, :WIDTH]
        flat_ref[875:876, :WIDTH] = qv[:, 2 * WIDTH :]
        lane = lax.broadcasted_iota(jnp.int32, (1, LANES), 1)
        scales = jnp.zeros((1, LANES), f32)
        for h in range(HEADS):
            total = jnp.sum(jnp.sum(dcos_ref[h], 0, keepdims=True), 1, keepdims=True)
            scales = jnp.where(lane == WIDTH + h, total * scale_ref[h : h + 1, :], scales)
        flat_ref[864:865, :] = flat_ref[864:865, :] + scales

        rows = []
        for h in range(HEADS):
            d = dpos_ref[h]
            d = jnp.where(first_half, d + pltpu.roll(d, PLACES, 1), 0.0)
            tile = jnp.zeros((WINDOW, LANES), f32)
            for j in range(WINDOW):
                tile = tile + pltpu.roll(d[8 * j : 8 * j + 8], 56 - 8 * j, 1)
            rows.append(jnp.concatenate([tile[r : r + 1] for r in range(WINDOW)], 1))
        rows.append(jnp.zeros((8 - HEADS, WINDOW * LANES), f32))
        found = dot_rows(three_parts(jnp.concatenate(rows, 0)), one_hot(target_ref[...]))
        d_table = add_parts(found)
        d_logit = d_table * gate_ref[...]

        def against(v, units):
            v_hi, v_lo = split(v)
            u_hi, u_lo = split(units)
            both = jnp.concatenate([v_hi.astype(f32), v_lo.astype(f32)], 0).astype(bf16)
            r = dot_rows(both, u_hi)
            return r[:8] + r[8:] + dot_rows(v_hi, u_lo)

        g_w2 = against(d_logit, net_ref[0])
        column = net_columns(vec_ref[16:24, :])
        d_hidden = sum(column(3 + h) * d_logit[h : h + 1] for h in range(HEADS))
        g_first = against(coords_ref[...], d_hidden * net_ref[1])
        for i, row in enumerate(
            [g_first[0:1], g_first[1:2], g_first[2:3], g_w2[0:1], g_w2[1:2], g_w2[2:3]]
        ):
            for k in range(4):
                at = 879 + 4 * i + k
                flat_ref[at : at + 1, :] = row[:, k * LANES : (k + 1) * LANES]

        slots, slot_rows, _ = grads_ref.shape
        share = slot_rows - 2
        for j in range(slots):
            grads_ref[j, 0:share, :] = flat_ref[share * j : share * (j + 1), :]
        for i in range(2):
            grads_ref[:, share + i : share + i + 1, :WIDTH] = jnp.broadcast_to(
                totals[9 + i][None], (slots, 1, WIDTH)
            )
            grads_ref[:, share + i : share + i + 1, WIDTH:] = jnp.zeros(
                (slots, 1, LANES - WIDTH), f32
            )

    if is_last:
        finish()


totals_shapes = [
    (3 * WIDTH, LANES),
    (WIDTH, LANES),
    (HIDDEN, LANES),
    (HIDDEN, LANES),
    (11, WIDTH, LANES),
    (HEADS, PLACES, LANES),
    (HEADS, 8, LANES),
]


def run_block(
    part,
    flags,
    lead,
    x,
    ct,
    halo,
    stats,
    weights,
    prepared,
    bias_net_parts,
    so_far,
    token_count,
):
    items, tile_rows, flat = x.shape
    half = flat // 2
    items = items // PARTS
    step_items = block_of(items, 16)
    steps = items // step_items
    is_first, is_last = part == 0, part == PARTS - 1

    def rows(n):
        return pl.BlockSpec((step_items, n, half), lambda i: (i, 0, 0))

    smem = pl.BlockSpec(memory_space=pltpu.SMEM)
    field = pl.BlockSpec((step_items, tile_rows, half), lambda i: (part * steps + i, 0, 1))
    out_rows = (12, 12, 24, 8, 8)
    slots = stats.shape[0]
    slot_rows = -(-PAYLOAD // slots)
    slot_rows = -(-(slot_rows + 2) // 8) * 8
    totals = [jax.ShapeDtypeStruct(s, f32) for s in totals_shapes]
    scratch = [pltpu.VMEM((2, WIDTH, LANES), f32)]
    if is_last:
        tail = [
            jax.ShapeDtypeStruct((slots, slot_rows, LANES), f32),
            jax.ShapeDtypeStruct((8, LANES), f32),
        ]
        scratch.append(pltpu.VMEM((slots * (slot_rows - 2), LANES), f32))
        scratch += [pltpu.VMEM(s, f32) for s in totals_shapes]
    else:
        tail = totals
    scratch += [
        pltpu.VMEM((3 * WIDTH, 3 * WIDTH), bf16),
        pltpu.VMEM((WIDTH, 3 * WIDTH), bf16),
        pltpu.VMEM((HIDDEN, 3 * WIDTH), bf16),
        pltpu.VMEM((WIDTH, 3 * HIDDEN), bf16),
        pltpu.VMEM((HIDDEN, 3 * WIDTH), bf16),
        pltpu.VMEM((WIDTH, 3 * HIDDEN), bf16),
        pltpu.VMEM((WIDTH, 3 * WIDTH), bf16),
        pltpu.VMEM((WIDTH, 9 * WIDTH), bf16),
        pltpu.VMEM((12, WIDTH, LANES), f32),
        pltpu.VMEM((HIDDEN, LANES), f32),
        pltpu.VMEM((4, HEADS, PLACES, LANES), f32),
    ]
    constants = (stats, *weights, *prepared, *(bias_net_parts if is_last else ()), *so_far)
    return pl.pallas_call(
        partial(block_kernel, step_items, part * items, float(token_count), is_first, is_last),
        grid=(steps,),
        in_specs=[smem, smem, field, rows(24), rows(8), rows(8), field]
        + [whole(a) for a in constants],
        out_specs=[rows(n) for n in out_rows] + [whole(a) for a in tail],
        out_shape=[jax.ShapeDtypeStruct((items, n, half), f32) for n in out_rows] + tail,
        scratch_shapes=scratch,
        cost_estimate=about(40),
        compiler_params=in_order,
    )(flags, lead, x, *halo, ct, *constants)


def place(ref_out, m, keep, right, down, corner, part, fn):
    half = keep.shape[2]
    at, low = 12 * part, 4 * part
    for rows, left, own in (
        (slice(0, SHIFT), corner[m, low : low + SHIFT, :], down[m, low : low + SHIFT, :]),
        (slice(SHIFT, 16), right[m, at : at + 12, :], keep[m]),
    ):
        for lanes, value in ((slice(0, half), left), (slice(half, 2 * half), own)):
            ref_out[m, rows, lanes] = fn(value, rows, lanes)


def final_kernel(token_count, part_steps, x_ref, norm_ref, sums_ref, *refs):
    cols = x_ref.shape[2] // WIDTH
    out_ref, grad_ref = refs[-2:]

    def wide(row):
        return jnp.concatenate([row[:, :WIDTH]] * cols, 1)

    mean, inv_std = norm_ref[0:1], norm_ref[1:2]
    at = sums_ref.shape[1] - 2
    mean_grad = sums_ref[0, at : at + 1] * (1.0 / token_count)
    mean_cross = sums_ref[0, at + 1 : at + 2] * (1.0 / token_count)
    factor, centre = wide(inv_std), wide(mean)
    offset, slope = wide(inv_std * mean_grad), wide(inv_std * inv_std * mean_cross)

    def work(out_keep, dn_keep, *halo):
        for m in range(x_ref.shape[0]):

            def grad(v, rows, lanes):
                x = x_ref[m, rows, lanes] - centre[:, lanes]
                return factor[:, lanes] * v - offset[:, lanes] - x * slope[:, lanes]

            place(out_ref, m, out_keep, *halo, 0, lambda v, rows, lanes: v)
            place(grad_ref, m, dn_keep, *halo, 1, grad)

    for n in range(PARTS):
        pl.when(pl.program_id(0) // part_steps == n)(partial(work, *refs[5 * n : 5 * n + 5]))


def finish_fields(x, parts, norm, sums, token_count):
    items, rows, flat = x.shape
    step_items = block_of(items // PARTS, 16)
    part_steps = items // PARTS // step_items

    def spec(part, n):
        return pl.BlockSpec(
            (step_items, n, flat // 2),
            lambda i: (jnp.clip(i - part * part_steps, 0, part_steps - 1), 0, 0),
        )

    field = pl.BlockSpec((step_items, rows, flat), lambda i: (i, 0, 0))
    return pl.pallas_call(
        partial(final_kernel, float(token_count), part_steps),
        grid=(items // step_items,),
        in_specs=[
            field,
            whole(norm),
            pl.BlockSpec((1,) + sums.shape[1:], lambda i: (0, 0, 0)),
        ]
        + [spec(part, n) for part in range(PARTS) for n in (12, 12, 24, 8, 8)],
        out_specs=[field] * 2,
        out_shape=[jax.ShapeDtypeStruct(x.shape, f32)] * 2,
        cost_estimate=about(60),
        compiler_params=in_order,
    )(x, norm, sums, *[a for part in parts for a in part])


def sum_slots_kernel(slots_ref, all_ref):
    total = slots_ref[0]
    for j in range(1, slots_ref.shape[0]):
        total = total + slots_ref[j]
    all_ref[...] = jnp.broadcast_to(total[None], all_ref.shape)


def sum_slots(slots):
    return pl.pallas_call(
        sum_slots_kernel,
        grid=(1,),
        in_specs=[whole(slots)],
        out_specs=whole(slots),
        out_shape=jax.ShapeDtypeStruct(slots.shape, f32),
        compiler_params=pltpu.CompilerParams(vmem_limit_bytes=16 * 1024 * 1024),
    )(slots)


def unpack_kernel(
    all_ref,
    qkv_ref,
    qv_ref,
    scale_ref,
    w1_ref,
    b1_ref,
    w2_ref,
    out_ref,
    b_out_ref,
    up_ref,
    b_up_ref,
    down_ref,
    b_down_ref,
    norm_ref,
    flat_ref,
):
    slots, slot_rows, _ = all_ref.shape
    share = slot_rows - 2
    for j in range(slots):
        flat_ref[share * j : share * (j + 1), :] = all_ref[j, 0:share, :]
    qkv_ref[:, 0:LANES] = flat_ref[0:96, :]
    qkv_ref[:, LANES : 2 * LANES] = flat_ref[96:192, :]
    qkv_ref[:, 2 * LANES :] = flat_ref[192:288, WIDTH:]
    out_ref[...] = flat_ref[192:288, :WIDTH]
    for k in range(3):
        lanes = slice(k * LANES, (k + 1) * LANES)
        up_ref[:, lanes] = flat_ref[288 + 96 * k : 384 + 96 * k, :]
        down_ref[:, lanes] = flat_ref[576 + 96 * k : 672 + 96 * k, :]
        b_up_ref[k : k + 1, :] = flat_ref[876 + k : 877 + k, :]
    norm_ref[...] = flat_ref[864:872, :WIDTH]
    scale_ref[...] = flat_ref[864:865, WIDTH : WIDTH + HEADS]
    b_down_ref[...] = flat_ref[872:873, :WIDTH]
    b_out_ref[...] = flat_ref[873:874, :WIDTH]
    qv_ref[...] = flat_ref[874:876, :WIDTH]
    for k in range(4):
        lanes = slice(k * LANES, (k + 1) * LANES)
        for i in range(2):
            w1_ref[i : i + 1, lanes] = flat_ref[879 + 4 * i + k : 880 + 4 * i + k, :]
        b1_ref[:, lanes] = flat_ref[887 + k : 888 + k, :]
        for i in range(3):
            w2_ref[i : i + 1, lanes] = flat_ref[891 + 4 * i + k : 892 + 4 * i + k, :]


def unpack(everything):
    slots, slot_rows, _ = everything.shape
    shapes = [
        (WIDTH, 3 * WIDTH),
        (2, WIDTH),
        (1, HEADS),
        (2, 512),
        (1, 512),
        (HEADS, 512),
        (WIDTH, WIDTH),
        (1, WIDTH),
        (WIDTH, HIDDEN),
        (3, LANES),
        (WIDTH, HIDDEN),
        (1, WIDTH),
        (8, WIDTH),
    ]
    shapes = [jax.ShapeDtypeStruct(s, f32) for s in shapes]
    return pl.pallas_call(
        unpack_kernel,
        grid=(1,),
        in_specs=[whole(everything)],
        out_specs=[whole(a) for a in shapes],
        out_shape=shapes,
        compiler_params=pltpu.CompilerParams(vmem_limit_bytes=16 * 1024 * 1024),
        scratch_shapes=[pltpu.VMEM((slots * (slot_rows - 2), LANES), f32)],
    )(everything)


def take_from(block, dy, dx):
    rows, cols = lax.axis_size("ty"), lax.axis_size("tx")
    route = []
    for i in range(rows * cols):
        y, x = divmod(i, cols)
        route.append((((y + dy) % rows) * cols + (x + dx) % cols, i))
    return lax.ppermute(block, ("ty", "tx"), route)


def exchange(slots):
    return lax.all_to_all(slots, axes_all, 0, 0, tiled=True)


def shards(
    inputs,
    regions,
    lead_step_index,
    running_channel_mean,
    running_channel_variance,
    query_key_value_weight,
    query_value_bias,
    log_cosine_scale,
    bias_net_weight1,
    bias_net_bias1,
    bias_net_weight2,
    output_weight,
    projection_bias,
    up_weight,
    up_bias,
    down_weight,
    down_bias,
    conditioned_norm_values,
    cotangent,
):
    items, tile_rows, flat = inputs.shape
    devices = lax.axis_size(axes_all)
    token_count = items * tile_rows * (flat // WIDTH) * devices

    stats, sent = pack(inputs, cotangent, devices)
    halos = []
    for part, (right, down, corner) in enumerate(sent):
        if part:
            (right, down, corner), halos[-1] = lax.optimization_barrier(
                ((right, down, corner), halos[-1])
            )
        halos.append((take_from(right, 0, 1), take_from(down, 1, 0), take_from(corner, 1, 1)))
    stats = exchange(stats)

    corners = regions.transpose(1, 2, 0)
    row_cut = corners[::WINDOW, 0] != corners[WINDOW - 1 :: WINDOW, 0]
    col_cut = corners[::WINDOW, 0] != corners[::WINDOW, WINDOW - 1]
    flags = 2 * row_cut.astype(jnp.int32) + col_cut.astype(jnp.int32)
    vectors = (
        query_value_bias,
        projection_bias,
        down_bias,
        conditioned_norm_values,
        up_bias,
        running_channel_mean,
        running_channel_variance,
        bias_net_weight1,
        bias_net_bias1,
        bias_net_weight2.T,
    )
    coords, target = offset_constants()
    weights = (query_key_value_weight, output_weight, up_weight, down_weight)
    *prepared, net, gate = prepare(log_cosine_scale, vectors, coords, target)
    bias_net_parts = (net, gate, coords, target)
    totals, out_parts, dn_parts, home = [], [], [], []
    for part in range(PARTS):
        out_keep, dn_keep, right, down, corner, *totals = run_block(
            part,
            flags,
            lead_step_index,
            inputs,
            cotangent,
            halos[part],
            stats,
            weights,
            prepared,
            bias_net_parts,
            totals,
            token_count,
        )
        home.append((take_from(right, 0, -1), take_from(down, -1, 0), take_from(corner, -1, -1)))
        out_parts.append(out_keep)
        dn_parts.append(dn_keep)
    grads, norm = totals
    shares = sum_slots(exchange(grads))
    outputs, grad_inputs = finish_fields(
        inputs,
        [(o, d, *h) for o, d, h in zip(out_parts, dn_parts, home)],
        norm,
        shares,
        token_count,
    )
    everything = exchange(shares)
    (
        g_qkv,
        g_qv,
        g_scale,
        g_w1,
        g_b1,
        g_w2,
        g_out,
        g_b_out,
        g_up,
        g_b_up,
        g_down,
        g_b_down,
        g_norm,
    ) = unpack(everything)
    return (
        outputs,
        grad_inputs,
        g_qkv,
        g_qv,
        g_scale.reshape(-1),
        g_w1,
        g_b1.reshape(-1),
        g_w2.T,
        g_out,
        g_b_out.reshape(-1),
        g_up,
        g_b_up.reshape(-1),
        g_down,
        g_b_down.reshape(-1),
        g_norm.reshape(2, 4, WIDTH),
        norm[2, :WIDTH],
        norm[3, :WIDTH],
    )


def solution(mesh):
    tiled = P("items", "ty", "tx")
    placed = (tiled, tiled, P("items")) + (P(),) * 15 + (tiled,)
    return jax.shard_map(
        shards,
        mesh=mesh,
        in_specs=placed,
        out_specs=(tiled, tiled) + (P(),) * 15,
        check_vma=False,
    )
```

```python
from functools import partial

import jax
import jax.numpy as jnp
import numpy as np
from jax import lax
from jax.experimental import pallas as pl
from jax.experimental.pallas import tpu as pltpu
from jax.sharding import PartitionSpec as P

HEADS = 3
HEAD_DIM = 32
WIDTH = 96
HIDDEN = 384
WINDOW = 8
SHIFT = 4
LEAD_STEPS = 14
PLACES = WINDOW * WINDOW
SPAN = 2 * WINDOW - 1
PAIR = 2 * PLACES
LANES = 128
OFFSETS = 256
PAYLOAD = 903
PARTS = 2

masked_score = -1000000000.0
norm_eps = 1e-05
unit_eps = 1e-06
momentum = 0.1
axes_all = ("ty", "tx", "items")

f32 = jnp.float32
bf16 = jnp.bfloat16

in_order = pltpu.CompilerParams(
    dimension_semantics=("arbitrary",), vmem_limit_bytes=60 * 1024 * 1024
)


def about(microseconds):
    return pl.CostEstimate(flops=microseconds * 10**9, bytes_accessed=10**6, transcendentals=0)


def block_of(items, most=8):
    return max(n for n in range(1, most + 1) if items % n == 0)


def whole(a):
    return pl.BlockSpec(a.shape, lambda i: (0,) * len(a.shape))


def dot(a, b):
    return lax.dot_general(a, b, (((1,), (0,)), ((), ())), preferred_element_type=f32)


def dot_rows(a, b):
    return lax.dot_general(a, b, (((1,), (1,)), ((), ())), preferred_element_type=f32)


def split(x):
    hi = x.astype(bf16)
    return hi, (x - hi.astype(f32)).astype(bf16)


def normal_parts(u):
    phi = 0.5 + 0.5 * lax.erf(u * 0.7071067811865476)
    return phi, (u * 0.3989422804014327) * jnp.exp(-0.5 * (u * u))


def pack_halo(fields, tops, right_ref, down_ref, corner_ref):
    for part, (ref, top) in enumerate(zip(fields, tops)):
        right_ref[:, 12 * part : 12 * part + 12, :] = ref[:, SHIFT:, :]
        corner_ref[:, 4 * part : 4 * part + 4, :] = ref[:, :SHIFT, :]
        down_ref[:, 4 * part : 4 * part + 4, :] = top[:, :SHIFT, :]


def pack_kernel(
    items, part_steps, x_ref, ct_ref, ct_top_ref, stats_ref, right_ref, down_ref, corner_ref, sums_ref
):
    step = pl.program_id(0)
    step_items, rows, flat = x_ref.shape
    cols = flat // WIDTH
    half = flat // 2

    @pl.when(step >= pl.num_programs(0) - part_steps)
    def _():
        fields = (x_ref.at[:, :, :half], ct_ref)
        pack_halo(fields, (x_ref.at[:, :, half:], ct_top_ref), right_ref, down_ref, corner_ref)

    def fold(v):
        total = v[:, :WIDTH]
        for j in range(1, cols):
            total = total + v[:, j * WIDTH : (j + 1) * WIDTH]
        return jnp.sum(total, 0, keepdims=True)

    def total(fn):
        acc = jnp.zeros((8, flat), f32)
        for i in range(step_items):
            acc = acc + fn(x_ref[i, 0:8, :]) + fn(x_ref[i, 8:16, :])
        return acc

    @pl.when(step == 0)
    def _():
        pivot = fold(total(lambda v: v)) * (1.0 / (step_items * rows * cols))
        sums_ref[0] = jnp.broadcast_to(jnp.concatenate([pivot] * cols, 1), (8, flat))
        sums_ref[1] = jnp.zeros((8, flat), f32)
        sums_ref[2] = jnp.zeros((8, flat), f32)

    pivot = sums_ref[0]
    sums_ref[1] += total(lambda v: v - pivot)
    sums_ref[2] += total(lambda v: (v - pivot) * (v - pivot))

    @pl.when(step == pl.num_programs(0) - 1)
    def _():
        count = items * rows * cols
        offset = fold(sums_ref[1]) * (1.0 / count)
        square = fold(sums_ref[2]) - count * offset * offset
        pad = jnp.zeros((1, LANES - WIDTH), f32)
        row = jnp.concatenate([sums_ref[0, 0:1, :WIDTH] + offset, pad, square, pad], 1)
        stats_ref[...] = jnp.broadcast_to(row[None], stats_ref.shape)


def pack(x, ct, devices):
    items, rows, flat = x.shape
    half = flat // 2
    part_items = items // PARTS
    step_items = block_of(part_items, 16)
    part_steps = part_items // step_items
    steps = items // step_items

    def of_part(count, lanes):
        return pl.BlockSpec(
            (step_items, count, half),
            lambda i: (jnp.minimum(steps - 1 - i, part_steps - 1), 0, lanes),
        )

    stats = jax.ShapeDtypeStruct((devices, 1, 2 * LANES), f32)
    counts = (24, 8, 8)
    stats, *sent = pl.pallas_call(
        partial(pack_kernel, items, part_steps),
        grid=(steps,),
        in_specs=[
            pl.BlockSpec((step_items, rows, flat), lambda i: (steps - 1 - i, 0, 0)),
            of_part(rows, 0),
            of_part(8, 1),
        ],
        out_specs=[whole(stats)] + [of_part(c, 0) for c in counts],
        out_shape=[stats] + [jax.ShapeDtypeStruct((part_items, c, half), f32) for c in counts],
        scratch_shapes=[pltpu.VMEM((3, 8, flat), f32)],
        cost_estimate=about(4),
        compiler_params=in_order,
    )(x, ct, ct)
    return stats, sent


def offset_constants():
    coords = np.zeros((8, OFFSETS), np.float32)
    o = np.arange(SPAN * SPAN)
    for k, along in enumerate((o // SPAN - (WINDOW - 1), o % SPAN - (WINDOW - 1))):
        u = along.astype(np.float32) * np.float32(8.0 / (WINDOW - 1))
        coords[k, : SPAN * SPAN] = np.sign(u) * np.log2(np.abs(u) + np.float32(1.0)) / np.float32(3.0)
    coords[2, : SPAN * SPAN] = 1.0
    key_row, lane = np.divmod(np.arange(WINDOW * LANES), LANES)
    across, row = np.divmod(lane, WINDOW)
    target = (row - key_row + WINDOW - 1) * SPAN + across
    target = np.where(across < SPAN, target, -1).astype(np.int32)
    return jnp.asarray(coords), jnp.asarray(np.broadcast_to(target, (8, target.size)).copy())


def exact(a, b):
    return jnp.dot(a, b, preferred_element_type=f32, precision=lax.Precision.HIGHEST)


def net_columns(net):
    columns = jnp.concatenate([net, jnp.zeros((LANES - 8, net.shape[1]), f32)], 0).T

    def column(i):
        return jnp.broadcast_to(columns[:, i : i + 1], (net.shape[1], OFFSETS))

    return column


def bias_net(net, coords):
    column = net_columns(net)
    u = column(0) * coords[0:1] + column(1) * coords[1:2] + column(2)
    phi, bell = normal_parts(u)
    return u * phi, phi + bell


def head_rows(net):
    return jnp.concatenate([net[3:6], jnp.zeros((5, net.shape[1]), f32)], 0)


def one_hot(target):
    rows = lax.broadcasted_iota(jnp.int32, (OFFSETS, WINDOW * LANES), 0)
    return jnp.where(rows == target[0:1], 1.0, 0.0).astype(bf16)


def three_parts(v):
    hi, lo = split(v)
    rest = v - hi.astype(f32) - lo.astype(f32)
    return jnp.concatenate([hi.astype(f32), lo.astype(f32), rest], 0).astype(bf16)


def add_parts(v):
    return v[:8] + v[8:16] + v[16:]


def prepare_kernel(
    part_refs,
    log_scale_ref,
    regions_ref,
    qv_ref,
    proj_ref,
    down_ref,
    norms_ref,
    up_ref,
    mean_ref,
    var_ref,
    w1_ref,
    b1_ref,
    w2_ref,
    coords_ref,
    target_ref,
    *refs,
):
    given, (flags_ref, scale_ref, bias_ref, vec_ref, net_ref, gate_ref), sent = (
        refs[: 4 * part_refs],
        refs[4 * part_refs : 4 * part_refs + 6],
        refs[4 * part_refs + 6 :],
    )
    for n in range(part_refs):
        x_ref, ct_ref, x_top_ref, ct_top_ref = given[4 * n : 4 * n + 4]
        pack_halo((x_ref, ct_ref), (x_top_ref, ct_top_ref), *sent[3 * n : 3 * n + 3])
    for w in range(flags_ref.shape[0]):
        first, last = WINDOW * w, WINDOW * w + WINDOW - 1
        corner = regions_ref[first, 0:1, :]
        row_cut = jnp.where(corner != regions_ref[last, 0:1, :], 2, 0)
        col_cut = jnp.where(corner != regions_ref[first, WINDOW - 1 : WINDOW, :], 1, 0)
        flags_ref[w : w + 1, :] = row_cut + col_cut

    def row(ref):
        return ref[...].reshape(1, ref.shape[0])

    vec_ref[...] = jnp.zeros_like(vec_ref)
    vec_ref[0:2, :WIDTH] = qv_ref[...]
    vec_ref[2:3, :WIDTH] = row(proj_ref)
    vec_ref[3:4, :WIDTH] = row(down_ref)
    vec_ref[4:8, :WIDTH] = norms_ref[0]
    vec_ref[8:12, :WIDTH] = norms_ref[1]
    vec_ref[12:13, :HIDDEN] = row(up_ref)
    vec_ref[13:14, :WIDTH] = row(mean_ref)
    vec_ref[14:15, :WIDTH] = row(var_ref)
    units = w1_ref.shape[1]
    net = jnp.concatenate([w1_ref[...], row(b1_ref), w2_ref[...], jnp.zeros((2, units), f32)], 0)
    vec_ref[16:24, :] = net
    lanes = lax.broadcasted_iota(jnp.int32, (1, LANES), 1)
    hidden, slope = bias_net(net, coords_ref[...])
    gate = 1.0 / (1.0 + jnp.exp(-exact(head_rows(net), hidden)))
    net_ref[0] = hidden
    net_ref[1] = slope
    gate_ref[...] = 16.0 * gate * (1.0 - gate)
    spots = one_hot(target_ref[...])
    tiles = add_parts(dot(three_parts(16.0 * gate), spots))
    scale_ref[...] = jnp.zeros_like(scale_ref)
    for h in range(HEADS):
        scale = jnp.exp(jnp.full((1, LANES), log_scale_ref[h], f32))
        scale_ref[h : h + 1, :] = scale
        tile = jnp.concatenate(
            [tiles[h : h + 1, r * LANES : (r + 1) * LANES] for r in range(WINDOW)], 0
        )
        columns = []
        for j in range(WINDOW):
            turned = pltpu.roll(tile, (72 + 8 * j) % LANES, 1)
            columns.append(jnp.where(lanes < PLACES, turned, pltpu.roll(turned, PLACES, 1)))
        bias_ref[h] = jnp.concatenate(columns, 0) - (scale + 16.0)


def prepare(x, ct, log_scale, regions, vectors, coords, target):
    units = vectors[-1].shape[1]
    items, rows, flat = x.shape
    half = flat // 2
    part_items = items // PARTS
    shapes = [
        (8, LANES),
        (HEADS, PLACES, LANES),
        (24, units),
        (2, units, OFFSETS),
        (8, OFFSETS),
    ]
    shapes = [jax.ShapeDtypeStruct(a, f32) for a in shapes]
    flags = jax.ShapeDtypeStruct((regions.shape[0] // WINDOW, regions.shape[2]), jnp.int32)
    shapes = [flags, *shapes]
    shapes += [
        jax.ShapeDtypeStruct((part_items, c, half), f32)
        for _ in range(1, PARTS)
        for c in (24, 8, 8)
    ]
    inputs = (regions, *vectors, coords, target)
    parts = []
    for n in range(1, PARTS):
        parts += [pl.BlockSpec((part_items, rows, half), lambda i, n=n: (n, 0, 0))] * 2
        parts += [pl.BlockSpec((part_items, 8, half), lambda i, n=n: (n, 0, 1))] * 2
    *made, = pl.pallas_call(
        partial(prepare_kernel, PARTS - 1),
        grid=(1,),
        in_specs=[pl.BlockSpec(memory_space=pltpu.SMEM)] + [whole(a) for a in inputs] + parts,
        out_specs=[whole(a) for a in shapes],
        out_shape=shapes,
        cost_estimate=about(0),
        compiler_params=in_order,
    )(log_scale, *inputs, *([x, ct, x, ct] * (PARTS - 1)))
    return made[:6], [made[6 + 3 * n : 9 + 3 * n] for n in range(PARTS - 1)]


def packed(w):
    hi, lo = split(w)
    return jnp.concatenate([hi, lo, hi], 1)


def stack_rows(hi, lo):
    return jnp.concatenate([hi, lo], 0)


def block_kernel(
    step_items,
    first_item,
    token_count,
    is_first,
    is_last,
    flags_ref,
    lead_ref,
    x_own,
    x_right,
    x_down,
    x_corner,
    ct_own,
    stats_ref,
    w_qkv_ref,
    w_out_ref,
    w_up_ref,
    w_down_ref,
    scale_ref,
    base_ref,
    vec_ref,
    *refs,
):
    step = pl.program_id(0)
    if is_last:
        (net_ref, gate_ref, coords_ref, target_ref), refs = refs[:4], refs[4:]
    refs, scratch = refs[:-11], refs[-11:]
    qkv_f, out_f, up_f, down_f, down_b, up_b, out_b, qkv_b, cols_ref, up_cols_ref, bias_ref = scratch
    count = len(totals_shapes)
    so_far, refs = (refs[:0], refs) if is_first else (refs[:count], refs[count:])
    out_keep, dn_keep, send_right, send_down, send_corner = refs[:5]
    refs = refs[5:]
    if is_last:
        grads_ref, norm_ref, affine_ref, flat_ref = refs[:4]
        refs = refs[4:]
    else:
        affine_ref, refs = refs[-1], refs[:-1]
    g_qkv_ref, g_out_ref, g_up_ref, g_down_ref, sums_ref, dpos_ref, dcos_ref = refs

    @pl.when(step == 0)
    def _():
        every = stats_ref[...]
        devices = every.shape[0]
        means, squares = every[:, 0, :LANES], every[:, 0, LANES:]
        mean = jnp.sum(means, 0, keepdims=True) * (1.0 / devices)
        apart = means - mean
        var = (
            jnp.sum(squares, 0, keepdims=True) * (1.0 / token_count)
            + jnp.sum(apart * apart, 0, keepdims=True) * (1.0 / devices)
        )
        inv_std = lax.rsqrt(var + norm_eps)
        affine_ref[0] = jnp.broadcast_to(mean, (LANES, LANES)).T[:WIDTH]
        affine_ref[1] = jnp.broadcast_to(inv_std, (LANES, LANES)).T[:WIDTH]
        if is_last:
            pad = jnp.zeros((2, LANES - WIDTH), f32)
            running = jnp.concatenate([vec_ref[13:15, :WIDTH], pad], 1)
            norm_ref[0:1] = mean
            norm_ref[1:2] = inv_std
            norm_ref[2:3] = (1.0 - momentum) * running[0:1] + momentum * mean
            norm_ref[3:4] = (1.0 - momentum) * running[1:2] + momentum * var * (
                token_count / (token_count - 1.0)
            )
            norm_ref[4:8] = jnp.zeros((4, LANES), f32)
        for n, ref in enumerate(refs):
            ref[...] = jnp.zeros_like(ref) if is_first else so_far[n][...]
        qkv_f[...] = packed(w_qkv_ref[...].T)
        qkv_b[...] = packed(w_qkv_ref[...])
        out_f[...] = packed(w_out_ref[...].T)
        out_b[...] = packed(w_out_ref[...])
        up_f[...] = packed(w_up_ref[...].T)
        up_b[...] = packed(w_up_ref[...])
        down_b[...] = packed(w_down_ref[...].T)
        down_f[...] = packed(w_down_ref[...])
        for i in range(cols_ref.shape[0]):
            cols_ref[i] = jnp.broadcast_to(vec_ref[i : i + 1, :WIDTH], (LANES, WIDTH)).T
        up_cols_ref[...] = jnp.broadcast_to(vec_ref[12:13, :HIDDEN], (LANES, HIDDEN)).T
        place = lax.broadcasted_iota(jnp.int32, (PLACES, LANES), 0)
        other = lax.broadcasted_iota(jnp.int32, (PLACES, LANES), 1) % PLACES
        apart_r = (place % WINDOW < SHIFT) != (other % WINDOW < SHIFT)
        apart_c = (place // WINDOW < SHIFT) != (other // WINDOW < SHIFT)
        for h in range(HEADS):
            bias = base_ref[h]
            bias_ref[0, h] = bias
            bias_ref[1, h] = jnp.where(apart_c, masked_score, bias)
            bias_ref[2, h] = jnp.where(apart_r, masked_score, bias)
            bias_ref[3, h] = jnp.where(apart_r | apart_c, masked_score, bias)

    first_half = lax.broadcasted_iota(jnp.int32, (1, PAIR), 1) < PLACES

    def product(weight, x_hi, x_lo):
        return dot(weight[...], jnp.concatenate([x_hi, x_hi, x_lo], 0))

    def halves(v):
        m = v.shape[0] // 2
        return jnp.where(first_half, v[:m], v[m:])

    def col(i):
        return cols_ref[i]

    def per_item(fn):
        return jnp.concatenate([fn(m) for m in range(step_items)], 1)

    def spread_cols(i):
        c = col(i)
        return jnp.concatenate([c] * step_items, 1)

    def gather(own, part, m):
        right, down = 12 * part, 4 * part
        top_l = own[m, SHIFT : SHIFT + WINDOW, :]
        top_r = x_right[m, right : right + WINDOW, :]
        low_l = jnp.concatenate([own[m, SHIFT + WINDOW :, :], x_down[m, down : down + SHIFT, :]], 0)
        low_r = jnp.concatenate(
            [x_right[m, right + WINDOW : right + 12, :], x_corner[m, down : down + SHIFT, :]], 0
        )
        tiles = [
            side[:, j * WIDTH : (j + 1) * WIDTH]
            for side in (top_l, top_r, low_l, low_r)
            for j in range(4)
        ]
        return jnp.concatenate(tiles, 0).T

    def scatter(value, keep, part, m):
        rows = value.T
        sides = [
            jnp.concatenate([rows[(4 * s + j) * 8 : (4 * s + j + 1) * 8] for j in range(4)], 1)
            for s in range(4)
        ]
        right, down = 12 * part, 4 * part
        keep[m, 0:WINDOW, :] = sides[0]
        keep[m, WINDOW:, :] = sides[2][:SHIFT]
        send_right[m, right : right + WINDOW, :] = sides[1]
        send_right[m, right + WINDOW : right + 12, :] = sides[3][:SHIFT]
        send_down[m, down : down + SHIFT, :] = sides[2][SHIFT:]
        send_corner[m, down : down + SHIFT, :] = sides[3][SHIFT:]

    def mean_rows(v):
        return jnp.sum(v, 0, keepdims=True) * (1.0 / WIDTH)

    def layer_norm(v):
        centred = v - mean_rows(v)
        rstd = lax.rsqrt(mean_rows(centred * centred) + norm_eps)
        return centred * rstd, rstd

    items = [first_item + step * step_items + m for m in range(step_items)]
    leads = [(lead_ref[i] + 1).astype(f32) * (1.0 / LEAD_STEPS) for i in items]
    raw = per_item(lambda m: gather(x_own, 0, m))
    mean = jnp.concatenate([affine_ref[0]] * step_items, 1)
    inv_std = jnp.concatenate([affine_ref[1]] * step_items, 1)
    normed = (raw - mean) * inv_std
    n_hi, n_lo = split(normed)

    joined = product(qkv_f, n_hi, n_lo)
    query = joined[:WIDTH] + spread_cols(0)
    key = joined[WIDTH : 2 * WIDTH]
    value = joined[2 * WIDTH :] + spread_cols(1)

    def unit(v):
        rows, inverses = [], []
        for h in range(HEADS):
            part = v[h * HEAD_DIM : (h + 1) * HEAD_DIM]
            inverse = lax.rsqrt(jnp.sum(part * part, 0, keepdims=True) + unit_eps)
            rows.append(part * inverse)
            inverses.append(inverse)
        return rows, inverses

    q_rows, q_inv = unit(query)
    k_rows, k_inv = unit(key)
    v_rows = [value[h * HEAD_DIM : (h + 1) * HEAD_DIM] for h in range(HEADS)]

    def of_item(v, m):
        return v[:, m * PAIR : (m + 1) * PAIR]

    def three(a_hi, a_lo, b_hi, b_lo):
        left = jnp.concatenate([a_hi, a_lo, a_hi], 0)
        right = jnp.concatenate([b_hi, b_hi, b_lo], 0)
        return halves(dot(left.T, right))

    def apart(x):
        zero = jnp.zeros_like(x)
        return jnp.concatenate(
            [jnp.where(first_half, x, zero), jnp.where(first_half, zero, x)], 0
        )

    def two_rows(v_hi, v_lo):
        return jnp.concatenate(
            [
                jnp.concatenate([v_hi, v_hi], 1),
                jnp.concatenate([v_lo, jnp.zeros_like(v_lo)], 1),
            ],
            0,
        )

    def over_keys(v_hi, v_lo, e_hi, e_lo):
        r = dot(two_rows(v_hi, v_lo), stack_rows(apart(e_hi), apart(e_lo)))
        return r[:HEAD_DIM] + r[HEAD_DIM:]

    def over_queries(v_hi, v_lo, e_hi, e_lo):
        weights = jnp.concatenate([e_hi, e_lo], 1)
        r = dot_rows(two_rows(apart(v_hi), apart(v_lo)), stack_rows(weights, weights))
        return halves(r[:PLACES] + r[PLACES:])

    pairs = [(m, h) for m in range(step_items) for h in range(HEADS)]
    q_parts = [split(of_item(q_rows[h], m)) for m, h in pairs]
    k_parts = [split(of_item(k_rows[h], m)) for m, h in pairs]
    v_parts = [split(of_item(v_rows[h], m)) for m, h in pairs]
    cosines = [three(*k, *q) for k, q in zip(k_parts, q_parts)]
    expos, inverses = [], []
    for (m, h), cosine in zip(pairs, cosines):
        flag0, flag1 = flags_ref[0, items[m]], flags_ref[1, items[m]]
        offset = jnp.where(first_half, bias_ref[flag0, h], bias_ref[flag1, h])
        expo = jnp.exp(cosine * scale_ref[h : h + 1, :] + offset)
        expos.append(expo)
        inverses.append(1.0 / jnp.sum(expo, 0, keepdims=True))
    e_parts = [split(e) for e in expos]
    mixes = [
        over_keys(*v, *e) * inverse for v, e, inverse in zip(v_parts, e_parts, inverses)
    ]
    mixed = jnp.concatenate(
        [jnp.concatenate(mixes[HEADS * m : HEADS * (m + 1)], 0) for m in range(step_items)], 1
    )

    o_hi, o_lo = split(mixed)
    attn_hat, attn_rstd = layer_norm(product(out_f, o_hi, o_lo) + spread_cols(2))

    def gain(base):
        return per_item(lambda m: 1.0 + col(base) + leads[m] * col(base + 1))

    def shift(base):
        return per_item(lambda m: col(base + 2) + leads[m] * col(base + 3))

    gain0 = gain(4)
    first = normed + attn_hat * gain0 + shift(4)
    f_hi, f_lo = split(first)

    up_bias = jnp.concatenate([up_cols_ref[...]] * step_items, 1)
    u = product(up_f, f_hi, f_lo) + up_bias
    phi, bell = normal_parts(u)
    hidden = u * phi
    slope = phi + bell
    h_hi, h_lo = split(hidden)
    branch = product(down_f, h_hi, h_lo) + spread_cols(3)
    hat, rstd = layer_norm(branch)
    gain1 = gain(8)
    out = first + hat * gain1 + shift(8)
    for m in range(step_items):
        scatter(of_item(out, m), out_keep, 0, m)

    def norm_back(g, hat, rstd, gain, base):
        weighted = g * hat
        for m in range(step_items):
            a, b = of_item(weighted, m), of_item(g, m)
            sums_ref[base] += a
            sums_ref[base + 1] += leads[m] * a
            sums_ref[base + 2] += b
            sums_ref[base + 3] += leads[m] * b
        e = g * gain
        return (e - mean_rows(e) - hat * mean_rows(e * hat)) * rstd

    def add_items(v):
        total = of_item(v, 0)
        for m in range(1, step_items):
            total = total + of_item(v, m)
        return total

    ones_rows = jnp.where(
        lax.broadcasted_iota(jnp.int32, (LANES - WIDTH, step_items * PAIR), 0) == 0, 1.0, 0.0
    ).astype(bf16)
    zero_rows = jnp.zeros((LANES - WIDTH, step_items * PAIR), bf16)

    def outer(a_hi, a_lo, b_hi, b_lo):
        right = jnp.concatenate([b_hi, ones_rows, b_lo, zero_rows], 0)
        r = dot_rows(stack_rows(a_hi, a_lo), right)
        m = a_hi.shape[0]
        return (r[:m, :LANES] + r[m:, :LANES]) + r[:m, LANES:]

    cot = per_item(lambda m: gather(ct_own, 1, m))
    d_branch = norm_back(cot, hat, rstd, gain1, 4)
    sums_ref[8] += add_items(d_branch)
    z_hi, z_lo = split(d_branch)
    g_down_ref[...] += outer(h_hi, h_lo, z_hi, z_lo)
    d_pre = product(down_b, z_hi, z_lo) * slope
    p_hi, p_lo = split(d_pre)
    g_up_ref[...] += outer(p_hi, p_lo, f_hi, f_lo)
    d_first = cot + product(up_b, p_hi, p_lo)
    d_attn = norm_back(d_first, attn_hat, attn_rstd, gain0, 0)
    a_hi, a_lo = split(d_attn)
    g_out_ref[...] += outer(a_hi, a_lo, o_hi, o_lo)
    d_mixed = product(out_b, a_hi, a_lo)

    d_outs = [
        of_item(d_mixed, m)[h * HEAD_DIM : (h + 1) * HEAD_DIM] * inverse
        for (m, h), inverse in zip(pairs, inverses)
    ]
    d_parts = [split(d) for d in d_outs]
    d_probs = [three(*v, *d) for v, d in zip(v_parts, d_parts)]
    s_parts = []
    for n, (m, h) in enumerate(pairs):
        delta = jnp.sum(d_outs[n] * mixes[n], 0, keepdims=True)
        d_scores = expos[n] * (d_probs[n] - delta)
        dpos_ref[h] += d_scores
        folded = d_scores * cosines[n]
        total = folded[0:8]
        for i in range(1, PLACES // 8):
            total = total + folded[8 * i : 8 * i + 8]
        dcos_ref[h] += total
        s_parts.append(split(d_scores))
    dv_rows = [over_queries(*d, *e) for d, e in zip(d_parts, e_parts)]
    dk_rows = [over_queries(*q, *d) for q, d in zip(q_parts, s_parts)]
    dq_rows = [over_keys(*k, *d) for k, d in zip(k_parts, s_parts)]

    def unit_back(grads, rows, inverse):
        out = []
        for n, (m, h) in enumerate(pairs):
            d = grads[n] * scale_ref[h : h + 1, :]
            row = of_item(rows[h], m)
            d = d - row * jnp.sum(row * d, 0, keepdims=True)
            out.append(d * of_item(inverse[h], m))
        return out

    dq_rows = unit_back(dq_rows, q_rows, q_inv)
    dk_rows = unit_back(dk_rows, k_rows, k_inv)
    d_joined = jnp.concatenate(
        [
            jnp.concatenate(
                [d for rows in (dq_rows, dk_rows, dv_rows) for d in rows[HEADS * m : HEADS * (m + 1)]], 0
            )
            for m in range(step_items)
        ],
        1,
    )
    j_hi, j_lo = split(d_joined)
    g_qkv_ref[...] += outer(j_hi, j_lo, n_hi, n_lo)
    d_normed = d_first + product(qkv_b, j_hi, j_lo)
    sums_ref[9] += add_items(d_normed)
    sums_ref[10] += add_items(d_normed * normed)
    for m in range(step_items):
        scatter(of_item(d_normed, m), dn_keep, 1, m)

    def finish():
        def lane_sums(v):
            return jnp.sum(v.T, 0, keepdims=True)

        flat_ref[...] = jnp.zeros_like(flat_ref)
        g = g_qkv_ref[...].T
        flat_ref[0:96, :] = g[:WIDTH, :LANES]
        flat_ref[96:192, :] = g[:WIDTH, LANES : 2 * LANES]
        qv = g[WIDTH : WIDTH + 1]
        g_out = g_out_ref[...].T
        flat_ref[192:288, :] = jnp.concatenate([g_out[:WIDTH], g[:WIDTH, 2 * LANES :]], 1)
        g_up = g_up_ref[...].T
        g_down = g_down_ref[...].T
        for k in range(3):
            lanes = slice(k * LANES, (k + 1) * LANES)
            flat_ref[288 + 96 * k : 384 + 96 * k, :] = g_up[:WIDTH, lanes]
            flat_ref[576 + 96 * k : 672 + 96 * k, :] = g_down[:WIDTH, lanes]
            flat_ref[876 + k : 877 + k, :] = g_up[WIDTH : WIDTH + 1, lanes]
        totals = [lane_sums(sums_ref[i]) for i in range(11)]
        for i in range(8):
            flat_ref[864 + i : 865 + i, :WIDTH] = totals[i]
        flat_ref[872:873, :WIDTH] = totals[8]
        flat_ref[873:874, :WIDTH] = g_out[WIDTH : WIDTH + 1]
        flat_ref[874:875, :WIDTH] = qv[:, :WIDTH]
        flat_ref[875:876, :WIDTH] = qv[:, 2 * WIDTH :]
        lane = lax.broadcasted_iota(jnp.int32, (1, LANES), 1)
        scales = jnp.zeros((1, LANES), f32)
        for h in range(HEADS):
            total = jnp.sum(jnp.sum(dcos_ref[h], 0, keepdims=True), 1, keepdims=True)
            scales = jnp.where(lane == WIDTH + h, total * scale_ref[h : h + 1, :], scales)
        flat_ref[864:865, :] = flat_ref[864:865, :] + scales

        rows = []
        for h in range(HEADS):
            d = dpos_ref[h]
            d = jnp.where(first_half, d + pltpu.roll(d, PLACES, 1), 0.0)
            tile = jnp.zeros((WINDOW, LANES), f32)
            for j in range(WINDOW):
                tile = tile + pltpu.roll(d[8 * j : 8 * j + 8], 56 - 8 * j, 1)
            rows.append(jnp.concatenate([tile[r : r + 1] for r in range(WINDOW)], 1))
        rows.append(jnp.zeros((8 - HEADS, WINDOW * LANES), f32))
        found = dot_rows(three_parts(jnp.concatenate(rows, 0)), one_hot(target_ref[...]))
        d_table = add_parts(found)
        d_logit = d_table * gate_ref[...]

        def against(v, units):
            v_hi, v_lo = split(v)
            u_hi, u_lo = split(units)
            both = jnp.concatenate([v_hi.astype(f32), v_lo.astype(f32)], 0).astype(bf16)
            r = dot_rows(both, u_hi)
            return r[:8] + r[8:] + dot_rows(v_hi, u_lo)

        g_w2 = against(d_logit, net_ref[0])
        column = net_columns(vec_ref[16:24, :])
        d_hidden = sum(column(3 + h) * d_logit[h : h + 1] for h in range(HEADS))
        g_first = against(coords_ref[...], d_hidden * net_ref[1])
        for i, row in enumerate(
            [g_first[0:1], g_first[1:2], g_first[2:3], g_w2[0:1], g_w2[1:2], g_w2[2:3]]
        ):
            for k in range(4):
                at = 879 + 4 * i + k
                flat_ref[at : at + 1, :] = row[:, k * LANES : (k + 1) * LANES]

        slots, slot_rows, _ = grads_ref.shape
        share = slot_rows - 2
        for j in range(slots):
            grads_ref[j, 0:share, :] = flat_ref[share * j : share * (j + 1), :]
        for i in range(2):
            grads_ref[:, share + i : share + i + 1, :WIDTH] = jnp.broadcast_to(
                totals[9 + i][None], (slots, 1, WIDTH)
            )
            grads_ref[:, share + i : share + i + 1, WIDTH:] = jnp.zeros(
                (slots, 1, LANES - WIDTH), f32
            )

    if is_last:
        finish()


totals_shapes = [
    (3 * WIDTH, LANES),
    (WIDTH, LANES),
    (HIDDEN, LANES),
    (HIDDEN, LANES),
    (11, WIDTH, LANES),
    (HEADS, PLACES, LANES),
    (HEADS, 8, LANES),
]


def run_block(
    part,
    flags,
    lead,
    x,
    ct,
    halo,
    stats,
    weights,
    prepared,
    bias_net_parts,
    so_far,
    token_count,
):
    items, tile_rows, flat = x.shape
    half = flat // 2
    items = items // PARTS
    step_items = block_of(items, 16)
    steps = items // step_items
    is_first, is_last = part == 0, part == PARTS - 1

    def rows(n):
        return pl.BlockSpec((step_items, n, half), lambda i: (i, 0, 0))

    smem = pl.BlockSpec(memory_space=pltpu.SMEM)
    field = pl.BlockSpec((step_items, tile_rows, half), lambda i: (part * steps + i, 0, 1))
    out_rows = (12, 12, 24, 8, 8)
    slots = stats.shape[0]
    slot_rows = -(-PAYLOAD // slots)
    slot_rows = -(-(slot_rows + 2) // 8) * 8
    totals = [jax.ShapeDtypeStruct(s, f32) for s in totals_shapes]
    scratch = [pltpu.VMEM((2, WIDTH, LANES), f32)]
    if is_last:
        tail = [
            jax.ShapeDtypeStruct((slots, slot_rows, LANES), f32),
            jax.ShapeDtypeStruct((8, LANES), f32),
        ]
        scratch.append(pltpu.VMEM((slots * (slot_rows - 2), LANES), f32))
        scratch += [pltpu.VMEM(s, f32) for s in totals_shapes]
    else:
        tail = totals
    scratch += [
        pltpu.VMEM((3 * WIDTH, 3 * WIDTH), bf16),
        pltpu.VMEM((WIDTH, 3 * WIDTH), bf16),
        pltpu.VMEM((HIDDEN, 3 * WIDTH), bf16),
        pltpu.VMEM((WIDTH, 3 * HIDDEN), bf16),
        pltpu.VMEM((HIDDEN, 3 * WIDTH), bf16),
        pltpu.VMEM((WIDTH, 3 * HIDDEN), bf16),
        pltpu.VMEM((WIDTH, 3 * WIDTH), bf16),
        pltpu.VMEM((WIDTH, 9 * WIDTH), bf16),
        pltpu.VMEM((12, WIDTH, LANES), f32),
        pltpu.VMEM((HIDDEN, LANES), f32),
        pltpu.VMEM((4, HEADS, PLACES, LANES), f32),
    ]
    constants = (stats, *weights, *prepared, *(bias_net_parts if is_last else ()), *so_far)
    return pl.pallas_call(
        partial(block_kernel, step_items, part * items, float(token_count), is_first, is_last),
        grid=(steps,),
        in_specs=[smem, smem, field, rows(24), rows(8), rows(8), field]
        + [whole(a) for a in constants],
        out_specs=[rows(n) for n in out_rows] + [whole(a) for a in tail],
        out_shape=[jax.ShapeDtypeStruct((items, n, half), f32) for n in out_rows] + tail,
        scratch_shapes=scratch,
        cost_estimate=about(40),
        compiler_params=pltpu.CompilerParams(
            dimension_semantics=("arbitrary",), vmem_limit_bytes=65024 * 1024
        ),
    )(flags, lead, x, *halo, ct, *constants)


def place(ref_out, m, keep, right, down, corner, part, fn):
    half = keep.shape[2]
    at, low = 12 * part, 4 * part
    for rows, left, own in (
        (slice(0, SHIFT), corner[m, low : low + SHIFT, :], down[m, low : low + SHIFT, :]),
        (slice(SHIFT, 16), right[m, at : at + 12, :], keep[m]),
    ):
        for lanes, value in ((slice(0, half), left), (slice(half, 2 * half), own)):
            ref_out[m, rows, lanes] = fn(value, rows, lanes)


def final_kernel(token_count, part_steps, x_ref, norm_ref, sums_ref, *refs):
    cols = x_ref.shape[2] // WIDTH
    out_ref, grad_ref = refs[-2:]

    def wide(row):
        return jnp.concatenate([row[:, :WIDTH]] * cols, 1)

    mean, inv_std = norm_ref[0:1], norm_ref[1:2]
    at = sums_ref.shape[1] - 2
    mean_grad = sums_ref[0, at : at + 1] * (1.0 / token_count)
    mean_cross = sums_ref[0, at + 1 : at + 2] * (1.0 / token_count)
    factor, centre = wide(inv_std), wide(mean)
    offset, slope = wide(inv_std * mean_grad), wide(inv_std * inv_std * mean_cross)

    def work(out_keep, dn_keep, *halo):
        for m in range(x_ref.shape[0]):

            def grad(v, rows, lanes):
                x = x_ref[m, rows, lanes] - centre[:, lanes]
                return factor[:, lanes] * v - offset[:, lanes] - x * slope[:, lanes]

            place(out_ref, m, out_keep, *halo, 0, lambda v, rows, lanes: v)
            place(grad_ref, m, dn_keep, *halo, 1, grad)

    for n in range(PARTS):
        pl.when(pl.program_id(0) // part_steps == n)(partial(work, *refs[5 * n : 5 * n + 5]))


def finish_fields(x, parts, norm, sums, token_count):
    items, rows, flat = x.shape
    step_items = block_of(items // PARTS, 16)
    part_steps = items // PARTS // step_items

    def spec(part, n):
        return pl.BlockSpec(
            (step_items, n, flat // 2),
            lambda i: (jnp.clip(i - part * part_steps, 0, part_steps - 1), 0, 0),
        )

    field = pl.BlockSpec((step_items, rows, flat), lambda i: (i, 0, 0))
    return pl.pallas_call(
        partial(final_kernel, float(token_count), part_steps),
        grid=(items // step_items,),
        in_specs=[
            field,
            whole(norm),
            pl.BlockSpec((1,) + sums.shape[1:], lambda i: (0, 0, 0)),
        ]
        + [spec(part, n) for part in range(PARTS) for n in (12, 12, 24, 8, 8)],
        out_specs=[field] * 2,
        out_shape=[jax.ShapeDtypeStruct(x.shape, f32)] * 2,
        cost_estimate=about(60),
        compiler_params=in_order,
    )(x, norm, sums, *[a for part in parts for a in part])


def sum_slots_kernel(slots_ref, all_ref):
    total = slots_ref[0]
    for j in range(1, slots_ref.shape[0]):
        total = total + slots_ref[j]
    all_ref[...] = jnp.broadcast_to(total[None], all_ref.shape)


def sum_slots(slots):
    return pl.pallas_call(
        sum_slots_kernel,
        grid=(1,),
        in_specs=[whole(slots)],
        out_specs=whole(slots),
        out_shape=jax.ShapeDtypeStruct(slots.shape, f32),
        compiler_params=pltpu.CompilerParams(vmem_limit_bytes=16 * 1024 * 1024),
    )(slots)


def unpack_kernel(
    all_ref,
    qkv_ref,
    qv_ref,
    scale_ref,
    w1_ref,
    b1_ref,
    w2_ref,
    out_ref,
    b_out_ref,
    up_ref,
    b_up_ref,
    down_ref,
    b_down_ref,
    norm_ref,
    flat_ref,
):
    slots, slot_rows, _ = all_ref.shape
    share = slot_rows - 2
    for j in range(slots):
        flat_ref[share * j : share * (j + 1), :] = all_ref[j, 0:share, :]
    qkv_ref[:, 0:LANES] = flat_ref[0:96, :]
    qkv_ref[:, LANES : 2 * LANES] = flat_ref[96:192, :]
    qkv_ref[:, 2 * LANES :] = flat_ref[192:288, WIDTH:]
    out_ref[...] = flat_ref[192:288, :WIDTH]
    for k in range(3):
        lanes = slice(k * LANES, (k + 1) * LANES)
        up_ref[:, lanes] = flat_ref[288 + 96 * k : 384 + 96 * k, :]
        down_ref[:, lanes] = flat_ref[576 + 96 * k : 672 + 96 * k, :]
        b_up_ref[k : k + 1, :] = flat_ref[876 + k : 877 + k, :]
    norm_ref[...] = flat_ref[864:872, :WIDTH]
    scale_ref[...] = flat_ref[864:865, WIDTH : WIDTH + HEADS]
    b_down_ref[...] = flat_ref[872:873, :WIDTH]
    b_out_ref[...] = flat_ref[873:874, :WIDTH]
    qv_ref[...] = flat_ref[874:876, :WIDTH]
    for k in range(4):
        lanes = slice(k * LANES, (k + 1) * LANES)
        for i in range(2):
            w1_ref[i : i + 1, lanes] = flat_ref[879 + 4 * i + k : 880 + 4 * i + k, :]
        b1_ref[:, lanes] = flat_ref[887 + k : 888 + k, :]
        for i in range(3):
            w2_ref[i : i + 1, lanes] = flat_ref[891 + 4 * i + k : 892 + 4 * i + k, :]


def unpack(everything):
    slots, slot_rows, _ = everything.shape
    shapes = [
        (WIDTH, 3 * WIDTH),
        (2, WIDTH),
        (1, HEADS),
        (2, 512),
        (1, 512),
        (HEADS, 512),
        (WIDTH, WIDTH),
        (1, WIDTH),
        (WIDTH, HIDDEN),
        (3, LANES),
        (WIDTH, HIDDEN),
        (1, WIDTH),
        (8, WIDTH),
    ]
    shapes = [jax.ShapeDtypeStruct(s, f32) for s in shapes]
    return pl.pallas_call(
        unpack_kernel,
        grid=(1,),
        in_specs=[whole(everything)],
        out_specs=[whole(a) for a in shapes],
        out_shape=shapes,
        compiler_params=pltpu.CompilerParams(vmem_limit_bytes=16 * 1024 * 1024),
        scratch_shapes=[pltpu.VMEM((slots * (slot_rows - 2), LANES), f32)],
    )(everything)


def take_from(block, dy, dx):
    rows, cols = lax.axis_size("ty"), lax.axis_size("tx")
    route = []
    for i in range(rows * cols):
        y, x = divmod(i, cols)
        route.append((((y + dy) % rows) * cols + (x + dx) % cols, i))
    return lax.ppermute(block, ("ty", "tx"), route)


def exchange(slots):
    return lax.all_to_all(slots, axes_all, 0, 0, tiled=True)


def shards(
    inputs,
    regions,
    lead_step_index,
    running_channel_mean,
    running_channel_variance,
    query_key_value_weight,
    query_value_bias,
    log_cosine_scale,
    bias_net_weight1,
    bias_net_bias1,
    bias_net_weight2,
    output_weight,
    projection_bias,
    up_weight,
    up_bias,
    down_weight,
    down_bias,
    conditioned_norm_values,
    cotangent,
):
    items, tile_rows, flat = inputs.shape
    devices = lax.axis_size(axes_all)
    token_count = items * tile_rows * (flat // WIDTH) * devices

    stats, sent = pack(inputs, cotangent, devices)
    stats = exchange(stats)

    vectors = (
        query_value_bias,
        projection_bias,
        down_bias,
        conditioned_norm_values,
        up_bias,
        running_channel_mean,
        running_channel_variance,
        bias_net_weight1,
        bias_net_bias1,
        bias_net_weight2.T,
    )
    coords, target = offset_constants()
    weights = (query_key_value_weight, output_weight, up_weight, down_weight)
    corners = regions.transpose(1, 2, 0)
    (flags, *prepared, net, gate), sent_later = prepare(
        inputs, cotangent, log_cosine_scale, corners, vectors, coords, target
    )
    halos = []
    for right, down, corner in (sent, *sent_later):
        if halos:
            (right, down, corner), halos[-1] = lax.optimization_barrier(
                ((right, down, corner), halos[-1])
            )
        halos.append((take_from(right, 0, 1), take_from(down, 1, 0), take_from(corner, 1, 1)))
    bias_net_parts = (net, gate, coords, target)
    totals, out_parts, dn_parts, home = [], [], [], []
    for part in range(PARTS):
        out_keep, dn_keep, right, down, corner, *totals = run_block(
            part,
            flags,
            lead_step_index,
            inputs,
            cotangent,
            halos[part],
            stats,
            weights,
            prepared,
            bias_net_parts,
            totals,
            token_count,
        )
        home.append((take_from(right, 0, -1), take_from(down, -1, 0), take_from(corner, -1, -1)))
        out_parts.append(out_keep)
        dn_parts.append(dn_keep)
    grads, norm = totals
    shares = sum_slots(exchange(grads))
    outputs, grad_inputs = finish_fields(
        inputs,
        [(o, d, *h) for o, d, h in zip(out_parts, dn_parts, home)],
        norm,
        shares,
        token_count,
    )
    everything = exchange(shares)
    (
        g_qkv,
        g_qv,
        g_scale,
        g_w1,
        g_b1,
        g_w2,
        g_out,
        g_b_out,
        g_up,
        g_b_up,
        g_down,
        g_b_down,
        g_norm,
    ) = unpack(everything)
    return (
        outputs,
        grad_inputs,
        g_qkv,
        g_qv,
        g_scale.reshape(-1),
        g_w1,
        g_b1.reshape(-1),
        g_w2.T,
        g_out,
        g_b_out.reshape(-1),
        g_up,
        g_b_up.reshape(-1),
        g_down,
        g_b_down.reshape(-1),
        g_norm.reshape(2, 4, WIDTH),
        norm[2, :WIDTH],
        norm[3, :WIDTH],
    )


def solution(mesh):
    tiled = P("items", "ty", "tx")
    placed = (tiled, tiled, P("items")) + (P(),) * 15 + (tiled,)
    return jax.shard_map(
        shards,
        mesh=mesh,
        in_specs=placed,
        out_specs=(tiled, tiled) + (P(),) * 15,
        check_vma=False,
    )
```

```python
from functools import partial

import jax
import jax.numpy as jnp
import numpy as np
from jax import lax
from jax.experimental import pallas as pl
from jax.experimental.pallas import tpu as pltpu
from jax.sharding import PartitionSpec as P

HEADS = 3
HEAD_DIM = 32
WIDTH = 96
HIDDEN = 384
WINDOW = 8
SHIFT = 4
LEAD_STEPS = 14
PLACES = WINDOW * WINDOW
SPAN = 2 * WINDOW - 1
PAIR = 2 * PLACES
LANES = 128
OFFSETS = 256
PAYLOAD = 903
PARTS = 2

masked_score = -1000000000.0
norm_eps = 1e-05
unit_eps = 1e-06
momentum = 0.1
axes_all = ("ty", "th", "tl", "items")
axes_far = ("ty", "th", "items")
axes_tiles = ("ty", "th", "tl")

f32 = jnp.float32
bf16 = jnp.bfloat16

in_order = pltpu.CompilerParams(
    dimension_semantics=("arbitrary",), vmem_limit_bytes=60 * 1024 * 1024
)


def about(microseconds):
    return pl.CostEstimate(flops=microseconds * 10**9, bytes_accessed=10**6, transcendentals=0)


def block_of(items, most=8):
    return max(n for n in range(1, most + 1) if items % n == 0)


def whole(a):
    return pl.BlockSpec(a.shape, lambda i: (0,) * len(a.shape))


def dot(a, b):
    return lax.dot_general(a, b, (((1,), (0,)), ((), ())), preferred_element_type=f32)


def dot_rows(a, b):
    return lax.dot_general(a, b, (((1,), (1,)), ((), ())), preferred_element_type=f32)


def split(x):
    hi = x.astype(bf16)
    return hi, (x - hi.astype(f32)).astype(bf16)


def normal_parts(u):
    phi = 0.5 + 0.5 * lax.erf(u * 0.7071067811865476)
    return phi, (u * 0.3989422804014327) * jnp.exp(-0.5 * (u * u))


def pack_halo(fields, tops, right_ref, down_ref, corner_ref):
    for part, (ref, top) in enumerate(zip(fields, tops)):
        right_ref[:, 12 * part : 12 * part + 12, :] = ref[:, SHIFT:, :]
        corner_ref[:, 4 * part : 4 * part + 4, :] = ref[:, :SHIFT, :]
        down_ref[:, 4 * part : 4 * part + 4, :] = top[:, :SHIFT, :]


def pack_kernel(
    items, part_steps, x_ref, ct_ref, ct_top_ref, stats_ref, right_ref, down_ref, corner_ref, sums_ref
):
    step = pl.program_id(0)
    step_items, rows, flat = x_ref.shape
    cols = flat // WIDTH
    half = flat // 2

    @pl.when(step >= pl.num_programs(0) - part_steps)
    def _():
        fields = (x_ref.at[:, :, :half], ct_ref)
        pack_halo(fields, (x_ref.at[:, :, half:], ct_top_ref), right_ref, down_ref, corner_ref)

    def fold(v):
        total = v[:, :WIDTH]
        for j in range(1, cols):
            total = total + v[:, j * WIDTH : (j + 1) * WIDTH]
        return jnp.sum(total, 0, keepdims=True)

    def total(fn):
        acc = jnp.zeros((8, flat), f32)
        for i in range(step_items):
            acc = acc + fn(x_ref[i, 0:8, :]) + fn(x_ref[i, 8:16, :])
        return acc

    @pl.when(step == 0)
    def _():
        pivot = fold(total(lambda v: v)) * (1.0 / (step_items * rows * cols))
        sums_ref[0] = jnp.broadcast_to(jnp.concatenate([pivot] * cols, 1), (8, flat))
        sums_ref[1] = jnp.zeros((8, flat), f32)
        sums_ref[2] = jnp.zeros((8, flat), f32)

    pivot = sums_ref[0]
    sums_ref[1] += total(lambda v: v - pivot)
    sums_ref[2] += total(lambda v: (v - pivot) * (v - pivot))

    @pl.when(step == pl.num_programs(0) - 1)
    def _():
        count = items * rows * cols
        offset = fold(sums_ref[1]) * (1.0 / count)
        square = fold(sums_ref[2]) - count * offset * offset
        pad = jnp.zeros((1, LANES - WIDTH), f32)
        row = jnp.concatenate([sums_ref[0, 0:1, :WIDTH] + offset, pad, square, pad], 1)
        stats_ref[...] = jnp.broadcast_to(row[None], stats_ref.shape)


def pack(x, ct, devices):
    items, rows, flat = x.shape
    half = flat // 2
    part_items = items // PARTS
    step_items = block_of(part_items, 16)
    part_steps = part_items // step_items
    steps = items // step_items

    def of_part(count, lanes):
        return pl.BlockSpec(
            (step_items, count, half),
            lambda i: (jnp.minimum(steps - 1 - i, part_steps - 1), 0, lanes),
        )

    stats = jax.ShapeDtypeStruct((devices, 1, 2 * LANES), f32)
    counts = (24, 8, 8)
    stats, *sent = pl.pallas_call(
        partial(pack_kernel, items, part_steps),
        grid=(steps,),
        in_specs=[
            pl.BlockSpec((step_items, rows, flat), lambda i: (steps - 1 - i, 0, 0)),
            of_part(rows, 0),
            of_part(8, 1),
        ],
        out_specs=[whole(stats)] + [of_part(c, 0) for c in counts],
        out_shape=[stats] + [jax.ShapeDtypeStruct((part_items, c, half), f32) for c in counts],
        scratch_shapes=[pltpu.VMEM((3, 8, flat), f32)],
        cost_estimate=about(4),
        compiler_params=in_order,
    )(x, ct, ct)
    return stats, sent


def offset_constants():
    coords = np.zeros((8, OFFSETS), np.float32)
    o = np.arange(SPAN * SPAN)
    for k, along in enumerate((o // SPAN - (WINDOW - 1), o % SPAN - (WINDOW - 1))):
        u = along.astype(np.float32) * np.float32(8.0 / (WINDOW - 1))
        coords[k, : SPAN * SPAN] = np.sign(u) * np.log2(np.abs(u) + np.float32(1.0)) / np.float32(3.0)
    coords[2, : SPAN * SPAN] = 1.0
    key_row, lane = np.divmod(np.arange(WINDOW * LANES), LANES)
    across, row = np.divmod(lane, WINDOW)
    target = (row - key_row + WINDOW - 1) * SPAN + across
    target = np.where(across < SPAN, target, -1).astype(np.int32)
    return jnp.asarray(coords), jnp.asarray(np.broadcast_to(target, (8, target.size)).copy())


def exact(a, b):
    return jnp.dot(a, b, preferred_element_type=f32, precision=lax.Precision.HIGHEST)


def net_columns(net):
    columns = jnp.concatenate([net, jnp.zeros((LANES - 8, net.shape[1]), f32)], 0).T

    def column(i):
        return jnp.broadcast_to(columns[:, i : i + 1], (net.shape[1], OFFSETS))

    return column


def bias_net(net, coords):
    column = net_columns(net)
    u = column(0) * coords[0:1] + column(1) * coords[1:2] + column(2)
    phi, bell = normal_parts(u)
    return u * phi, phi + bell


def head_rows(net):
    return jnp.concatenate([net[3:6], jnp.zeros((5, net.shape[1]), f32)], 0)


def one_hot(target):
    rows = lax.broadcasted_iota(jnp.int32, (OFFSETS, WINDOW * LANES), 0)
    return jnp.where(rows == target[0:1], 1.0, 0.0).astype(bf16)


def three_parts(v):
    hi, lo = split(v)
    rest = v - hi.astype(f32) - lo.astype(f32)
    return jnp.concatenate([hi.astype(f32), lo.astype(f32), rest], 0).astype(bf16)


def add_parts(v):
    return v[:8] + v[8:16] + v[16:]


def prepare_kernel(
    part_refs,
    log_scale_ref,
    regions_ref,
    qv_ref,
    proj_ref,
    down_ref,
    norms_ref,
    up_ref,
    mean_ref,
    var_ref,
    w1_ref,
    b1_ref,
    w2_ref,
    coords_ref,
    target_ref,
    *refs,
):
    given, (flags_ref, scale_ref, bias_ref, vec_ref, net_ref, gate_ref), sent = (
        refs[: 4 * part_refs],
        refs[4 * part_refs : 4 * part_refs + 6],
        refs[4 * part_refs + 6 :],
    )
    for n in range(part_refs):
        x_ref, ct_ref, x_top_ref, ct_top_ref = given[4 * n : 4 * n + 4]
        pack_halo((x_ref, ct_ref), (x_top_ref, ct_top_ref), *sent[3 * n : 3 * n + 3])
    for w in range(flags_ref.shape[0]):
        first, last = WINDOW * w, WINDOW * w + WINDOW - 1
        corner = regions_ref[first, 0:1, :]
        row_cut = jnp.where(corner != regions_ref[last, 0:1, :], 2, 0)
        col_cut = jnp.where(corner != regions_ref[first, WINDOW - 1 : WINDOW, :], 1, 0)
        flags_ref[w : w + 1, :] = row_cut + col_cut

    def row(ref):
        return ref[...].reshape(1, ref.shape[0])

    vec_ref[...] = jnp.zeros_like(vec_ref)
    vec_ref[0:2, :WIDTH] = qv_ref[...]
    vec_ref[2:3, :WIDTH] = row(proj_ref)
    vec_ref[3:4, :WIDTH] = row(down_ref)
    vec_ref[4:8, :WIDTH] = norms_ref[0]
    vec_ref[8:12, :WIDTH] = norms_ref[1]
    vec_ref[12:13, :HIDDEN] = row(up_ref)
    vec_ref[13:14, :WIDTH] = row(mean_ref)
    vec_ref[14:15, :WIDTH] = row(var_ref)
    units = w1_ref.shape[1]
    net = jnp.concatenate([w1_ref[...], row(b1_ref), w2_ref[...], jnp.zeros((2, units), f32)], 0)
    vec_ref[16:24, :] = net
    lanes = lax.broadcasted_iota(jnp.int32, (1, LANES), 1)
    hidden, slope = bias_net(net, coords_ref[...])
    gate = 1.0 / (1.0 + jnp.exp(-exact(head_rows(net), hidden)))
    net_ref[0] = hidden
    net_ref[1] = slope
    gate_ref[...] = 16.0 * gate * (1.0 - gate)
    spots = one_hot(target_ref[...])
    tiles = add_parts(dot(three_parts(16.0 * gate), spots))
    scale_ref[...] = jnp.zeros_like(scale_ref)
    for h in range(HEADS):
        scale = jnp.exp(jnp.full((1, LANES), log_scale_ref[h], f32))
        scale_ref[h : h + 1, :] = scale
        tile = jnp.concatenate(
            [tiles[h : h + 1, r * LANES : (r + 1) * LANES] for r in range(WINDOW)], 0
        )
        columns = []
        for j in range(WINDOW):
            turned = pltpu.roll(tile, (72 + 8 * j) % LANES, 1)
            columns.append(jnp.where(lanes < PLACES, turned, pltpu.roll(turned, PLACES, 1)))
        bias_ref[h] = jnp.concatenate(columns, 0) - (scale + 16.0)


def prepare(x, ct, log_scale, regions, vectors, coords, target):
    units = vectors[-1].shape[1]
    items, rows, flat = x.shape
    half = flat // 2
    part_items = items // PARTS
    shapes = [
        (8, LANES),
        (HEADS, PLACES, LANES),
        (24, units),
        (2, units, OFFSETS),
        (8, OFFSETS),
    ]
    shapes = [jax.ShapeDtypeStruct(a, f32) for a in shapes]
    flags = jax.ShapeDtypeStruct((regions.shape[0] // WINDOW, regions.shape[2]), jnp.int32)
    shapes = [flags, *shapes]
    shapes += [
        jax.ShapeDtypeStruct((part_items, c, half), f32)
        for _ in range(1, PARTS)
        for c in (24, 8, 8)
    ]
    inputs = (regions, *vectors, coords, target)
    parts = []
    for n in range(1, PARTS):
        parts += [pl.BlockSpec((part_items, rows, half), lambda i, n=n: (n, 0, 0))] * 2
        parts += [pl.BlockSpec((part_items, 8, half), lambda i, n=n: (n, 0, 1))] * 2
    *made, = pl.pallas_call(
        partial(prepare_kernel, PARTS - 1),
        grid=(1,),
        in_specs=[pl.BlockSpec(memory_space=pltpu.SMEM)] + [whole(a) for a in inputs] + parts,
        out_specs=[whole(a) for a in shapes],
        out_shape=shapes,
        cost_estimate=about(0),
        compiler_params=in_order,
    )(log_scale, *inputs, *([x, ct, x, ct] * (PARTS - 1)))
    return made[:6], [made[6 + 3 * n : 9 + 3 * n] for n in range(PARTS - 1)]


def packed(w):
    hi, lo = split(w)
    return jnp.concatenate([hi, lo, hi], 1)


def stack_rows(hi, lo):
    return jnp.concatenate([hi, lo], 0)


def block_kernel(
    step_items,
    first_item,
    token_count,
    is_first,
    is_last,
    flags_ref,
    lead_ref,
    side_ref,
    x_own,
    x_right,
    x_down,
    x_corner,
    ct_own,
    stats_ref,
    w_qkv_ref,
    w_out_ref,
    w_up_ref,
    w_down_ref,
    scale_ref,
    base_ref,
    vec_ref,
    *refs,
):
    step = pl.program_id(0)
    if is_last:
        (net_ref, gate_ref, coords_ref, target_ref), refs = refs[:4], refs[4:]
    refs, scratch = refs[:-11], refs[-11:]
    qkv_f, out_f, up_f, down_f, down_b, up_b, out_b, qkv_b, cols_ref, up_cols_ref, bias_ref = scratch
    count = len(totals_shapes)
    so_far, refs = (refs[:0], refs) if is_first else (refs[:count], refs[count:])
    out_keep, dn_keep, send_right, send_down, send_corner = refs[:5]
    refs = refs[5:]
    if is_last:
        own_ref, give_ref, norm_ref, affine_ref, flat_ref = refs[:5]
        refs = refs[5:]
    else:
        affine_ref, refs = refs[-1], refs[:-1]
    g_qkv_ref, g_out_ref, g_up_ref, g_down_ref, sums_ref, dpos_ref, dcos_ref = refs

    @pl.when(step == 0)
    def _():
        every = stats_ref[...]
        devices = every.shape[0]
        means, squares = every[:, 0, :LANES], every[:, 0, LANES:]
        mean = jnp.sum(means, 0, keepdims=True) * (1.0 / devices)
        apart = means - mean
        var = (
            jnp.sum(squares, 0, keepdims=True) * (1.0 / token_count)
            + jnp.sum(apart * apart, 0, keepdims=True) * (1.0 / devices)
        )
        inv_std = lax.rsqrt(var + norm_eps)
        affine_ref[0] = jnp.broadcast_to(mean, (LANES, LANES)).T[:WIDTH]
        affine_ref[1] = jnp.broadcast_to(inv_std, (LANES, LANES)).T[:WIDTH]
        if is_last:
            pad = jnp.zeros((2, LANES - WIDTH), f32)
            running = jnp.concatenate([vec_ref[13:15, :WIDTH], pad], 1)
            norm_ref[0:1] = mean
            norm_ref[1:2] = inv_std
            norm_ref[2:3] = (1.0 - momentum) * running[0:1] + momentum * mean
            norm_ref[3:4] = (1.0 - momentum) * running[1:2] + momentum * var * (
                token_count / (token_count - 1.0)
            )
            norm_ref[4:8] = jnp.zeros((4, LANES), f32)
        for n, ref in enumerate(refs):
            ref[...] = jnp.zeros_like(ref) if is_first else so_far[n][...]
        qkv_f[...] = packed(w_qkv_ref[...].T)
        qkv_b[...] = packed(w_qkv_ref[...])
        out_f[...] = packed(w_out_ref[...].T)
        out_b[...] = packed(w_out_ref[...])
        up_f[...] = packed(w_up_ref[...].T)
        up_b[...] = packed(w_up_ref[...])
        down_b[...] = packed(w_down_ref[...].T)
        down_f[...] = packed(w_down_ref[...])
        for i in range(cols_ref.shape[0]):
            cols_ref[i] = jnp.broadcast_to(vec_ref[i : i + 1, :WIDTH], (LANES, WIDTH)).T
        up_cols_ref[...] = jnp.broadcast_to(vec_ref[12:13, :HIDDEN], (LANES, HIDDEN)).T
        place = lax.broadcasted_iota(jnp.int32, (PLACES, LANES), 0)
        other = lax.broadcasted_iota(jnp.int32, (PLACES, LANES), 1) % PLACES
        apart_r = (place % WINDOW < SHIFT) != (other % WINDOW < SHIFT)
        apart_c = (place // WINDOW < SHIFT) != (other // WINDOW < SHIFT)
        for h in range(HEADS):
            bias = base_ref[h]
            bias_ref[0, h] = bias
            bias_ref[1, h] = jnp.where(apart_c, masked_score, bias)
            bias_ref[2, h] = jnp.where(apart_r, masked_score, bias)
            bias_ref[3, h] = jnp.where(apart_r | apart_c, masked_score, bias)

    first_half = lax.broadcasted_iota(jnp.int32, (1, PAIR), 1) < PLACES

    def product(weight, x_hi, x_lo):
        return dot(weight[...], jnp.concatenate([x_hi, x_hi, x_lo], 0))

    def halves(v):
        m = v.shape[0] // 2
        return jnp.where(first_half, v[:m], v[m:])

    def col(i):
        return cols_ref[i]

    def per_item(fn):
        return jnp.concatenate([fn(m) for m in range(step_items)], 1)

    def spread_cols(i):
        c = col(i)
        return jnp.concatenate([c] * step_items, 1)

    def gather(own, part, m):
        right, down = 12 * part, 4 * part
        top_l = own[m, SHIFT : SHIFT + WINDOW, :]
        top_r = x_right[m, right : right + WINDOW, :]
        low_l = jnp.concatenate([own[m, SHIFT + WINDOW :, :], x_down[m, down : down + SHIFT, :]], 0)
        low_r = jnp.concatenate(
            [x_right[m, right + WINDOW : right + 12, :], x_corner[m, down : down + SHIFT, :]], 0
        )
        tiles = [
            side[:, j * WIDTH : (j + 1) * WIDTH]
            for side in (top_l, top_r, low_l, low_r)
            for j in range(4)
        ]
        return jnp.concatenate(tiles, 0).T

    def scatter(value, keep, part, m):
        rows = value.T
        sides = [
            jnp.concatenate([rows[(4 * s + j) * 8 : (4 * s + j + 1) * 8] for j in range(4)], 1)
            for s in range(4)
        ]
        right, down = 12 * part, 4 * part
        keep[m, 0:WINDOW, :] = sides[0]
        keep[m, WINDOW:, :] = sides[2][:SHIFT]
        send_right[m, right : right + WINDOW, :] = sides[1]
        send_right[m, right + WINDOW : right + 12, :] = sides[3][:SHIFT]
        send_down[m, down : down + SHIFT, :] = sides[2][SHIFT:]
        send_corner[m, down : down + SHIFT, :] = sides[3][SHIFT:]

    def mean_rows(v):
        return jnp.sum(v, 0, keepdims=True) * (1.0 / WIDTH)

    def layer_norm(v):
        centred = v - mean_rows(v)
        rstd = lax.rsqrt(mean_rows(centred * centred) + norm_eps)
        return centred * rstd, rstd

    items = [first_item + step * step_items + m for m in range(step_items)]
    leads = [(lead_ref[i] + 1).astype(f32) * (1.0 / LEAD_STEPS) for i in items]
    raw = per_item(lambda m: gather(x_own, 0, m))
    mean = jnp.concatenate([affine_ref[0]] * step_items, 1)
    inv_std = jnp.concatenate([affine_ref[1]] * step_items, 1)
    normed = (raw - mean) * inv_std
    n_hi, n_lo = split(normed)

    joined = product(qkv_f, n_hi, n_lo)
    query = joined[:WIDTH] + spread_cols(0)
    key = joined[WIDTH : 2 * WIDTH]
    value = joined[2 * WIDTH :] + spread_cols(1)

    def unit(v):
        rows, inverses = [], []
        for h in range(HEADS):
            part = v[h * HEAD_DIM : (h + 1) * HEAD_DIM]
            inverse = lax.rsqrt(jnp.sum(part * part, 0, keepdims=True) + unit_eps)
            rows.append(part * inverse)
            inverses.append(inverse)
        return rows, inverses

    q_rows, q_inv = unit(query)
    k_rows, k_inv = unit(key)
    v_rows = [value[h * HEAD_DIM : (h + 1) * HEAD_DIM] for h in range(HEADS)]

    def of_item(v, m):
        return v[:, m * PAIR : (m + 1) * PAIR]

    def three(a_hi, a_lo, b_hi, b_lo):
        left = jnp.concatenate([a_hi, a_lo, a_hi], 0)
        right = jnp.concatenate([b_hi, b_hi, b_lo], 0)
        return halves(dot(left.T, right))

    def apart(x):
        zero = jnp.zeros_like(x)
        return jnp.concatenate(
            [jnp.where(first_half, x, zero), jnp.where(first_half, zero, x)], 0
        )

    def two_rows(v_hi, v_lo):
        return jnp.concatenate(
            [
                jnp.concatenate([v_hi, v_hi], 1),
                jnp.concatenate([v_lo, jnp.zeros_like(v_lo)], 1),
            ],
            0,
        )

    def over_keys(v_hi, v_lo, e_hi, e_lo):
        r = dot(two_rows(v_hi, v_lo), stack_rows(apart(e_hi), apart(e_lo)))
        return r[:HEAD_DIM] + r[HEAD_DIM:]

    def over_queries(v_hi, v_lo, e_hi, e_lo):
        weights = jnp.concatenate([e_hi, e_lo], 1)
        r = dot_rows(two_rows(apart(v_hi), apart(v_lo)), stack_rows(weights, weights))
        return halves(r[:PLACES] + r[PLACES:])

    pairs = [(m, h) for m in range(step_items) for h in range(HEADS)]
    q_parts = [split(of_item(q_rows[h], m)) for m, h in pairs]
    k_parts = [split(of_item(k_rows[h], m)) for m, h in pairs]
    v_parts = [split(of_item(v_rows[h], m)) for m, h in pairs]
    cosines = [three(*k, *q) for k, q in zip(k_parts, q_parts)]
    expos, inverses = [], []
    for (m, h), cosine in zip(pairs, cosines):
        flag0, flag1 = flags_ref[0, items[m]], flags_ref[1, items[m]]
        offset = jnp.where(first_half, bias_ref[flag0, h], bias_ref[flag1, h])
        expo = jnp.exp(cosine * scale_ref[h : h + 1, :] + offset)
        expos.append(expo)
        inverses.append(1.0 / jnp.sum(expo, 0, keepdims=True))
    e_parts = [split(e) for e in expos]
    mixes = [
        over_keys(*v, *e) * inverse for v, e, inverse in zip(v_parts, e_parts, inverses)
    ]
    mixed = jnp.concatenate(
        [jnp.concatenate(mixes[HEADS * m : HEADS * (m + 1)], 0) for m in range(step_items)], 1
    )

    o_hi, o_lo = split(mixed)
    attn_hat, attn_rstd = layer_norm(product(out_f, o_hi, o_lo) + spread_cols(2))

    def gain(base):
        return per_item(lambda m: 1.0 + col(base) + leads[m] * col(base + 1))

    def shift(base):
        return per_item(lambda m: col(base + 2) + leads[m] * col(base + 3))

    gain0 = gain(4)
    first = normed + attn_hat * gain0 + shift(4)
    f_hi, f_lo = split(first)

    up_bias = jnp.concatenate([up_cols_ref[...]] * step_items, 1)
    u = product(up_f, f_hi, f_lo) + up_bias
    phi, bell = normal_parts(u)
    hidden = u * phi
    slope = phi + bell
    h_hi, h_lo = split(hidden)
    branch = product(down_f, h_hi, h_lo) + spread_cols(3)
    hat, rstd = layer_norm(branch)
    gain1 = gain(8)
    out = first + hat * gain1 + shift(8)
    for m in range(step_items):
        scatter(of_item(out, m), out_keep, 0, m)

    def norm_back(g, hat, rstd, gain, base):
        weighted = g * hat
        for m in range(step_items):
            a, b = of_item(weighted, m), of_item(g, m)
            sums_ref[base] += a
            sums_ref[base + 1] += leads[m] * a
            sums_ref[base + 2] += b
            sums_ref[base + 3] += leads[m] * b
        e = g * gain
        return (e - mean_rows(e) - hat * mean_rows(e * hat)) * rstd

    def add_items(v):
        total = of_item(v, 0)
        for m in range(1, step_items):
            total = total + of_item(v, m)
        return total

    ones_rows = jnp.where(
        lax.broadcasted_iota(jnp.int32, (LANES - WIDTH, step_items * PAIR), 0) == 0, 1.0, 0.0
    ).astype(bf16)
    zero_rows = jnp.zeros((LANES - WIDTH, step_items * PAIR), bf16)

    def outer(a_hi, a_lo, b_hi, b_lo):
        right = jnp.concatenate([b_hi, ones_rows, b_lo, zero_rows], 0)
        r = dot_rows(stack_rows(a_hi, a_lo), right)
        m = a_hi.shape[0]
        return (r[:m, :LANES] + r[m:, :LANES]) + r[:m, LANES:]

    cot = per_item(lambda m: gather(ct_own, 1, m))
    d_branch = norm_back(cot, hat, rstd, gain1, 4)
    sums_ref[8] += add_items(d_branch)
    z_hi, z_lo = split(d_branch)
    g_down_ref[...] += outer(h_hi, h_lo, z_hi, z_lo)
    d_pre = product(down_b, z_hi, z_lo) * slope
    p_hi, p_lo = split(d_pre)
    g_up_ref[...] += outer(p_hi, p_lo, f_hi, f_lo)
    d_first = cot + product(up_b, p_hi, p_lo)
    d_attn = norm_back(d_first, attn_hat, attn_rstd, gain0, 0)
    a_hi, a_lo = split(d_attn)
    g_out_ref[...] += outer(a_hi, a_lo, o_hi, o_lo)
    d_mixed = product(out_b, a_hi, a_lo)

    d_outs = [
        of_item(d_mixed, m)[h * HEAD_DIM : (h + 1) * HEAD_DIM] * inverse
        for (m, h), inverse in zip(pairs, inverses)
    ]
    d_parts = [split(d) for d in d_outs]
    d_probs = [three(*v, *d) for v, d in zip(v_parts, d_parts)]
    s_parts = []
    for n, (m, h) in enumerate(pairs):
        delta = jnp.sum(d_outs[n] * mixes[n], 0, keepdims=True)
        d_scores = expos[n] * (d_probs[n] - delta)
        dpos_ref[h] += d_scores
        folded = d_scores * cosines[n]
        total = folded[0:8]
        for i in range(1, PLACES // 8):
            total = total + folded[8 * i : 8 * i + 8]
        dcos_ref[h] += total
        s_parts.append(split(d_scores))
    dv_rows = [over_queries(*d, *e) for d, e in zip(d_parts, e_parts)]
    dk_rows = [over_queries(*q, *d) for q, d in zip(q_parts, s_parts)]
    dq_rows = [over_keys(*k, *d) for k, d in zip(k_parts, s_parts)]

    def unit_back(grads, rows, inverse):
        out = []
        for n, (m, h) in enumerate(pairs):
            d = grads[n] * scale_ref[h : h + 1, :]
            row = of_item(rows[h], m)
            d = d - row * jnp.sum(row * d, 0, keepdims=True)
            out.append(d * of_item(inverse[h], m))
        return out

    dq_rows = unit_back(dq_rows, q_rows, q_inv)
    dk_rows = unit_back(dk_rows, k_rows, k_inv)
    d_joined = jnp.concatenate(
        [
            jnp.concatenate(
                [d for rows in (dq_rows, dk_rows, dv_rows) for d in rows[HEADS * m : HEADS * (m + 1)]], 0
            )
            for m in range(step_items)
        ],
        1,
    )
    j_hi, j_lo = split(d_joined)
    g_qkv_ref[...] += outer(j_hi, j_lo, n_hi, n_lo)
    d_normed = d_first + product(qkv_b, j_hi, j_lo)
    sums_ref[9] += add_items(d_normed)
    sums_ref[10] += add_items(d_normed * normed)
    for m in range(step_items):
        scatter(of_item(d_normed, m), dn_keep, 1, m)

    def finish():
        def lane_sums(v):
            return jnp.sum(v.T, 0, keepdims=True)

        flat_ref[...] = jnp.zeros_like(flat_ref)
        g = g_qkv_ref[...].T
        flat_ref[0:96, :] = g[:WIDTH, :LANES]
        flat_ref[96:192, :] = g[:WIDTH, LANES : 2 * LANES]
        qv = g[WIDTH : WIDTH + 1]
        g_out = g_out_ref[...].T
        flat_ref[192:288, :] = jnp.concatenate([g_out[:WIDTH], g[:WIDTH, 2 * LANES :]], 1)
        g_up = g_up_ref[...].T
        g_down = g_down_ref[...].T
        for k in range(3):
            lanes = slice(k * LANES, (k + 1) * LANES)
            flat_ref[288 + 96 * k : 384 + 96 * k, :] = g_up[:WIDTH, lanes]
            flat_ref[576 + 96 * k : 672 + 96 * k, :] = g_down[:WIDTH, lanes]
            flat_ref[876 + k : 877 + k, :] = g_up[WIDTH : WIDTH + 1, lanes]
        totals = [lane_sums(sums_ref[i]) for i in range(11)]
        for i in range(8):
            flat_ref[864 + i : 865 + i, :WIDTH] = totals[i]
        flat_ref[872:873, :WIDTH] = totals[8]
        flat_ref[873:874, :WIDTH] = g_out[WIDTH : WIDTH + 1]
        flat_ref[874:875, :WIDTH] = qv[:, :WIDTH]
        flat_ref[875:876, :WIDTH] = qv[:, 2 * WIDTH :]
        lane = lax.broadcasted_iota(jnp.int32, (1, LANES), 1)
        scales = jnp.zeros((1, LANES), f32)
        for h in range(HEADS):
            total = jnp.sum(jnp.sum(dcos_ref[h], 0, keepdims=True), 1, keepdims=True)
            scales = jnp.where(lane == WIDTH + h, total * scale_ref[h : h + 1, :], scales)
        flat_ref[864:865, :] = flat_ref[864:865, :] + scales

        rows = []
        for h in range(HEADS):
            d = dpos_ref[h]
            d = jnp.where(first_half, d + pltpu.roll(d, PLACES, 1), 0.0)
            tile = jnp.zeros((WINDOW, LANES), f32)
            for j in range(WINDOW):
                tile = tile + pltpu.roll(d[8 * j : 8 * j + 8], 56 - 8 * j, 1)
            rows.append(jnp.concatenate([tile[r : r + 1] for r in range(WINDOW)], 1))
        rows.append(jnp.zeros((8 - HEADS, WINDOW * LANES), f32))
        found = dot_rows(three_parts(jnp.concatenate(rows, 0)), one_hot(target_ref[...]))
        d_table = add_parts(found)
        d_logit = d_table * gate_ref[...]

        def against(v, units):
            v_hi, v_lo = split(v)
            u_hi, u_lo = split(units)
            both = jnp.concatenate([v_hi.astype(f32), v_lo.astype(f32)], 0).astype(bf16)
            r = dot_rows(both, u_hi)
            return r[:8] + r[8:] + dot_rows(v_hi, u_lo)

        g_w2 = against(d_logit, net_ref[0])
        column = net_columns(vec_ref[16:24, :])
        d_hidden = sum(column(3 + h) * d_logit[h : h + 1] for h in range(HEADS))
        g_first = against(coords_ref[...], d_hidden * net_ref[1])
        for i, row in enumerate(
            [g_first[0:1], g_first[1:2], g_first[2:3], g_w2[0:1], g_w2[1:2], g_w2[2:3]]
        ):
            for k in range(4):
                at = 879 + 4 * i + k
                flat_ref[at : at + 1, :] = row[:, k * LANES : (k + 1) * LANES]

        slots, slot_rows, _ = own_ref.shape
        share = slot_rows - 2
        first_side = side_ref[0] == 0
        for j in range(slots):
            near = flat_ref[share * j : share * (j + 1), :]
            far = flat_ref[share * (slots + j) : share * (slots + j + 1), :]
            own_ref[j, 0:share, :] = jnp.where(first_side, near, far)
            give_ref[j, 0:share, :] = jnp.where(first_side, far, near)
        for ref in (own_ref, give_ref):
            for i in range(2):
                ref[:, share + i : share + i + 1, :WIDTH] = jnp.broadcast_to(
                    totals[9 + i][None], (slots, 1, WIDTH)
                )
                ref[:, share + i : share + i + 1, WIDTH:] = jnp.zeros(
                    (slots, 1, LANES - WIDTH), f32
                )

    if is_last:
        finish()


totals_shapes = [
    (3 * WIDTH, LANES),
    (WIDTH, LANES),
    (HIDDEN, LANES),
    (HIDDEN, LANES),
    (11, WIDTH, LANES),
    (HEADS, PLACES, LANES),
    (HEADS, 8, LANES),
]


def run_block(
    part,
    flags,
    lead,
    side,
    x,
    ct,
    halo,
    stats,
    weights,
    prepared,
    bias_net_parts,
    so_far,
    token_count,
):
    items, tile_rows, flat = x.shape
    half = flat // 2
    items = items // PARTS
    step_items = block_of(items, 16)
    steps = items // step_items
    is_first, is_last = part == 0, part == PARTS - 1

    def rows(n):
        return pl.BlockSpec((step_items, n, half), lambda i: (i, 0, 0))

    smem = pl.BlockSpec(memory_space=pltpu.SMEM)
    field = pl.BlockSpec((step_items, tile_rows, half), lambda i: (part * steps + i, 0, 1))
    out_rows = (12, 12, 24, 8, 8)
    slots = stats.shape[0]
    slot_rows = -(-PAYLOAD // slots)
    slot_rows = -(-(slot_rows + 2) // 8) * 8
    totals = [jax.ShapeDtypeStruct(s, f32) for s in totals_shapes]
    scratch = [pltpu.VMEM((2, WIDTH, LANES), f32)]
    if is_last:
        tail = [
            jax.ShapeDtypeStruct((slots // 2, slot_rows, LANES), f32),
            jax.ShapeDtypeStruct((slots // 2, slot_rows, LANES), f32),
            jax.ShapeDtypeStruct((8, LANES), f32),
        ]
        scratch.append(pltpu.VMEM((slots * (slot_rows - 2), LANES), f32))
        scratch += [pltpu.VMEM(s, f32) for s in totals_shapes]
    else:
        tail = totals
    scratch += [
        pltpu.VMEM((3 * WIDTH, 3 * WIDTH), bf16),
        pltpu.VMEM((WIDTH, 3 * WIDTH), bf16),
        pltpu.VMEM((HIDDEN, 3 * WIDTH), bf16),
        pltpu.VMEM((WIDTH, 3 * HIDDEN), bf16),
        pltpu.VMEM((HIDDEN, 3 * WIDTH), bf16),
        pltpu.VMEM((WIDTH, 3 * HIDDEN), bf16),
        pltpu.VMEM((WIDTH, 3 * WIDTH), bf16),
        pltpu.VMEM((WIDTH, 9 * WIDTH), bf16),
        pltpu.VMEM((12, WIDTH, LANES), f32),
        pltpu.VMEM((HIDDEN, LANES), f32),
        pltpu.VMEM((4, HEADS, PLACES, LANES), f32),
    ]
    constants = (stats, *weights, *prepared, *(bias_net_parts if is_last else ()), *so_far)
    return pl.pallas_call(
        partial(block_kernel, step_items, part * items, float(token_count), is_first, is_last),
        grid=(steps,),
        in_specs=[smem, smem, smem, field, rows(24), rows(8), rows(8), field]
        + [whole(a) for a in constants],
        out_specs=[rows(n) for n in out_rows] + [whole(a) for a in tail],
        out_shape=[jax.ShapeDtypeStruct((items, n, half), f32) for n in out_rows] + tail,
        scratch_shapes=scratch,
        cost_estimate=about(40),
        compiler_params=pltpu.CompilerParams(
            dimension_semantics=("arbitrary",), vmem_limit_bytes=65024 * 1024
        ),
    )(flags, lead, side, x, *halo, ct, *constants)


def place(ref_out, m, keep, right, down, corner, part, fn):
    half = keep.shape[2]
    at, low = 12 * part, 4 * part
    for rows, left, own in (
        (slice(0, SHIFT), corner[m, low : low + SHIFT, :], down[m, low : low + SHIFT, :]),
        (slice(SHIFT, 16), right[m, at : at + 12, :], keep[m]),
    ):
        for lanes, value in ((slice(0, half), left), (slice(half, 2 * half), own)):
            ref_out[m, rows, lanes] = fn(value, rows, lanes)


def final_kernel(token_count, part_steps, x_ref, norm_ref, sums_ref, *refs):
    cols = x_ref.shape[2] // WIDTH
    out_ref, grad_ref = refs[-2:]

    def wide(row):
        return jnp.concatenate([row[:, :WIDTH]] * cols, 1)

    mean, inv_std = norm_ref[0:1], norm_ref[1:2]
    at = sums_ref.shape[1] - 2
    mean_grad = sums_ref[0, at : at + 1] * (1.0 / token_count)
    mean_cross = sums_ref[0, at + 1 : at + 2] * (1.0 / token_count)
    factor, centre = wide(inv_std), wide(mean)
    offset, slope = wide(inv_std * mean_grad), wide(inv_std * inv_std * mean_cross)

    def work(out_keep, dn_keep, *halo):
        for m in range(x_ref.shape[0]):

            def grad(v, rows, lanes):
                x = x_ref[m, rows, lanes] - centre[:, lanes]
                return factor[:, lanes] * v - offset[:, lanes] - x * slope[:, lanes]

            place(out_ref, m, out_keep, *halo, 0, lambda v, rows, lanes: v)
            place(grad_ref, m, dn_keep, *halo, 1, grad)

    for n in range(PARTS):
        pl.when(pl.program_id(0) // part_steps == n)(partial(work, *refs[5 * n : 5 * n + 5]))


def finish_fields(x, parts, norm, sums, token_count):
    items, rows, flat = x.shape
    step_items = block_of(items // PARTS, 16)
    part_steps = items // PARTS // step_items

    def spec(part, n):
        return pl.BlockSpec(
            (step_items, n, flat // 2),
            lambda i: (jnp.clip(i - part * part_steps, 0, part_steps - 1), 0, 0),
        )

    field = pl.BlockSpec((step_items, rows, flat), lambda i: (i, 0, 0))
    return pl.pallas_call(
        partial(final_kernel, float(token_count), part_steps),
        grid=(items // step_items,),
        in_specs=[
            field,
            whole(norm),
            pl.BlockSpec((1,) + sums.shape[1:], lambda i: (0, 0, 0)),
        ]
        + [spec(part, n) for part in range(PARTS) for n in (12, 12, 24, 8, 8)],
        out_specs=[field] * 2,
        out_shape=[jax.ShapeDtypeStruct(x.shape, f32)] * 2,
        cost_estimate=about(60),
        compiler_params=in_order,
    )(x, norm, sums, *[a for part in parts for a in part])


def sum_slots_kernel(slots_ref, all_ref):
    total = slots_ref[0]
    for j in range(1, slots_ref.shape[0]):
        total = total + slots_ref[j]
    all_ref[...] = jnp.broadcast_to(total[None], all_ref.shape)


def sum_slots(slots):
    return pl.pallas_call(
        sum_slots_kernel,
        grid=(1,),
        in_specs=[whole(slots)],
        out_specs=whole(slots),
        out_shape=jax.ShapeDtypeStruct(slots.shape, f32),
        compiler_params=pltpu.CompilerParams(vmem_limit_bytes=16 * 1024 * 1024),
    )(slots)


def unpack_kernel(
    side_ref,
    mine_ref,
    other_ref,
    qkv_ref,
    qv_ref,
    scale_ref,
    w1_ref,
    b1_ref,
    w2_ref,
    out_ref,
    b_out_ref,
    up_ref,
    b_up_ref,
    down_ref,
    b_down_ref,
    norm_ref,
    flat_ref,
):
    slots, slot_rows, _ = mine_ref.shape
    share = slot_rows - 2
    first_side = side_ref[0] == 0
    for j in range(slots):
        mine, other = mine_ref[j, 0:share, :], other_ref[j, 0:share, :]
        flat_ref[share * j : share * (j + 1), :] = jnp.where(first_side, mine, other)
        flat_ref[share * (slots + j) : share * (slots + j + 1), :] = jnp.where(
            first_side, other, mine
        )
    qkv_ref[:, 0:LANES] = flat_ref[0:96, :]
    qkv_ref[:, LANES : 2 * LANES] = flat_ref[96:192, :]
    qkv_ref[:, 2 * LANES :] = flat_ref[192:288, WIDTH:]
    out_ref[...] = flat_ref[192:288, :WIDTH]
    for k in range(3):
        lanes = slice(k * LANES, (k + 1) * LANES)
        up_ref[:, lanes] = flat_ref[288 + 96 * k : 384 + 96 * k, :]
        down_ref[:, lanes] = flat_ref[576 + 96 * k : 672 + 96 * k, :]
        b_up_ref[k : k + 1, :] = flat_ref[876 + k : 877 + k, :]
    norm_ref[...] = flat_ref[864:872, :WIDTH]
    scale_ref[...] = flat_ref[864:865, WIDTH : WIDTH + HEADS]
    b_down_ref[...] = flat_ref[872:873, :WIDTH]
    b_out_ref[...] = flat_ref[873:874, :WIDTH]
    qv_ref[...] = flat_ref[874:876, :WIDTH]
    for k in range(4):
        lanes = slice(k * LANES, (k + 1) * LANES)
        for i in range(2):
            w1_ref[i : i + 1, lanes] = flat_ref[879 + 4 * i + k : 880 + 4 * i + k, :]
        b1_ref[:, lanes] = flat_ref[887 + k : 888 + k, :]
        for i in range(3):
            w2_ref[i : i + 1, lanes] = flat_ref[891 + 4 * i + k : 892 + 4 * i + k, :]


def unpack(side, mine, other):
    slots, slot_rows, _ = mine.shape
    shapes = [
        (WIDTH, 3 * WIDTH),
        (2, WIDTH),
        (1, HEADS),
        (2, 512),
        (1, 512),
        (HEADS, 512),
        (WIDTH, WIDTH),
        (1, WIDTH),
        (WIDTH, HIDDEN),
        (3, LANES),
        (WIDTH, HIDDEN),
        (1, WIDTH),
        (8, WIDTH),
    ]
    shapes = [jax.ShapeDtypeStruct(s, f32) for s in shapes]
    return pl.pallas_call(
        unpack_kernel,
        grid=(1,),
        in_specs=[pl.BlockSpec(memory_space=pltpu.SMEM), whole(mine), whole(other)],
        out_specs=[whole(a) for a in shapes],
        out_shape=shapes,
        compiler_params=pltpu.CompilerParams(vmem_limit_bytes=16 * 1024 * 1024),
        scratch_shapes=[pltpu.VMEM((2 * slots * (slot_rows - 2), LANES), f32)],
    )(side, mine, other)


def take_from(block, dy, dx):
    rows, cols = lax.axis_size("ty"), lax.axis_size(("th", "tl"))
    route = []
    for i in range(rows * cols):
        y, x = divmod(i, cols)
        route.append((((y + dy) % rows) * cols + (x + dx) % cols, i))
    return lax.ppermute(block, axes_tiles, route)


def exchange(slots, axes):
    return lax.all_to_all(slots, axes, 0, 0, tiled=True)


def swap(block):
    return lax.ppermute(block, "tl", [(0, 1), (1, 0)])


def shards(
    inputs,
    regions,
    lead_step_index,
    running_channel_mean,
    running_channel_variance,
    query_key_value_weight,
    query_value_bias,
    log_cosine_scale,
    bias_net_weight1,
    bias_net_bias1,
    bias_net_weight2,
    output_weight,
    projection_bias,
    up_weight,
    up_bias,
    down_weight,
    down_bias,
    conditioned_norm_values,
    cotangent,
):
    items, tile_rows, flat = inputs.shape
    devices = lax.axis_size(axes_all)
    token_count = items * tile_rows * (flat // WIDTH) * devices

    stats, sent = pack(inputs, cotangent, devices)
    stats = exchange(stats, axes_all)
    side = lax.axis_index("tl").astype(jnp.int32).reshape(1)

    vectors = (
        query_value_bias,
        projection_bias,
        down_bias,
        conditioned_norm_values,
        up_bias,
        running_channel_mean,
        running_channel_variance,
        bias_net_weight1,
        bias_net_bias1,
        bias_net_weight2.T,
    )
    coords, target = offset_constants()
    weights = (query_key_value_weight, output_weight, up_weight, down_weight)
    corners = regions.transpose(1, 2, 0)
    (flags, *prepared, net, gate), sent_later = prepare(
        inputs, cotangent, log_cosine_scale, corners, vectors, coords, target
    )
    halos = []
    for right, down, corner in (sent, *sent_later):
        if halos:
            (right, down, corner), halos[-1] = lax.optimization_barrier(
                ((right, down, corner), halos[-1])
            )
        halos.append((take_from(right, 0, 1), take_from(down, 1, 0), take_from(corner, 1, 1)))
    bias_net_parts = (net, gate, coords, target)
    totals, out_parts, dn_parts, home = [], [], [], []
    for part in range(PARTS):
        out_keep, dn_keep, right, down, corner, *totals = run_block(
            part,
            flags,
            lead_step_index,
            side,
            inputs,
            cotangent,
            halos[part],
            stats,
            weights,
            prepared,
            bias_net_parts,
            totals,
            token_count,
        )
        home.append((take_from(right, 0, -1), take_from(down, -1, 0), take_from(corner, -1, -1)))
        out_parts.append(out_keep)
        dn_parts.append(dn_keep)
    own, give, norm = totals
    give, home[:-1] = lax.optimization_barrier((give, home[:-1]))
    shares = sum_slots(exchange(own + swap(give), axes_far))
    outputs, grad_inputs = finish_fields(
        inputs,
        [(o, d, *h) for o, d, h in zip(out_parts, dn_parts, home)],
        norm,
        shares,
        token_count,
    )
    mine = exchange(shares, axes_far)
    mine, outputs, grad_inputs = lax.optimization_barrier((mine, outputs, grad_inputs))
    other = swap(mine)
    (
        g_qkv,
        g_qv,
        g_scale,
        g_w1,
        g_b1,
        g_w2,
        g_out,
        g_b_out,
        g_up,
        g_b_up,
        g_down,
        g_b_down,
        g_norm,
    ) = unpack(side, mine, other)
    return (
        outputs,
        grad_inputs,
        g_qkv,
        g_qv,
        g_scale.reshape(-1),
        g_w1,
        g_b1.reshape(-1),
        g_w2.T,
        g_out,
        g_b_out.reshape(-1),
        g_up,
        g_b_up.reshape(-1),
        g_down,
        g_b_down.reshape(-1),
        g_norm.reshape(2, 4, WIDTH),
        norm[2, :WIDTH],
        norm[3, :WIDTH],
    )


def solution(mesh):
    rows, cols, depth = (mesh.shape[a] for a in ("ty", "tx", "items"))
    split_mesh = jax.sharding.Mesh(mesh.devices.reshape(rows, cols // 2, 2, depth), axes_all)
    tiled = P("items", "ty", ("th", "tl"))
    placed = (tiled, tiled, P("items")) + (P(),) * 15 + (tiled,)
    return jax.shard_map(
        shards,
        mesh=split_mesh,
        in_specs=placed,
        out_specs=(tiled, tiled) + (P(),) * 15,
        check_vma=False,
    )
```

```python
from functools import partial

import jax
import jax.numpy as jnp
import numpy as np
from jax import lax
from jax.experimental import pallas as pl
from jax.experimental.pallas import tpu as pltpu
from jax.sharding import PartitionSpec as P

HEADS = 3
HEAD_DIM = 32
WIDTH = 96
HIDDEN = 384
WINDOW = 8
SHIFT = 4
LEAD_STEPS = 14
PLACES = WINDOW * WINDOW
SPAN = 2 * WINDOW - 1
PAIR = 2 * PLACES
LANES = 128
OFFSETS = 256
PAYLOAD = 903
PARTS = 2

masked_score = -1000000000.0
norm_eps = 1e-05
unit_eps = 1e-06
momentum = 0.1
axes_all = ("ty", "th", "tl", "items")
axes_far = ("ty", "th", "items")
axes_tiles = ("ty", "th", "tl")

f32 = jnp.float32
bf16 = jnp.bfloat16

in_order = pltpu.CompilerParams(
    dimension_semantics=("arbitrary",), vmem_limit_bytes=60 * 1024 * 1024
)


def about(microseconds):
    return pl.CostEstimate(flops=microseconds * 10**9, bytes_accessed=10**6, transcendentals=0)


def block_of(items, most=8):
    return max(n for n in range(1, most + 1) if items % n == 0)


def whole(a):
    return pl.BlockSpec(a.shape, lambda i: (0,) * len(a.shape))


def dot(a, b):
    return lax.dot_general(a, b, (((1,), (0,)), ((), ())), preferred_element_type=f32)


def dot_rows(a, b):
    return lax.dot_general(a, b, (((1,), (1,)), ((), ())), preferred_element_type=f32)


def split(x):
    hi = x.astype(bf16)
    return hi, (x - hi.astype(f32)).astype(bf16)


def normal_parts(u):
    phi = 0.5 + 0.5 * lax.erf(u * 0.7071067811865476)
    return phi, (u * 0.3989422804014327) * jnp.exp(-0.5 * (u * u))


def pack_halo(fields, tops, right_ref, down_ref, corner_ref):
    for part, (ref, top) in enumerate(zip(fields, tops)):
        right_ref[:, 12 * part : 12 * part + 12, :] = ref[:, SHIFT:, :]
        corner_ref[:, 4 * part : 4 * part + 4, :] = ref[:, :SHIFT, :]
        down_ref[:, 4 * part : 4 * part + 4, :] = top[:, :SHIFT, :]


def pack_kernel(
    items, part_steps, x_ref, ct_ref, ct_top_ref, stats_ref, right_ref, down_ref, corner_ref, sums_ref
):
    step = pl.program_id(0)
    step_items, rows, flat = x_ref.shape
    cols = flat // WIDTH
    half = flat // 2

    @pl.when(step >= pl.num_programs(0) - part_steps)
    def _():
        fields = (x_ref.at[:, :, :half], ct_ref)
        pack_halo(fields, (x_ref.at[:, :, half:], ct_top_ref), right_ref, down_ref, corner_ref)

    def fold(v):
        total = v[:, :WIDTH]
        for j in range(1, cols):
            total = total + v[:, j * WIDTH : (j + 1) * WIDTH]
        return jnp.sum(total, 0, keepdims=True)

    def total(fn):
        acc = jnp.zeros((8, flat), f32)
        for i in range(step_items):
            acc = acc + fn(x_ref[i, 0:8, :]) + fn(x_ref[i, 8:16, :])
        return acc

    @pl.when(step == 0)
    def _():
        pivot = fold(total(lambda v: v)) * (1.0 / (step_items * rows * cols))
        sums_ref[0] = jnp.broadcast_to(jnp.concatenate([pivot] * cols, 1), (8, flat))
        sums_ref[1] = jnp.zeros((8, flat), f32)
        sums_ref[2] = jnp.zeros((8, flat), f32)

    pivot = sums_ref[0]
    sums_ref[1] += total(lambda v: v - pivot)
    sums_ref[2] += total(lambda v: (v - pivot) * (v - pivot))

    @pl.when(step == pl.num_programs(0) - 1)
    def _():
        count = items * rows * cols
        offset = fold(sums_ref[1]) * (1.0 / count)
        square = fold(sums_ref[2]) - count * offset * offset
        pad = jnp.zeros((1, LANES - WIDTH), f32)
        row = jnp.concatenate([sums_ref[0, 0:1, :WIDTH] + offset, pad, square, pad], 1)
        stats_ref[...] = jnp.broadcast_to(row[None], stats_ref.shape)


def pack(x, ct, devices):
    items, rows, flat = x.shape
    half = flat // 2
    part_items = items // PARTS
    step_items = block_of(part_items, 16)
    part_steps = part_items // step_items
    steps = items // step_items

    def of_part(count, lanes):
        return pl.BlockSpec(
            (step_items, count, half),
            lambda i: (jnp.minimum(steps - 1 - i, part_steps - 1), 0, lanes),
        )

    stats = jax.ShapeDtypeStruct((devices, 1, 2 * LANES), f32)
    counts = (24, 8, 8)
    stats, *sent = pl.pallas_call(
        partial(pack_kernel, items, part_steps),
        grid=(steps,),
        in_specs=[
            pl.BlockSpec((step_items, rows, flat), lambda i: (steps - 1 - i, 0, 0)),
            of_part(rows, 0),
            of_part(8, 1),
        ],
        out_specs=[whole(stats)] + [of_part(c, 0) for c in counts],
        out_shape=[stats] + [jax.ShapeDtypeStruct((part_items, c, half), f32) for c in counts],
        scratch_shapes=[pltpu.VMEM((3, 8, flat), f32)],
        cost_estimate=about(4),
        compiler_params=in_order,
    )(x, ct, ct)
    return stats, sent


def offset_constants():
    coords = np.zeros((8, OFFSETS), np.float32)
    o = np.arange(SPAN * SPAN)
    for k, along in enumerate((o // SPAN - (WINDOW - 1), o % SPAN - (WINDOW - 1))):
        u = along.astype(np.float32) * np.float32(8.0 / (WINDOW - 1))
        coords[k, : SPAN * SPAN] = np.sign(u) * np.log2(np.abs(u) + np.float32(1.0)) / np.float32(3.0)
    coords[2, : SPAN * SPAN] = 1.0
    key_row, lane = np.divmod(np.arange(WINDOW * LANES), LANES)
    across, row = np.divmod(lane, WINDOW)
    target = (row - key_row + WINDOW - 1) * SPAN + across
    target = np.where(across < SPAN, target, -1).astype(np.int32)
    return jnp.asarray(coords), jnp.asarray(np.broadcast_to(target, (8, target.size)).copy())


def exact(a, b):
    return jnp.dot(a, b, preferred_element_type=f32, precision=lax.Precision.HIGHEST)


def net_columns(net):
    columns = jnp.concatenate([net, jnp.zeros((LANES - 8, net.shape[1]), f32)], 0).T

    def column(i):
        return jnp.broadcast_to(columns[:, i : i + 1], (net.shape[1], OFFSETS))

    return column


def bias_net(net, coords):
    column = net_columns(net)
    u = column(0) * coords[0:1] + column(1) * coords[1:2] + column(2)
    phi, bell = normal_parts(u)
    return u * phi, phi + bell


def head_rows(net):
    return jnp.concatenate([net[3:6], jnp.zeros((5, net.shape[1]), f32)], 0)


def one_hot(target):
    rows = lax.broadcasted_iota(jnp.int32, (OFFSETS, WINDOW * LANES), 0)
    return jnp.where(rows == target[0:1], 1.0, 0.0).astype(bf16)


def three_parts(v):
    hi, lo = split(v)
    rest = v - hi.astype(f32) - lo.astype(f32)
    return jnp.concatenate([hi.astype(f32), lo.astype(f32), rest], 0).astype(bf16)


def add_parts(v):
    return v[:8] + v[8:16] + v[16:]


def prepare_kernel(
    part_refs,
    log_scale_ref,
    regions_ref,
    qv_ref,
    proj_ref,
    down_ref,
    norms_ref,
    up_ref,
    mean_ref,
    var_ref,
    w1_ref,
    b1_ref,
    w2_ref,
    coords_ref,
    target_ref,
    *refs,
):
    given, (flags_ref, scale_ref, bias_ref, vec_ref, net_ref, gate_ref), sent = (
        refs[: 4 * part_refs],
        refs[4 * part_refs : 4 * part_refs + 6],
        refs[4 * part_refs + 6 :],
    )
    for n in range(part_refs):
        x_ref, ct_ref, x_top_ref, ct_top_ref = given[4 * n : 4 * n + 4]
        pack_halo((x_ref, ct_ref), (x_top_ref, ct_top_ref), *sent[3 * n : 3 * n + 3])
    for w in range(flags_ref.shape[0]):
        first, last = WINDOW * w, WINDOW * w + WINDOW - 1
        corner = regions_ref[first, 0:1, :]
        row_cut = jnp.where(corner != regions_ref[last, 0:1, :], 2, 0)
        col_cut = jnp.where(corner != regions_ref[first, WINDOW - 1 : WINDOW, :], 1, 0)
        flags_ref[w : w + 1, :] = row_cut + col_cut

    def row(ref):
        return ref[...].reshape(1, ref.shape[0])

    vec_ref[...] = jnp.zeros_like(vec_ref)
    vec_ref[0:2, :WIDTH] = qv_ref[...]
    vec_ref[2:3, :WIDTH] = row(proj_ref)
    vec_ref[3:4, :WIDTH] = row(down_ref)
    vec_ref[4:8, :WIDTH] = norms_ref[0]
    vec_ref[8:12, :WIDTH] = norms_ref[1]
    vec_ref[12:13, :HIDDEN] = row(up_ref)
    vec_ref[13:14, :WIDTH] = row(mean_ref)
    vec_ref[14:15, :WIDTH] = row(var_ref)
    units = w1_ref.shape[1]
    net = jnp.concatenate([w1_ref[...], row(b1_ref), w2_ref[...], jnp.zeros((2, units), f32)], 0)
    vec_ref[16:24, :] = net
    lanes = lax.broadcasted_iota(jnp.int32, (1, LANES), 1)
    hidden, slope = bias_net(net, coords_ref[...])
    gate = 1.0 / (1.0 + jnp.exp(-exact(head_rows(net), hidden)))
    net_ref[0] = hidden
    net_ref[1] = slope
    gate_ref[...] = 16.0 * gate * (1.0 - gate)
    spots = one_hot(target_ref[...])
    tiles = add_parts(dot(three_parts(16.0 * gate), spots))
    scale_ref[...] = jnp.zeros_like(scale_ref)
    for h in range(HEADS):
        scale = jnp.exp(jnp.full((1, LANES), log_scale_ref[h], f32))
        scale_ref[h : h + 1, :] = scale
        tile = jnp.concatenate(
            [tiles[h : h + 1, r * LANES : (r + 1) * LANES] for r in range(WINDOW)], 0
        )
        columns = []
        for j in range(WINDOW):
            turned = pltpu.roll(tile, (72 + 8 * j) % LANES, 1)
            columns.append(jnp.where(lanes < PLACES, turned, pltpu.roll(turned, PLACES, 1)))
        bias_ref[h] = jnp.concatenate(columns, 0) - (scale + 16.0)


def prepare(x, ct, log_scale, regions, vectors, coords, target):
    units = vectors[-1].shape[1]
    items, rows, flat = x.shape
    half = flat // 2
    part_items = items // PARTS
    shapes = [
        (8, LANES),
        (HEADS, PLACES, LANES),
        (24, units),
        (2, units, OFFSETS),
        (8, OFFSETS),
    ]
    shapes = [jax.ShapeDtypeStruct(a, f32) for a in shapes]
    flags = jax.ShapeDtypeStruct((regions.shape[0] // WINDOW, regions.shape[2]), jnp.int32)
    shapes = [flags, *shapes]
    shapes += [
        jax.ShapeDtypeStruct((part_items, c, half), f32)
        for _ in range(1, PARTS)
        for c in (24, 8, 8)
    ]
    inputs = (regions, *vectors, coords, target)
    parts = []
    for n in range(1, PARTS):
        parts += [pl.BlockSpec((part_items, rows, half), lambda i, n=n: (n, 0, 0))] * 2
        parts += [pl.BlockSpec((part_items, 8, half), lambda i, n=n: (n, 0, 1))] * 2
    *made, = pl.pallas_call(
        partial(prepare_kernel, PARTS - 1),
        grid=(1,),
        in_specs=[pl.BlockSpec(memory_space=pltpu.SMEM)] + [whole(a) for a in inputs] + parts,
        out_specs=[whole(a) for a in shapes],
        out_shape=shapes,
        cost_estimate=about(0),
        compiler_params=in_order,
    )(log_scale, *inputs, *([x, ct, x, ct] * (PARTS - 1)))
    return made[:6], [made[6 + 3 * n : 9 + 3 * n] for n in range(PARTS - 1)]


def packed(w):
    hi, lo = split(w)
    return jnp.concatenate([hi, lo, hi], 1)


def stack_rows(hi, lo):
    return jnp.concatenate([hi, lo], 0)


def block_kernel(
    step_items,
    first_item,
    token_count,
    is_first,
    is_last,
    flags_ref,
    lead_ref,
    side_ref,
    x_own,
    x_right,
    x_down,
    x_corner,
    ct_own,
    stats_ref,
    w_qkv_ref,
    w_out_ref,
    w_up_ref,
    w_down_ref,
    scale_ref,
    base_ref,
    vec_ref,
    *refs,
):
    step = pl.program_id(0)
    if is_last:
        (net_ref, gate_ref, coords_ref, target_ref), refs = refs[:4], refs[4:]
    refs, scratch = refs[:-11], refs[-11:]
    qkv_f, out_f, up_f, down_f, down_b, up_b, out_b, qkv_b, cols_ref, up_cols_ref, bias_ref = scratch
    count = len(totals_shapes)
    so_far, refs = (refs[:0], refs) if is_first else (refs[:count], refs[count:])
    out_keep, dn_keep, send_right, send_down, send_corner = refs[:5]
    refs = refs[5:]
    if is_last:
        own_ref, give_ref, norm_ref, affine_ref, flat_ref = refs[:5]
        refs = refs[5:]
    else:
        (affine_ref, sums_ref), refs = refs[-2:], refs[:-2]
        passed_ref = refs[4]
        refs = (*refs[:4], sums_ref, *refs[5:])
    g_qkv_ref, g_out_ref, g_up_ref, g_down_ref, sums_ref, dpos_ref, dcos_ref = refs

    @pl.when(step == 0)
    def _():
        every = stats_ref[...]
        devices = every.shape[0]
        means, squares = every[:, 0, :LANES], every[:, 0, LANES:]
        mean = jnp.sum(means, 0, keepdims=True) * (1.0 / devices)
        apart = means - mean
        var = (
            jnp.sum(squares, 0, keepdims=True) * (1.0 / token_count)
            + jnp.sum(apart * apart, 0, keepdims=True) * (1.0 / devices)
        )
        inv_std = lax.rsqrt(var + norm_eps)
        affine_ref[0] = jnp.broadcast_to(mean, (LANES, LANES)).T[:WIDTH]
        affine_ref[1] = jnp.broadcast_to(inv_std, (LANES, LANES)).T[:WIDTH]
        if is_last:
            pad = jnp.zeros((2, LANES - WIDTH), f32)
            running = jnp.concatenate([vec_ref[13:15, :WIDTH], pad], 1)
            norm_ref[0:1] = mean
            norm_ref[1:2] = inv_std
            norm_ref[2:3] = (1.0 - momentum) * running[0:1] + momentum * mean
            norm_ref[3:4] = (1.0 - momentum) * running[1:2] + momentum * var * (
                token_count / (token_count - 1.0)
            )
            norm_ref[4:8] = jnp.zeros((4, LANES), f32)
        for n, ref in enumerate(refs):
            ref[...] = jnp.zeros_like(ref) if is_first or n == 4 else so_far[n][...]
        qkv_f[...] = packed(w_qkv_ref[...].T)
        qkv_b[...] = packed(w_qkv_ref[...])
        out_f[...] = packed(w_out_ref[...].T)
        out_b[...] = packed(w_out_ref[...])
        up_f[...] = packed(w_up_ref[...].T)
        up_b[...] = packed(w_up_ref[...])
        down_b[...] = packed(w_down_ref[...].T)
        down_f[...] = packed(w_down_ref[...])
        for i in range(cols_ref.shape[0]):
            cols_ref[i] = jnp.broadcast_to(vec_ref[i : i + 1, :WIDTH], (LANES, WIDTH)).T
        up_cols_ref[...] = jnp.broadcast_to(vec_ref[12:13, :HIDDEN], (LANES, HIDDEN)).T
        place = lax.broadcasted_iota(jnp.int32, (PLACES, LANES), 0)
        other = lax.broadcasted_iota(jnp.int32, (PLACES, LANES), 1) % PLACES
        apart_r = (place % WINDOW < SHIFT) != (other % WINDOW < SHIFT)
        apart_c = (place // WINDOW < SHIFT) != (other // WINDOW < SHIFT)
        for h in range(HEADS):
            bias = base_ref[h]
            bias_ref[0, h] = bias
            bias_ref[1, h] = jnp.where(apart_c, masked_score, bias)
            bias_ref[2, h] = jnp.where(apart_r, masked_score, bias)
            bias_ref[3, h] = jnp.where(apart_r | apart_c, masked_score, bias)

    first_half = lax.broadcasted_iota(jnp.int32, (1, PAIR), 1) < PLACES

    def product(weight, x_hi, x_lo):
        return dot(weight[...], jnp.concatenate([x_hi, x_hi, x_lo], 0))

    def halves(v):
        m = v.shape[0] // 2
        return jnp.where(first_half, v[:m], v[m:])

    def col(i):
        return cols_ref[i]

    def per_item(fn):
        return jnp.concatenate([fn(m) for m in range(step_items)], 1)

    def spread_cols(i):
        c = col(i)
        return jnp.concatenate([c] * step_items, 1)

    def gather(own, part, m):
        right, down = 12 * part, 4 * part
        top_l = own[m, SHIFT : SHIFT + WINDOW, :]
        top_r = x_right[m, right : right + WINDOW, :]
        low_l = jnp.concatenate([own[m, SHIFT + WINDOW :, :], x_down[m, down : down + SHIFT, :]], 0)
        low_r = jnp.concatenate(
            [x_right[m, right + WINDOW : right + 12, :], x_corner[m, down : down + SHIFT, :]], 0
        )
        tiles = [
            side[:, j * WIDTH : (j + 1) * WIDTH]
            for side in (top_l, top_r, low_l, low_r)
            for j in range(4)
        ]
        return jnp.concatenate(tiles, 0).T

    def scatter(value, keep, part, m):
        rows = value.T
        sides = [
            jnp.concatenate([rows[(4 * s + j) * 8 : (4 * s + j + 1) * 8] for j in range(4)], 1)
            for s in range(4)
        ]
        right, down = 12 * part, 4 * part
        keep[m, 0:WINDOW, :] = sides[0]
        keep[m, WINDOW:, :] = sides[2][:SHIFT]
        send_right[m, right : right + WINDOW, :] = sides[1]
        send_right[m, right + WINDOW : right + 12, :] = sides[3][:SHIFT]
        send_down[m, down : down + SHIFT, :] = sides[2][SHIFT:]
        send_corner[m, down : down + SHIFT, :] = sides[3][SHIFT:]

    def mean_rows(v):
        return jnp.sum(v, 0, keepdims=True) * (1.0 / WIDTH)

    def layer_norm(v):
        centred = v - mean_rows(v)
        rstd = lax.rsqrt(mean_rows(centred * centred) + norm_eps)
        return centred * rstd, rstd

    items = [first_item + step * step_items + m for m in range(step_items)]
    leads = [(lead_ref[i] + 1).astype(f32) * (1.0 / LEAD_STEPS) for i in items]
    raw = per_item(lambda m: gather(x_own, 0, m))
    mean = jnp.concatenate([affine_ref[0]] * step_items, 1)
    inv_std = jnp.concatenate([affine_ref[1]] * step_items, 1)
    normed = (raw - mean) * inv_std
    n_hi, n_lo = split(normed)

    joined = product(qkv_f, n_hi, n_lo)
    query = joined[:WIDTH] + spread_cols(0)
    key = joined[WIDTH : 2 * WIDTH]
    value = joined[2 * WIDTH :] + spread_cols(1)

    def unit(v):
        rows, inverses = [], []
        for h in range(HEADS):
            part = v[h * HEAD_DIM : (h + 1) * HEAD_DIM]
            inverse = lax.rsqrt(jnp.sum(part * part, 0, keepdims=True) + unit_eps)
            rows.append(part * inverse)
            inverses.append(inverse)
        return rows, inverses

    q_rows, q_inv = unit(query)
    k_rows, k_inv = unit(key)
    v_rows = [value[h * HEAD_DIM : (h + 1) * HEAD_DIM] for h in range(HEADS)]

    def of_item(v, m):
        return v[:, m * PAIR : (m + 1) * PAIR]

    def three(a_hi, a_lo, b_hi, b_lo):
        left = jnp.concatenate([a_hi, a_lo, a_hi], 0)
        right = jnp.concatenate([b_hi, b_hi, b_lo], 0)
        return halves(dot(left.T, right))

    def apart(x):
        zero = jnp.zeros_like(x)
        return jnp.concatenate(
            [jnp.where(first_half, x, zero), jnp.where(first_half, zero, x)], 0
        )

    def two_rows(v_hi, v_lo):
        return jnp.concatenate(
            [
                jnp.concatenate([v_hi, v_hi], 1),
                jnp.concatenate([v_lo, jnp.zeros_like(v_lo)], 1),
            ],
            0,
        )

    def over_keys(v_hi, v_lo, e_hi, e_lo):
        r = dot(two_rows(v_hi, v_lo), stack_rows(apart(e_hi), apart(e_lo)))
        return r[:HEAD_DIM] + r[HEAD_DIM:]

    def over_queries(v_hi, v_lo, e_hi, e_lo):
        weights = jnp.concatenate([e_hi, e_lo], 1)
        r = dot_rows(two_rows(apart(v_hi), apart(v_lo)), stack_rows(weights, weights))
        return halves(r[:PLACES] + r[PLACES:])

    pairs = [(m, h) for m in range(step_items) for h in range(HEADS)]
    q_parts = [split(of_item(q_rows[h], m)) for m, h in pairs]
    k_parts = [split(of_item(k_rows[h], m)) for m, h in pairs]
    v_parts = [split(of_item(v_rows[h], m)) for m, h in pairs]
    cosines = [three(*k, *q) for k, q in zip(k_parts, q_parts)]
    expos, inverses = [], []
    for (m, h), cosine in zip(pairs, cosines):
        flag0, flag1 = flags_ref[0, items[m]], flags_ref[1, items[m]]
        offset = jnp.where(first_half, bias_ref[flag0, h], bias_ref[flag1, h])
        expo = jnp.exp(cosine * scale_ref[h : h + 1, :] + offset)
        expos.append(expo)
        inverses.append(1.0 / jnp.sum(expo, 0, keepdims=True))
    e_parts = [split(e) for e in expos]
    mixes = [
        over_keys(*v, *e) * inverse for v, e, inverse in zip(v_parts, e_parts, inverses)
    ]
    mixed = jnp.concatenate(
        [jnp.concatenate(mixes[HEADS * m : HEADS * (m + 1)], 0) for m in range(step_items)], 1
    )

    o_hi, o_lo = split(mixed)
    attn_hat, attn_rstd = layer_norm(product(out_f, o_hi, o_lo) + spread_cols(2))

    def gain(base):
        return per_item(lambda m: 1.0 + col(base) + leads[m] * col(base + 1))

    def shift(base):
        return per_item(lambda m: col(base + 2) + leads[m] * col(base + 3))

    gain0 = gain(4)
    first = normed + attn_hat * gain0 + shift(4)
    f_hi, f_lo = split(first)

    up_bias = jnp.concatenate([up_cols_ref[...]] * step_items, 1)
    u = product(up_f, f_hi, f_lo) + up_bias
    phi, bell = normal_parts(u)
    hidden = u * phi
    slope = phi + bell
    h_hi, h_lo = split(hidden)
    branch = product(down_f, h_hi, h_lo) + spread_cols(3)
    hat, rstd = layer_norm(branch)
    gain1 = gain(8)
    out = first + hat * gain1 + shift(8)
    for m in range(step_items):
        scatter(of_item(out, m), out_keep, 0, m)

    def norm_back(g, hat, rstd, gain, base):
        weighted = g * hat
        for m in range(step_items):
            a, b = of_item(weighted, m), of_item(g, m)
            sums_ref[base] += a
            sums_ref[base + 1] += leads[m] * a
            sums_ref[base + 2] += b
            sums_ref[base + 3] += leads[m] * b
        e = g * gain
        return (e - mean_rows(e) - hat * mean_rows(e * hat)) * rstd

    def add_items(v):
        total = of_item(v, 0)
        for m in range(1, step_items):
            total = total + of_item(v, m)
        return total

    ones_rows = jnp.where(
        lax.broadcasted_iota(jnp.int32, (LANES - WIDTH, step_items * PAIR), 0) == 0, 1.0, 0.0
    ).astype(bf16)
    zero_rows = jnp.zeros((LANES - WIDTH, step_items * PAIR), bf16)

    def outer(a_hi, a_lo, b_hi, b_lo):
        right = jnp.concatenate([b_hi, ones_rows, b_lo, zero_rows], 0)
        r = dot_rows(stack_rows(a_hi, a_lo), right)
        m = a_hi.shape[0]
        return (r[:m, :LANES] + r[m:, :LANES]) + r[:m, LANES:]

    cot = per_item(lambda m: gather(ct_own, 1, m))
    d_branch = norm_back(cot, hat, rstd, gain1, 4)
    sums_ref[8] += add_items(d_branch)
    z_hi, z_lo = split(d_branch)
    g_down_ref[...] += outer(h_hi, h_lo, z_hi, z_lo)
    d_pre = product(down_b, z_hi, z_lo) * slope
    p_hi, p_lo = split(d_pre)
    g_up_ref[...] += outer(p_hi, p_lo, f_hi, f_lo)
    d_first = cot + product(up_b, p_hi, p_lo)
    d_attn = norm_back(d_first, attn_hat, attn_rstd, gain0, 0)
    a_hi, a_lo = split(d_attn)
    g_out_ref[...] += outer(a_hi, a_lo, o_hi, o_lo)
    d_mixed = product(out_b, a_hi, a_lo)

    d_outs = [
        of_item(d_mixed, m)[h * HEAD_DIM : (h + 1) * HEAD_DIM] * inverse
        for (m, h), inverse in zip(pairs, inverses)
    ]
    d_parts = [split(d) for d in d_outs]
    d_probs = [three(*v, *d) for v, d in zip(v_parts, d_parts)]
    s_parts = []
    for n, (m, h) in enumerate(pairs):
        delta = jnp.sum(d_outs[n] * mixes[n], 0, keepdims=True)
        d_scores = expos[n] * (d_probs[n] - delta)
        dpos_ref[h] += d_scores
        folded = d_scores * cosines[n]
        total = folded[0:8]
        for i in range(1, PLACES // 8):
            total = total + folded[8 * i : 8 * i + 8]
        dcos_ref[h] += total
        s_parts.append(split(d_scores))
    dv_rows = [over_queries(*d, *e) for d, e in zip(d_parts, e_parts)]
    dk_rows = [over_queries(*q, *d) for q, d in zip(q_parts, s_parts)]
    dq_rows = [over_keys(*k, *d) for k, d in zip(k_parts, s_parts)]

    def unit_back(grads, rows, inverse):
        out = []
        for n, (m, h) in enumerate(pairs):
            d = grads[n] * scale_ref[h : h + 1, :]
            row = of_item(rows[h], m)
            d = d - row * jnp.sum(row * d, 0, keepdims=True)
            out.append(d * of_item(inverse[h], m))
        return out

    dq_rows = unit_back(dq_rows, q_rows, q_inv)
    dk_rows = unit_back(dk_rows, k_rows, k_inv)
    d_joined = jnp.concatenate(
        [
            jnp.concatenate(
                [d for rows in (dq_rows, dk_rows, dv_rows) for d in rows[HEADS * m : HEADS * (m + 1)]], 0
            )
            for m in range(step_items)
        ],
        1,
    )
    j_hi, j_lo = split(d_joined)
    g_qkv_ref[...] += outer(j_hi, j_lo, n_hi, n_lo)
    d_normed = d_first + product(qkv_b, j_hi, j_lo)
    sums_ref[9] += add_items(d_normed)
    sums_ref[10] += add_items(d_normed * normed)
    for m in range(step_items):
        scatter(of_item(d_normed, m), dn_keep, 1, m)

    def row_sums():
        rows = [jnp.sum(sums_ref[i].T, 0, keepdims=True) for i in range(11)]
        return rows if is_first else [r + so_far[4][i : i + 1, :WIDTH] for i, r in enumerate(rows)]

    def finish():
        flat_ref[...] = jnp.zeros_like(flat_ref)
        g = g_qkv_ref[...].T
        flat_ref[0:96, :] = g[:WIDTH, :LANES]
        flat_ref[96:192, :] = g[:WIDTH, LANES : 2 * LANES]
        qv = g[WIDTH : WIDTH + 1]
        g_out = g_out_ref[...].T
        flat_ref[192:288, :] = jnp.concatenate([g_out[:WIDTH], g[:WIDTH, 2 * LANES :]], 1)
        g_up = g_up_ref[...].T
        g_down = g_down_ref[...].T
        for k in range(3):
            lanes = slice(k * LANES, (k + 1) * LANES)
            flat_ref[288 + 96 * k : 384 + 96 * k, :] = g_up[:WIDTH, lanes]
            flat_ref[576 + 96 * k : 672 + 96 * k, :] = g_down[:WIDTH, lanes]
            flat_ref[876 + k : 877 + k, :] = g_up[WIDTH : WIDTH + 1, lanes]
        totals = row_sums()
        for i in range(8):
            flat_ref[864 + i : 865 + i, :WIDTH] = totals[i]
        flat_ref[872:873, :WIDTH] = totals[8]
        flat_ref[873:874, :WIDTH] = g_out[WIDTH : WIDTH + 1]
        flat_ref[874:875, :WIDTH] = qv[:, :WIDTH]
        flat_ref[875:876, :WIDTH] = qv[:, 2 * WIDTH :]
        lane = lax.broadcasted_iota(jnp.int32, (1, LANES), 1)
        scales = jnp.zeros((1, LANES), f32)
        for h in range(HEADS):
            total = jnp.sum(jnp.sum(dcos_ref[h], 0, keepdims=True), 1, keepdims=True)
            scales = jnp.where(lane == WIDTH + h, total * scale_ref[h : h + 1, :], scales)
        flat_ref[864:865, :] = flat_ref[864:865, :] + scales

        rows = []
        for h in range(HEADS):
            d = dpos_ref[h]
            d = jnp.where(first_half, d + pltpu.roll(d, PLACES, 1), 0.0)
            tile = jnp.zeros((WINDOW, LANES), f32)
            for j in range(WINDOW):
                tile = tile + pltpu.roll(d[8 * j : 8 * j + 8], 56 - 8 * j, 1)
            rows.append(jnp.concatenate([tile[r : r + 1] for r in range(WINDOW)], 1))
        rows.append(jnp.zeros((8 - HEADS, WINDOW * LANES), f32))
        found = dot_rows(three_parts(jnp.concatenate(rows, 0)), one_hot(target_ref[...]))
        d_table = add_parts(found)
        d_logit = d_table * gate_ref[...]

        def against(v, units):
            v_hi, v_lo = split(v)
            u_hi, u_lo = split(units)
            both = jnp.concatenate([v_hi.astype(f32), v_lo.astype(f32)], 0).astype(bf16)
            r = dot_rows(both, u_hi)
            return r[:8] + r[8:] + dot_rows(v_hi, u_lo)

        g_w2 = against(d_logit, net_ref[0])
        column = net_columns(vec_ref[16:24, :])
        d_hidden = sum(column(3 + h) * d_logit[h : h + 1] for h in range(HEADS))
        g_first = against(coords_ref[...], d_hidden * net_ref[1])
        for i, row in enumerate(
            [g_first[0:1], g_first[1:2], g_first[2:3], g_w2[0:1], g_w2[1:2], g_w2[2:3]]
        ):
            for k in range(4):
                at = 879 + 4 * i + k
                flat_ref[at : at + 1, :] = row[:, k * LANES : (k + 1) * LANES]

        slots, slot_rows, _ = own_ref.shape
        share = slot_rows - 2
        first_side = side_ref[0] == 0
        for j in range(slots):
            near = flat_ref[share * j : share * (j + 1), :]
            far = flat_ref[share * (slots + j) : share * (slots + j + 1), :]
            own_ref[j, 0:share, :] = jnp.where(first_side, near, far)
            give_ref[j, 0:share, :] = jnp.where(first_side, far, near)
        for ref in (own_ref, give_ref):
            for i in range(2):
                ref[:, share + i : share + i + 1, :WIDTH] = jnp.broadcast_to(
                    totals[9 + i][None], (slots, 1, WIDTH)
                )
                ref[:, share + i : share + i + 1, WIDTH:] = jnp.zeros(
                    (slots, 1, LANES - WIDTH), f32
                )

    if is_last:
        finish()
    else:
        for i, row in enumerate(row_sums()):
            passed_ref[i : i + 1, :WIDTH] = row


totals_shapes = [
    (3 * WIDTH, LANES),
    (WIDTH, LANES),
    (HIDDEN, LANES),
    (HIDDEN, LANES),
    (11, WIDTH, LANES),
    (HEADS, PLACES, LANES),
    (HEADS, 8, LANES),
]


def run_block(
    part,
    flags,
    lead,
    side,
    x,
    ct,
    halo,
    stats,
    weights,
    prepared,
    bias_net_parts,
    so_far,
    token_count,
):
    items, tile_rows, flat = x.shape
    half = flat // 2
    items = items // PARTS
    step_items = block_of(items, 16)
    steps = items // step_items
    is_first, is_last = part == 0, part == PARTS - 1

    def rows(n):
        return pl.BlockSpec((step_items, n, half), lambda i: (i, 0, 0))

    smem = pl.BlockSpec(memory_space=pltpu.SMEM)
    field = pl.BlockSpec((step_items, tile_rows, half), lambda i: (part * steps + i, 0, 1))
    out_rows = (12, 12, 24, 8, 8)
    slots = stats.shape[0]
    slot_rows = -(-PAYLOAD // slots)
    slot_rows = -(-(slot_rows + 2) // 8) * 8
    totals = [jax.ShapeDtypeStruct(s, f32) for s in totals_shapes]
    totals[4] = jax.ShapeDtypeStruct((16, LANES), f32)
    scratch = [pltpu.VMEM((2, WIDTH, LANES), f32)]
    if is_last:
        tail = [
            jax.ShapeDtypeStruct((slots // 2, slot_rows, LANES), f32),
            jax.ShapeDtypeStruct((slots // 2, slot_rows, LANES), f32),
            jax.ShapeDtypeStruct((8, LANES), f32),
        ]
        scratch.append(pltpu.VMEM((slots * (slot_rows - 2), LANES), f32))
        scratch += [pltpu.VMEM(s, f32) for s in totals_shapes]
    else:
        tail = totals
        scratch.append(pltpu.VMEM(totals_shapes[4], f32))
    scratch += [
        pltpu.VMEM((3 * WIDTH, 3 * WIDTH), bf16),
        pltpu.VMEM((WIDTH, 3 * WIDTH), bf16),
        pltpu.VMEM((HIDDEN, 3 * WIDTH), bf16),
        pltpu.VMEM((WIDTH, 3 * HIDDEN), bf16),
        pltpu.VMEM((HIDDEN, 3 * WIDTH), bf16),
        pltpu.VMEM((WIDTH, 3 * HIDDEN), bf16),
        pltpu.VMEM((WIDTH, 3 * WIDTH), bf16),
        pltpu.VMEM((WIDTH, 9 * WIDTH), bf16),
        pltpu.VMEM((12, WIDTH, LANES), f32),
        pltpu.VMEM((HIDDEN, LANES), f32),
        pltpu.VMEM((4, HEADS, PLACES, LANES), f32),
    ]
    constants = (stats, *weights, *prepared, *(bias_net_parts if is_last else ()), *so_far)
    return pl.pallas_call(
        partial(block_kernel, step_items, part * items, float(token_count), is_first, is_last),
        grid=(steps,),
        in_specs=[smem, smem, smem, field, rows(24), rows(8), rows(8), field]
        + [whole(a) for a in constants],
        out_specs=[rows(n) for n in out_rows] + [whole(a) for a in tail],
        out_shape=[jax.ShapeDtypeStruct((items, n, half), f32) for n in out_rows] + tail,
        scratch_shapes=scratch,
        cost_estimate=about(40),
        compiler_params=pltpu.CompilerParams(
            dimension_semantics=("arbitrary",), vmem_limit_bytes=65024 * 1024
        ),
    )(flags, lead, side, x, *halo, ct, *constants)


def place(ref_out, m, keep, right, down, corner, part, fn):
    half = keep.shape[2]
    at, low = 12 * part, 4 * part
    for rows, left, own in (
        (slice(0, SHIFT), corner[m, low : low + SHIFT, :], down[m, low : low + SHIFT, :]),
        (slice(SHIFT, 16), right[m, at : at + 12, :], keep[m]),
    ):
        for lanes, value in ((slice(0, half), left), (slice(half, 2 * half), own)):
            ref_out[m, rows, lanes] = fn(value, rows, lanes)


def final_kernel(token_count, part_steps, x_ref, norm_ref, sums_ref, *refs):
    cols = x_ref.shape[2] // WIDTH
    out_ref, grad_ref = refs[-2:]

    def wide(row):
        return jnp.concatenate([row[:, :WIDTH]] * cols, 1)

    mean, inv_std = norm_ref[0:1], norm_ref[1:2]
    at = sums_ref.shape[1] - 2
    mean_grad = sums_ref[0, at : at + 1] * (1.0 / token_count)
    mean_cross = sums_ref[0, at + 1 : at + 2] * (1.0 / token_count)
    factor, centre = wide(inv_std), wide(mean)
    offset, slope = wide(inv_std * mean_grad), wide(inv_std * inv_std * mean_cross)

    def work(out_keep, dn_keep, *halo):
        for m in range(x_ref.shape[0]):

            def grad(v, rows, lanes):
                x = x_ref[m, rows, lanes] - centre[:, lanes]
                return factor[:, lanes] * v - offset[:, lanes] - x * slope[:, lanes]

            place(out_ref, m, out_keep, *halo, 0, lambda v, rows, lanes: v)
            place(grad_ref, m, dn_keep, *halo, 1, grad)

    for n in range(PARTS):
        pl.when(pl.program_id(0) // part_steps == n)(partial(work, *refs[5 * n : 5 * n + 5]))


def finish_fields(x, parts, norm, sums, token_count):
    items, rows, flat = x.shape
    step_items = block_of(items // PARTS, 16)
    part_steps = items // PARTS // step_items

    def spec(part, n):
        return pl.BlockSpec(
            (step_items, n, flat // 2),
            lambda i: (jnp.clip(i - part * part_steps, 0, part_steps - 1), 0, 0),
        )

    field = pl.BlockSpec((step_items, rows, flat), lambda i: (i, 0, 0))
    return pl.pallas_call(
        partial(final_kernel, float(token_count), part_steps),
        grid=(items // step_items,),
        in_specs=[
            field,
            whole(norm),
            pl.BlockSpec((1,) + sums.shape[1:], lambda i: (0, 0, 0)),
        ]
        + [spec(part, n) for part in range(PARTS) for n in (12, 12, 24, 8, 8)],
        out_specs=[field] * 2,
        out_shape=[jax.ShapeDtypeStruct(x.shape, f32)] * 2,
        cost_estimate=about(60),
        compiler_params=in_order,
    )(x, norm, sums, *[a for part in parts for a in part])


def sum_slots_kernel(slots_ref, all_ref):
    total = slots_ref[0]
    for j in range(1, slots_ref.shape[0]):
        total = total + slots_ref[j]
    all_ref[...] = jnp.broadcast_to(total[None], all_ref.shape)


def sum_slots(slots):
    return pl.pallas_call(
        sum_slots_kernel,
        grid=(1,),
        in_specs=[whole(slots)],
        out_specs=whole(slots),
        out_shape=jax.ShapeDtypeStruct(slots.shape, f32),
        compiler_params=pltpu.CompilerParams(vmem_limit_bytes=16 * 1024 * 1024),
    )(slots)


def unpack_kernel(
    side_ref,
    mine_ref,
    other_ref,
    qkv_ref,
    qv_ref,
    scale_ref,
    w1_ref,
    b1_ref,
    w2_ref,
    out_ref,
    b_out_ref,
    up_ref,
    b_up_ref,
    down_ref,
    b_down_ref,
    norm_ref,
    flat_ref,
):
    slots, slot_rows, _ = mine_ref.shape
    share = slot_rows - 2
    first_side = side_ref[0] == 0
    for j in range(slots):
        mine, other = mine_ref[j, 0:share, :], other_ref[j, 0:share, :]
        flat_ref[share * j : share * (j + 1), :] = jnp.where(first_side, mine, other)
        flat_ref[share * (slots + j) : share * (slots + j + 1), :] = jnp.where(
            first_side, other, mine
        )
    qkv_ref[:, 0:LANES] = flat_ref[0:96, :]
    qkv_ref[:, LANES : 2 * LANES] = flat_ref[96:192, :]
    qkv_ref[:, 2 * LANES :] = flat_ref[192:288, WIDTH:]
    out_ref[...] = flat_ref[192:288, :WIDTH]
    for k in range(3):
        lanes = slice(k * LANES, (k + 1) * LANES)
        up_ref[:, lanes] = flat_ref[288 + 96 * k : 384 + 96 * k, :]
        down_ref[:, lanes] = flat_ref[576 + 96 * k : 672 + 96 * k, :]
        b_up_ref[k : k + 1, :] = flat_ref[876 + k : 877 + k, :]
    norm_ref[...] = flat_ref[864:872, :WIDTH]
    scale_ref[...] = flat_ref[864:865, WIDTH : WIDTH + HEADS]
    b_down_ref[...] = flat_ref[872:873, :WIDTH]
    b_out_ref[...] = flat_ref[873:874, :WIDTH]
    qv_ref[...] = flat_ref[874:876, :WIDTH]
    for k in range(4):
        lanes = slice(k * LANES, (k + 1) * LANES)
        for i in range(2):
            w1_ref[i : i + 1, lanes] = flat_ref[879 + 4 * i + k : 880 + 4 * i + k, :]
        b1_ref[:, lanes] = flat_ref[887 + k : 888 + k, :]
        for i in range(3):
            w2_ref[i : i + 1, lanes] = flat_ref[891 + 4 * i + k : 892 + 4 * i + k, :]


def unpack(side, mine, other):
    slots, slot_rows, _ = mine.shape
    shapes = [
        (WIDTH, 3 * WIDTH),
        (2, WIDTH),
        (1, HEADS),
        (2, 512),
        (1, 512),
        (HEADS, 512),
        (WIDTH, WIDTH),
        (1, WIDTH),
        (WIDTH, HIDDEN),
        (3, LANES),
        (WIDTH, HIDDEN),
        (1, WIDTH),
        (8, WIDTH),
    ]
    shapes = [jax.ShapeDtypeStruct(s, f32) for s in shapes]
    return pl.pallas_call(
        unpack_kernel,
        grid=(1,),
        in_specs=[pl.BlockSpec(memory_space=pltpu.SMEM), whole(mine), whole(other)],
        out_specs=[whole(a) for a in shapes],
        out_shape=shapes,
        compiler_params=pltpu.CompilerParams(vmem_limit_bytes=16 * 1024 * 1024),
        scratch_shapes=[pltpu.VMEM((2 * slots * (slot_rows - 2), LANES), f32)],
    )(side, mine, other)


def take_from(block, dy, dx):
    rows, cols = lax.axis_size("ty"), lax.axis_size(("th", "tl"))
    route = []
    for i in range(rows * cols):
        y, x = divmod(i, cols)
        route.append((((y + dy) % rows) * cols + (x + dx) % cols, i))
    return lax.ppermute(block, axes_tiles, route)


def exchange(slots, axes):
    return lax.all_to_all(slots, axes, 0, 0, tiled=True)


def swap(block):
    return lax.ppermute(block, "tl", [(0, 1), (1, 0)])


def shards(
    inputs,
    regions,
    lead_step_index,
    running_channel_mean,
    running_channel_variance,
    query_key_value_weight,
    query_value_bias,
    log_cosine_scale,
    bias_net_weight1,
    bias_net_bias1,
    bias_net_weight2,
    output_weight,
    projection_bias,
    up_weight,
    up_bias,
    down_weight,
    down_bias,
    conditioned_norm_values,
    cotangent,
):
    items, tile_rows, flat = inputs.shape
    devices = lax.axis_size(axes_all)
    token_count = items * tile_rows * (flat // WIDTH) * devices

    stats, sent = pack(inputs, cotangent, devices)
    stats = exchange(stats, axes_all)
    side = lax.axis_index("tl").astype(jnp.int32).reshape(1)

    vectors = (
        query_value_bias,
        projection_bias,
        down_bias,
        conditioned_norm_values,
        up_bias,
        running_channel_mean,
        running_channel_variance,
        bias_net_weight1,
        bias_net_bias1,
        bias_net_weight2.T,
    )
    coords, target = offset_constants()
    weights = (query_key_value_weight, output_weight, up_weight, down_weight)
    corners = regions.transpose(1, 2, 0)
    (flags, *prepared, net, gate), sent_later = prepare(
        inputs, cotangent, log_cosine_scale, corners, vectors, coords, target
    )
    halos = []
    for right, down, corner in (sent, *sent_later):
        if halos:
            (right, down, corner), halos[-1] = lax.optimization_barrier(
                ((right, down, corner), halos[-1])
            )
        halos.append((take_from(right, 0, 1), take_from(down, 1, 0), take_from(corner, 1, 1)))
    bias_net_parts = (net, gate, coords, target)
    totals, out_parts, dn_parts, home = [], [], [], []
    for part in range(PARTS):
        out_keep, dn_keep, right, down, corner, *totals = run_block(
            part,
            flags,
            lead_step_index,
            side,
            inputs,
            cotangent,
            halos[part],
            stats,
            weights,
            prepared,
            bias_net_parts,
            totals,
            token_count,
        )
        home.append((take_from(right, 0, -1), take_from(down, -1, 0), take_from(corner, -1, -1)))
        out_parts.append(out_keep)
        dn_parts.append(dn_keep)
    own, give, norm = totals
    give, home[:-1] = lax.optimization_barrier((give, home[:-1]))
    shares = sum_slots(exchange(own + swap(give), axes_far))
    outputs, grad_inputs = finish_fields(
        inputs,
        [(o, d, *h) for o, d, h in zip(out_parts, dn_parts, home)],
        norm,
        shares,
        token_count,
    )
    mine = exchange(shares, axes_far)
    mine, outputs, grad_inputs = lax.optimization_barrier((mine, outputs, grad_inputs))
    other = swap(mine)
    (
        g_qkv,
        g_qv,
        g_scale,
        g_w1,
        g_b1,
        g_w2,
        g_out,
        g_b_out,
        g_up,
        g_b_up,
        g_down,
        g_b_down,
        g_norm,
    ) = unpack(side, mine, other)
    return (
        outputs,
        grad_inputs,
        g_qkv,
        g_qv,
        g_scale.reshape(-1),
        g_w1,
        g_b1.reshape(-1),
        g_w2.T,
        g_out,
        g_b_out.reshape(-1),
        g_up,
        g_b_up.reshape(-1),
        g_down,
        g_b_down.reshape(-1),
        g_norm.reshape(2, 4, WIDTH),
        norm[2, :WIDTH],
        norm[3, :WIDTH],
    )


def solution(mesh):
    rows, cols, depth = (mesh.shape[a] for a in ("ty", "tx", "items"))
    split_mesh = jax.sharding.Mesh(mesh.devices.reshape(rows, cols // 2, 2, depth), axes_all)
    tiled = P("items", "ty", ("th", "tl"))
    placed = (tiled, tiled, P("items")) + (P(),) * 15 + (tiled,)
    return jax.shard_map(
        shards,
        mesh=split_mesh,
        in_specs=placed,
        out_specs=(tiled, tiled) + (P(),) * 15,
        check_vma=False,
    )
```

```python
from functools import partial

import jax
import jax.numpy as jnp
import numpy as np
from jax import lax
from jax.experimental import pallas as pl
from jax.experimental.pallas import tpu as pltpu
from jax.sharding import PartitionSpec as P

HEADS = 3
HEAD_DIM = 32
WIDTH = 96
HIDDEN = 384
WINDOW = 8
SHIFT = 4
LEAD_STEPS = 14
PLACES = WINDOW * WINDOW
SPAN = 2 * WINDOW - 1
PAIR = 2 * PLACES
LANES = 128
OFFSETS = 256
PAYLOAD = 903
PARTS = 2

masked_score = -1000000000.0
norm_eps = 1e-05
unit_eps = 1e-06
momentum = 0.1
axes_all = ("ty", "th", "tl", "items")
axes_far = ("ty", "th", "items")
axes_tiles = ("ty", "th", "tl")

f32 = jnp.float32
bf16 = jnp.bfloat16

in_order = pltpu.CompilerParams(
    dimension_semantics=("arbitrary",), vmem_limit_bytes=60 * 1024 * 1024
)


def about(microseconds):
    return pl.CostEstimate(flops=microseconds * 10**9, bytes_accessed=10**6, transcendentals=0)


def block_of(items, most=8):
    return max(n for n in range(1, most + 1) if items % n == 0)


def whole(a):
    return pl.BlockSpec(a.shape, lambda i: (0,) * len(a.shape))


def dot(a, b):
    return lax.dot_general(a, b, (((1,), (0,)), ((), ())), preferred_element_type=f32)


def dot_rows(a, b):
    return lax.dot_general(a, b, (((1,), (1,)), ((), ())), preferred_element_type=f32)


def split(x):
    hi = x.astype(bf16)
    return hi, (x - hi.astype(f32)).astype(bf16)


def normal_parts(u):
    phi = 0.5 + 0.5 * lax.erf(u * 0.7071067811865476)
    return phi, (u * 0.3989422804014327) * jnp.exp(-0.5 * (u * u))


def pack_halo(fields, tops, right_ref, down_ref, corner_ref):
    for part, (ref, top) in enumerate(zip(fields, tops)):
        right_ref[:, 12 * part : 12 * part + 12, :] = ref[:, SHIFT:, :]
        corner_ref[:, 4 * part : 4 * part + 4, :] = ref[:, :SHIFT, :]
        down_ref[:, 4 * part : 4 * part + 4, :] = top[:, :SHIFT, :]


def pack_kernel(
    items, part_steps, x_ref, ct_ref, ct_top_ref, stats_ref, right_ref, down_ref, corner_ref, sums_ref
):
    step = pl.program_id(0)
    step_items, rows, flat = x_ref.shape
    cols = flat // WIDTH
    half = flat // 2

    @pl.when(step >= pl.num_programs(0) - part_steps)
    def _():
        fields = (x_ref.at[:, :, :half], ct_ref)
        pack_halo(fields, (x_ref.at[:, :, half:], ct_top_ref), right_ref, down_ref, corner_ref)

    def fold(v):
        total = v[:, :WIDTH]
        for j in range(1, cols):
            total = total + v[:, j * WIDTH : (j + 1) * WIDTH]
        return jnp.sum(total, 0, keepdims=True)

    def total(fn):
        acc = jnp.zeros((8, flat), f32)
        for i in range(step_items):
            acc = acc + fn(x_ref[i, 0:8, :]) + fn(x_ref[i, 8:16, :])
        return acc

    @pl.when(step == 0)
    def _():
        pivot = fold(total(lambda v: v)) * (1.0 / (step_items * rows * cols))
        sums_ref[0] = jnp.broadcast_to(jnp.concatenate([pivot] * cols, 1), (8, flat))
        sums_ref[1] = jnp.zeros((8, flat), f32)
        sums_ref[2] = jnp.zeros((8, flat), f32)

    pivot = sums_ref[0]
    sums_ref[1] += total(lambda v: v - pivot)
    sums_ref[2] += total(lambda v: (v - pivot) * (v - pivot))

    @pl.when(step == pl.num_programs(0) - 1)
    def _():
        count = items * rows * cols
        offset = fold(sums_ref[1]) * (1.0 / count)
        square = fold(sums_ref[2]) - count * offset * offset
        pad = jnp.zeros((1, LANES - WIDTH), f32)
        row = jnp.concatenate([sums_ref[0, 0:1, :WIDTH] + offset, pad, square, pad], 1)
        stats_ref[...] = jnp.broadcast_to(row[None], stats_ref.shape)


def pack(x, ct, devices):
    items, rows, flat = x.shape
    half = flat // 2
    part_items = items // PARTS
    step_items = block_of(part_items, 16)
    part_steps = part_items // step_items
    steps = items // step_items

    def of_part(count, lanes):
        return pl.BlockSpec(
            (step_items, count, half),
            lambda i: (jnp.minimum(steps - 1 - i, part_steps - 1), 0, lanes),
        )

    stats = jax.ShapeDtypeStruct((devices, 1, 2 * LANES), f32)
    counts = (24, 8, 8)
    stats, *sent = pl.pallas_call(
        partial(pack_kernel, items, part_steps),
        grid=(steps,),
        in_specs=[
            pl.BlockSpec((step_items, rows, flat), lambda i: (steps - 1 - i, 0, 0)),
            of_part(rows, 0),
            of_part(8, 1),
        ],
        out_specs=[whole(stats)] + [of_part(c, 0) for c in counts],
        out_shape=[stats] + [jax.ShapeDtypeStruct((part_items, c, half), f32) for c in counts],
        scratch_shapes=[pltpu.VMEM((3, 8, flat), f32)],
        cost_estimate=about(4),
        compiler_params=in_order,
    )(x, ct, ct)
    return stats, sent


def offset_constants():
    coords = np.zeros((8, OFFSETS), np.float32)
    o = np.arange(SPAN * SPAN)
    for k, along in enumerate((o // SPAN - (WINDOW - 1), o % SPAN - (WINDOW - 1))):
        u = along.astype(np.float32) * np.float32(8.0 / (WINDOW - 1))
        coords[k, : SPAN * SPAN] = np.sign(u) * np.log2(np.abs(u) + np.float32(1.0)) / np.float32(3.0)
    coords[2, : SPAN * SPAN] = 1.0
    key_row, lane = np.divmod(np.arange(WINDOW * LANES), LANES)
    across, row = np.divmod(lane, WINDOW)
    target = (row - key_row + WINDOW - 1) * SPAN + across
    target = np.where(across < SPAN, target, -1).astype(np.int32)
    return jnp.asarray(coords), jnp.asarray(np.broadcast_to(target, (8, target.size)).copy())


def exact(a, b):
    return jnp.dot(a, b, preferred_element_type=f32, precision=lax.Precision.HIGHEST)


def net_columns(net):
    columns = jnp.concatenate([net, jnp.zeros((LANES - 8, net.shape[1]), f32)], 0).T

    def column(i):
        return jnp.broadcast_to(columns[:, i : i + 1], (net.shape[1], OFFSETS))

    return column


def bias_net(net, coords):
    column = net_columns(net)
    u = column(0) * coords[0:1] + column(1) * coords[1:2] + column(2)
    phi, bell = normal_parts(u)
    return u * phi, phi + bell


def head_rows(net):
    return jnp.concatenate([net[3:6], jnp.zeros((5, net.shape[1]), f32)], 0)


def one_hot(target):
    rows = lax.broadcasted_iota(jnp.int32, (OFFSETS, WINDOW * LANES), 0)
    return jnp.where(rows == target[0:1], 1.0, 0.0).astype(bf16)


def three_parts(v):
    hi, lo = split(v)
    rest = v - hi.astype(f32) - lo.astype(f32)
    return jnp.concatenate([hi.astype(f32), lo.astype(f32), rest], 0).astype(bf16)


def add_parts(v):
    return v[:8] + v[8:16] + v[16:]


def prepare_kernel(
    part_refs,
    log_scale_ref,
    regions_ref,
    qv_ref,
    proj_ref,
    down_ref,
    norms_ref,
    up_ref,
    mean_ref,
    var_ref,
    w1_ref,
    b1_ref,
    w2_ref,
    coords_ref,
    target_ref,
    *refs,
):
    given, (flags_ref, scale_ref, bias_ref, vec_ref, gate_ref), sent = (
        refs[: 4 * part_refs],
        refs[4 * part_refs : 4 * part_refs + 5],
        refs[4 * part_refs + 5 :],
    )
    for n in range(part_refs):
        x_ref, ct_ref, x_top_ref, ct_top_ref = given[4 * n : 4 * n + 4]
        pack_halo((x_ref, ct_ref), (x_top_ref, ct_top_ref), *sent[3 * n : 3 * n + 3])
    for w in range(flags_ref.shape[0]):
        first, last = WINDOW * w, WINDOW * w + WINDOW - 1
        corner = regions_ref[first, 0:1, :]
        row_cut = jnp.where(corner != regions_ref[last, 0:1, :], 2, 0)
        col_cut = jnp.where(corner != regions_ref[first, WINDOW - 1 : WINDOW, :], 1, 0)
        flags_ref[w : w + 1, :] = row_cut + col_cut

    def row(ref):
        return ref[...].reshape(1, ref.shape[0])

    vec_ref[...] = jnp.zeros_like(vec_ref)
    vec_ref[0:2, :WIDTH] = qv_ref[...]
    vec_ref[2:3, :WIDTH] = row(proj_ref)
    vec_ref[3:4, :WIDTH] = row(down_ref)
    vec_ref[4:8, :WIDTH] = norms_ref[0]
    vec_ref[8:12, :WIDTH] = norms_ref[1]
    vec_ref[12:13, :HIDDEN] = row(up_ref)
    vec_ref[13:14, :WIDTH] = row(mean_ref)
    vec_ref[14:15, :WIDTH] = row(var_ref)
    units = w1_ref.shape[1]
    net = jnp.concatenate([w1_ref[...], row(b1_ref), w2_ref[...], jnp.zeros((2, units), f32)], 0)
    vec_ref[16:24, :] = net
    lanes = lax.broadcasted_iota(jnp.int32, (1, LANES), 1)
    hidden, _ = bias_net(net, coords_ref[...])
    gate = 1.0 / (1.0 + jnp.exp(-exact(head_rows(net), hidden)))
    gate_ref[...] = 16.0 * gate * (1.0 - gate)
    spots = one_hot(target_ref[...])
    tiles = add_parts(dot(three_parts(16.0 * gate), spots))
    scale_ref[...] = jnp.zeros_like(scale_ref)
    for h in range(HEADS):
        scale = jnp.exp(jnp.full((1, LANES), log_scale_ref[h], f32))
        scale_ref[h : h + 1, :] = scale
        tile = jnp.concatenate(
            [tiles[h : h + 1, r * LANES : (r + 1) * LANES] for r in range(WINDOW)], 0
        )
        columns = []
        for j in range(WINDOW):
            turned = pltpu.roll(tile, (72 + 8 * j) % LANES, 1)
            columns.append(jnp.where(lanes < PLACES, turned, pltpu.roll(turned, PLACES, 1)))
        bias_ref[h] = jnp.concatenate(columns, 0) - (scale + 16.0)


def prepare(x, ct, log_scale, regions, vectors, coords, target):
    units = vectors[-1].shape[1]
    items, rows, flat = x.shape
    half = flat // 2
    part_items = items // PARTS
    shapes = [
        (8, LANES),
        (HEADS, PLACES, LANES),
        (24, units),
        (8, OFFSETS),
    ]
    shapes = [jax.ShapeDtypeStruct(a, f32) for a in shapes]
    flags = jax.ShapeDtypeStruct((regions.shape[0] // WINDOW, regions.shape[2]), jnp.int32)
    shapes = [flags, *shapes]
    shapes += [
        jax.ShapeDtypeStruct((part_items, c, half), f32)
        for _ in range(1, PARTS)
        for c in (24, 8, 8)
    ]
    inputs = (regions, *vectors, coords, target)
    parts = []
    for n in range(1, PARTS):
        parts += [pl.BlockSpec((part_items, rows, half), lambda i, n=n: (n, 0, 0))] * 2
        parts += [pl.BlockSpec((part_items, 8, half), lambda i, n=n: (n, 0, 1))] * 2
    *made, = pl.pallas_call(
        partial(prepare_kernel, PARTS - 1),
        grid=(1,),
        in_specs=[pl.BlockSpec(memory_space=pltpu.SMEM)] + [whole(a) for a in inputs] + parts,
        out_specs=[whole(a) for a in shapes],
        out_shape=shapes,
        cost_estimate=about(0),
        compiler_params=in_order,
    )(log_scale, *inputs, *([x, ct, x, ct] * (PARTS - 1)))
    return made[:5], [made[5 + 3 * n : 8 + 3 * n] for n in range(PARTS - 1)]


def packed(w):
    hi, lo = split(w)
    return jnp.concatenate([hi, lo, hi], 1)


def stack_rows(hi, lo):
    return jnp.concatenate([hi, lo], 0)


def block_kernel(
    step_items,
    first_item,
    token_count,
    is_first,
    is_last,
    flags_ref,
    lead_ref,
    side_ref,
    x_own,
    x_right,
    x_down,
    x_corner,
    ct_own,
    stats_ref,
    w_qkv_ref,
    w_out_ref,
    w_up_ref,
    w_down_ref,
    scale_ref,
    base_ref,
    vec_ref,
    *refs,
):
    step = pl.program_id(0)
    if is_last:
        (gate_ref, coords_ref, target_ref), refs = refs[:3], refs[3:]
    refs, scratch = refs[:-11], refs[-11:]
    qkv_f, out_f, up_f, down_f, down_b, up_b, out_b, qkv_b, cols_ref, up_cols_ref, bias_ref = scratch
    count = len(totals_shapes)
    so_far, refs = (refs[:0], refs) if is_first else (refs[:count], refs[count:])
    out_keep, dn_keep, send_right, send_down, send_corner = refs[:5]
    refs = refs[5:]
    if is_last:
        own_ref, give_ref, norm_ref, affine_ref, flat_ref = refs[:5]
        refs = refs[5:]
    else:
        (affine_ref, sums_ref), refs = refs[-2:], refs[:-2]
        passed_ref = refs[4]
        refs = (*refs[:4], sums_ref, *refs[5:])
    g_qkv_ref, g_out_ref, g_up_ref, g_down_ref, sums_ref, dpos_ref, dcos_ref = refs

    @pl.when(step == 0)
    def _():
        every = stats_ref[...]
        devices = every.shape[0]
        means, squares = every[:, 0, :LANES], every[:, 0, LANES:]
        mean = jnp.sum(means, 0, keepdims=True) * (1.0 / devices)
        apart = means - mean
        var = (
            jnp.sum(squares, 0, keepdims=True) * (1.0 / token_count)
            + jnp.sum(apart * apart, 0, keepdims=True) * (1.0 / devices)
        )
        inv_std = lax.rsqrt(var + norm_eps)
        affine_ref[0] = jnp.broadcast_to(mean, (LANES, LANES)).T[:WIDTH]
        affine_ref[1] = jnp.broadcast_to(inv_std, (LANES, LANES)).T[:WIDTH]
        if is_last:
            pad = jnp.zeros((2, LANES - WIDTH), f32)
            running = jnp.concatenate([vec_ref[13:15, :WIDTH], pad], 1)
            norm_ref[0:1] = mean
            norm_ref[1:2] = inv_std
            norm_ref[2:3] = (1.0 - momentum) * running[0:1] + momentum * mean
            norm_ref[3:4] = (1.0 - momentum) * running[1:2] + momentum * var * (
                token_count / (token_count - 1.0)
            )
            norm_ref[4:8] = jnp.zeros((4, LANES), f32)
        for n, ref in enumerate(refs):
            ref[...] = jnp.zeros_like(ref) if is_first or n == 4 else so_far[n][...]
        qkv_f[...] = packed(w_qkv_ref[...].T)
        qkv_b[...] = packed(w_qkv_ref[...])
        out_f[...] = packed(w_out_ref[...].T)
        out_b[...] = packed(w_out_ref[...])
        up_f[...] = packed(w_up_ref[...].T)
        up_b[...] = packed(w_up_ref[...])
        down_b[...] = packed(w_down_ref[...].T)
        down_f[...] = packed(w_down_ref[...])
        for i in range(cols_ref.shape[0]):
            cols_ref[i] = jnp.broadcast_to(vec_ref[i : i + 1, :WIDTH], (LANES, WIDTH)).T
        up_cols_ref[...] = jnp.broadcast_to(vec_ref[12:13, :HIDDEN], (LANES, HIDDEN)).T
        place = lax.broadcasted_iota(jnp.int32, (PLACES, LANES), 0)
        other = lax.broadcasted_iota(jnp.int32, (PLACES, LANES), 1) % PLACES
        apart_r = (place % WINDOW < SHIFT) != (other % WINDOW < SHIFT)
        apart_c = (place // WINDOW < SHIFT) != (other // WINDOW < SHIFT)
        for h in range(HEADS):
            bias = base_ref[h]
            bias_ref[0, h] = bias
            bias_ref[1, h] = jnp.where(apart_c, masked_score, bias)
            bias_ref[2, h] = jnp.where(apart_r, masked_score, bias)
            bias_ref[3, h] = jnp.where(apart_r | apart_c, masked_score, bias)

    first_half = lax.broadcasted_iota(jnp.int32, (1, PAIR), 1) < PLACES

    def product(weight, x_hi, x_lo):
        return dot(weight[...], jnp.concatenate([x_hi, x_hi, x_lo], 0))

    def halves(v):
        m = v.shape[0] // 2
        return jnp.where(first_half, v[:m], v[m:])

    def col(i):
        return cols_ref[i]

    def per_item(fn):
        return jnp.concatenate([fn(m) for m in range(step_items)], 1)

    def spread_cols(i):
        c = col(i)
        return jnp.concatenate([c] * step_items, 1)

    def gather(own, part, m):
        right, down = 12 * part, 4 * part
        top_l = own[m, SHIFT : SHIFT + WINDOW, :]
        top_r = x_right[m, right : right + WINDOW, :]
        low_l = jnp.concatenate([own[m, SHIFT + WINDOW :, :], x_down[m, down : down + SHIFT, :]], 0)
        low_r = jnp.concatenate(
            [x_right[m, right + WINDOW : right + 12, :], x_corner[m, down : down + SHIFT, :]], 0
        )
        tiles = [
            side[:, j * WIDTH : (j + 1) * WIDTH]
            for side in (top_l, top_r, low_l, low_r)
            for j in range(4)
        ]
        return jnp.concatenate(tiles, 0).T

    def scatter(value, keep, part, m):
        rows = value.T
        sides = [
            jnp.concatenate([rows[(4 * s + j) * 8 : (4 * s + j + 1) * 8] for j in range(4)], 1)
            for s in range(4)
        ]
        right, down = 12 * part, 4 * part
        keep[m, 0:WINDOW, :] = sides[0]
        keep[m, WINDOW:, :] = sides[2][:SHIFT]
        send_right[m, right : right + WINDOW, :] = sides[1]
        send_right[m, right + WINDOW : right + 12, :] = sides[3][:SHIFT]
        send_down[m, down : down + SHIFT, :] = sides[2][SHIFT:]
        send_corner[m, down : down + SHIFT, :] = sides[3][SHIFT:]

    def mean_rows(v):
        return jnp.sum(v, 0, keepdims=True) * (1.0 / WIDTH)

    def layer_norm(v):
        centred = v - mean_rows(v)
        rstd = lax.rsqrt(mean_rows(centred * centred) + norm_eps)
        return centred * rstd, rstd

    items = [first_item + step * step_items + m for m in range(step_items)]
    leads = [(lead_ref[i] + 1).astype(f32) * (1.0 / LEAD_STEPS) for i in items]
    raw = per_item(lambda m: gather(x_own, 0, m))
    mean = jnp.concatenate([affine_ref[0]] * step_items, 1)
    inv_std = jnp.concatenate([affine_ref[1]] * step_items, 1)
    normed = (raw - mean) * inv_std
    n_hi, n_lo = split(normed)

    joined = product(qkv_f, n_hi, n_lo)
    query = joined[:WIDTH] + spread_cols(0)
    key = joined[WIDTH : 2 * WIDTH]
    value = joined[2 * WIDTH :] + spread_cols(1)

    def unit(v):
        rows, inverses = [], []
        for h in range(HEADS):
            part = v[h * HEAD_DIM : (h + 1) * HEAD_DIM]
            inverse = lax.rsqrt(jnp.sum(part * part, 0, keepdims=True) + unit_eps)
            rows.append(part * inverse)
            inverses.append(inverse)
        return rows, inverses

    q_rows, q_inv = unit(query)
    k_rows, k_inv = unit(key)
    v_rows = [value[h * HEAD_DIM : (h + 1) * HEAD_DIM] for h in range(HEADS)]

    def of_item(v, m):
        return v[:, m * PAIR : (m + 1) * PAIR]

    def three(a_hi, a_lo, b_hi, b_lo):
        left = jnp.concatenate([a_hi, a_lo, a_hi], 0)
        right = jnp.concatenate([b_hi, b_hi, b_lo], 0)
        return halves(dot(left.T, right))

    def apart(x):
        zero = jnp.zeros_like(x)
        return jnp.concatenate(
            [jnp.where(first_half, x, zero), jnp.where(first_half, zero, x)], 0
        )

    def two_rows(v_hi, v_lo):
        return jnp.concatenate(
            [
                jnp.concatenate([v_hi, v_hi], 1),
                jnp.concatenate([v_lo, jnp.zeros_like(v_lo)], 1),
            ],
            0,
        )

    def over_keys(v_hi, v_lo, e_hi, e_lo):
        r = dot(two_rows(v_hi, v_lo), stack_rows(apart(e_hi), apart(e_lo)))
        return r[:HEAD_DIM] + r[HEAD_DIM:]

    def over_queries(v_hi, v_lo, e_hi, e_lo):
        weights = jnp.concatenate([e_hi, e_lo], 1)
        r = dot_rows(two_rows(apart(v_hi), apart(v_lo)), stack_rows(weights, weights))
        return halves(r[:PLACES] + r[PLACES:])

    pairs = [(m, h) for m in range(step_items) for h in range(HEADS)]
    q_parts = [split(of_item(q_rows[h], m)) for m, h in pairs]
    k_parts = [split(of_item(k_rows[h], m)) for m, h in pairs]
    v_parts = [split(of_item(v_rows[h], m)) for m, h in pairs]
    cosines = [three(*k, *q) for k, q in zip(k_parts, q_parts)]
    expos, inverses = [], []
    for (m, h), cosine in zip(pairs, cosines):
        flag0, flag1 = flags_ref[0, items[m]], flags_ref[1, items[m]]
        offset = jnp.where(first_half, bias_ref[flag0, h], bias_ref[flag1, h])
        expo = jnp.exp(cosine * scale_ref[h : h + 1, :] + offset)
        expos.append(expo)
        inverses.append(1.0 / jnp.sum(expo, 0, keepdims=True))
    e_parts = [split(e) for e in expos]
    mixes = [
        over_keys(*v, *e) * inverse for v, e, inverse in zip(v_parts, e_parts, inverses)
    ]
    mixed = jnp.concatenate(
        [jnp.concatenate(mixes[HEADS * m : HEADS * (m + 1)], 0) for m in range(step_items)], 1
    )

    o_hi, o_lo = split(mixed)
    attn_hat, attn_rstd = layer_norm(product(out_f, o_hi, o_lo) + spread_cols(2))

    def gain(base):
        return per_item(lambda m: 1.0 + col(base) + leads[m] * col(base + 1))

    def shift(base):
        return per_item(lambda m: col(base + 2) + leads[m] * col(base + 3))

    gain0 = gain(4)
    first = normed + attn_hat * gain0 + shift(4)
    f_hi, f_lo = split(first)

    up_bias = jnp.concatenate([up_cols_ref[...]] * step_items, 1)
    size = HIDDEN // 2 if is_first else HIDDEN
    slopes, h_parts = [], []
    for c in range(0, HIDDEN, size):
        u = product(up_f.at[c : c + size, :], f_hi, f_lo) + up_bias[c : c + size]
        phi, bell = normal_parts(u)
        slopes.append(phi + bell)
        h_parts.append(split(u * phi))
    h_hi, h_lo = (jnp.concatenate(p, 0) for p in zip(*h_parts))
    branch = product(down_f, h_hi, h_lo) + spread_cols(3)
    hat, rstd = layer_norm(branch)
    gain1 = gain(8)
    out = first + hat * gain1 + shift(8)
    for m in range(step_items):
        scatter(of_item(out, m), out_keep, 0, m)

    def norm_back(g, hat, rstd, gain, base):
        weighted = g * hat
        for m in range(step_items):
            a, b = of_item(weighted, m), of_item(g, m)
            sums_ref[base] += a
            sums_ref[base + 1] += leads[m] * a
            sums_ref[base + 2] += b
            sums_ref[base + 3] += leads[m] * b
        e = g * gain
        return (e - mean_rows(e) - hat * mean_rows(e * hat)) * rstd

    def add_items(v):
        total = of_item(v, 0)
        for m in range(1, step_items):
            total = total + of_item(v, m)
        return total

    ones_rows = jnp.where(
        lax.broadcasted_iota(jnp.int32, (LANES - WIDTH, step_items * PAIR), 0) == 0, 1.0, 0.0
    ).astype(bf16)
    zero_rows = jnp.zeros((LANES - WIDTH, step_items * PAIR), bf16)

    def outer(a_hi, a_lo, b_hi, b_lo):
        right = jnp.concatenate([b_hi, ones_rows, b_lo, zero_rows], 0)
        r = dot_rows(stack_rows(a_hi, a_lo), right)
        m = a_hi.shape[0]
        return (r[:m, :LANES] + r[m:, :LANES]) + r[:m, LANES:]

    cot = per_item(lambda m: gather(ct_own, 1, m))
    d_branch = norm_back(cot, hat, rstd, gain1, 4)
    sums_ref[8] += add_items(d_branch)
    z_hi, z_lo = split(d_branch)
    g_down_ref[...] += outer(h_hi, h_lo, z_hi, z_lo)
    p_parts = [
        split(product(down_b.at[c : c + size, :], z_hi, z_lo) * slopes[c // size])
        for c in range(0, HIDDEN, size)
    ]
    p_hi, p_lo = (jnp.concatenate(p, 0) for p in zip(*p_parts))
    g_up_ref[...] += outer(p_hi, p_lo, f_hi, f_lo)
    d_first = cot + product(up_b, p_hi, p_lo)
    d_attn = norm_back(d_first, attn_hat, attn_rstd, gain0, 0)
    a_hi, a_lo = split(d_attn)
    g_out_ref[...] += outer(a_hi, a_lo, o_hi, o_lo)
    d_mixed = product(out_b, a_hi, a_lo)

    d_outs = [
        of_item(d_mixed, m)[h * HEAD_DIM : (h + 1) * HEAD_DIM] * inverse
        for (m, h), inverse in zip(pairs, inverses)
    ]
    d_parts = [split(d) for d in d_outs]
    d_probs = [three(*v, *d) for v, d in zip(v_parts, d_parts)]
    s_parts = []
    for n, (m, h) in enumerate(pairs):
        delta = jnp.sum(d_outs[n] * mixes[n], 0, keepdims=True)
        d_scores = expos[n] * (d_probs[n] - delta)
        dpos_ref[h] += d_scores
        folded = d_scores * cosines[n]
        total = folded[0:8]
        for i in range(1, PLACES // 8):
            total = total + folded[8 * i : 8 * i + 8]
        dcos_ref[h] += total
        s_parts.append(split(d_scores))
    dv_rows = [over_queries(*d, *e) for d, e in zip(d_parts, e_parts)]
    dk_rows = [over_queries(*q, *d) for q, d in zip(q_parts, s_parts)]
    dq_rows = [over_keys(*k, *d) for k, d in zip(k_parts, s_parts)]

    def unit_back(grads, rows, inverse):
        out = []
        for n, (m, h) in enumerate(pairs):
            d = grads[n] * scale_ref[h : h + 1, :]
            row = of_item(rows[h], m)
            d = d - row * jnp.sum(row * d, 0, keepdims=True)
            out.append(d * of_item(inverse[h], m))
        return out

    dq_rows = unit_back(dq_rows, q_rows, q_inv)
    dk_rows = unit_back(dk_rows, k_rows, k_inv)
    d_joined = jnp.concatenate(
        [
            jnp.concatenate(
                [d for rows in (dq_rows, dk_rows, dv_rows) for d in rows[HEADS * m : HEADS * (m + 1)]], 0
            )
            for m in range(step_items)
        ],
        1,
    )
    j_hi, j_lo = split(d_joined)
    g_qkv_ref[...] += outer(j_hi, j_lo, n_hi, n_lo)
    d_normed = d_first + product(qkv_b, j_hi, j_lo)
    sums_ref[9] += add_items(d_normed)
    sums_ref[10] += add_items(d_normed * normed)
    for m in range(step_items):
        scatter(of_item(d_normed, m), dn_keep, 1, m)

    def row_sums():
        rows = [jnp.sum(sums_ref[i].T, 0, keepdims=True) for i in range(11)]
        return rows if is_first else [r + so_far[4][i : i + 1, :WIDTH] for i, r in enumerate(rows)]

    def finish():
        flat_ref[...] = jnp.zeros_like(flat_ref)
        g = g_qkv_ref[...].T
        flat_ref[0:96, :] = g[:WIDTH, :LANES]
        flat_ref[96:192, :] = g[:WIDTH, LANES : 2 * LANES]
        qv = g[WIDTH : WIDTH + 1]
        g_out = g_out_ref[...].T
        flat_ref[192:288, :] = jnp.concatenate([g_out[:WIDTH], g[:WIDTH, 2 * LANES :]], 1)
        g_up = g_up_ref[...].T
        g_down = g_down_ref[...].T
        for k in range(3):
            lanes = slice(k * LANES, (k + 1) * LANES)
            flat_ref[288 + 96 * k : 384 + 96 * k, :] = g_up[:WIDTH, lanes]
            flat_ref[576 + 96 * k : 672 + 96 * k, :] = g_down[:WIDTH, lanes]
            flat_ref[876 + k : 877 + k, :] = g_up[WIDTH : WIDTH + 1, lanes]
        totals = row_sums()
        for i in range(8):
            flat_ref[864 + i : 865 + i, :WIDTH] = totals[i]
        flat_ref[872:873, :WIDTH] = totals[8]
        flat_ref[873:874, :WIDTH] = g_out[WIDTH : WIDTH + 1]
        flat_ref[874:875, :WIDTH] = qv[:, :WIDTH]
        flat_ref[875:876, :WIDTH] = qv[:, 2 * WIDTH :]
        lane = lax.broadcasted_iota(jnp.int32, (1, LANES), 1)
        scales = jnp.zeros((1, LANES), f32)
        for h in range(HEADS):
            total = jnp.sum(jnp.sum(dcos_ref[h], 0, keepdims=True), 1, keepdims=True)
            scales = jnp.where(lane == WIDTH + h, total * scale_ref[h : h + 1, :], scales)
        flat_ref[864:865, :] = flat_ref[864:865, :] + scales

        rows = []
        for h in range(HEADS):
            d = dpos_ref[h]
            d = jnp.where(first_half, d + pltpu.roll(d, PLACES, 1), 0.0)
            tile = jnp.zeros((WINDOW, LANES), f32)
            for j in range(WINDOW):
                tile = tile + pltpu.roll(d[8 * j : 8 * j + 8], 56 - 8 * j, 1)
            rows.append(jnp.concatenate([tile[r : r + 1] for r in range(WINDOW)], 1))
        rows.append(jnp.zeros((8 - HEADS, WINDOW * LANES), f32))
        found = dot_rows(three_parts(jnp.concatenate(rows, 0)), one_hot(target_ref[...]))
        d_table = add_parts(found)
        d_logit = d_table * gate_ref[...]

        def against(v, units):
            v_hi, v_lo = split(v)
            u_hi, u_lo = split(units)
            both = jnp.concatenate([v_hi.astype(f32), v_lo.astype(f32)], 0).astype(bf16)
            r = dot_rows(both, u_hi)
            return r[:8] + r[8:] + dot_rows(v_hi, u_lo)

        hidden_units, unit_slope = bias_net(vec_ref[16:24, :], coords_ref[...])
        g_w2 = against(d_logit, hidden_units)
        column = net_columns(vec_ref[16:24, :])
        d_hidden = sum(column(3 + h) * d_logit[h : h + 1] for h in range(HEADS))
        g_first = against(coords_ref[...], d_hidden * unit_slope)
        for i, row in enumerate(
            [g_first[0:1], g_first[1:2], g_first[2:3], g_w2[0:1], g_w2[1:2], g_w2[2:3]]
        ):
            for k in range(4):
                at = 879 + 4 * i + k
                flat_ref[at : at + 1, :] = row[:, k * LANES : (k + 1) * LANES]

        slots, slot_rows, _ = own_ref.shape
        share = slot_rows - 2
        first_side = side_ref[0] == 0
        for j in range(slots):
            near = flat_ref[share * j : share * (j + 1), :]
            far = flat_ref[share * (slots + j) : share * (slots + j + 1), :]
            own_ref[j, 0:share, :] = jnp.where(first_side, near, far)
            give_ref[j, 0:share, :] = jnp.where(first_side, far, near)
        for ref in (own_ref, give_ref):
            for i in range(2):
                ref[:, share + i : share + i + 1, :WIDTH] = jnp.broadcast_to(
                    totals[9 + i][None], (slots, 1, WIDTH)
                )
                ref[:, share + i : share + i + 1, WIDTH:] = jnp.zeros(
                    (slots, 1, LANES - WIDTH), f32
                )

    if is_last:
        finish()
    else:
        for i, row in enumerate(row_sums()):
            passed_ref[i : i + 1, :WIDTH] = row


totals_shapes = [
    (3 * WIDTH, LANES),
    (WIDTH, LANES),
    (HIDDEN, LANES),
    (HIDDEN, LANES),
    (11, WIDTH, LANES),
    (HEADS, PLACES, LANES),
    (HEADS, 8, LANES),
]


def run_block(
    part,
    flags,
    lead,
    side,
    x,
    ct,
    halo,
    stats,
    weights,
    prepared,
    bias_net_parts,
    so_far,
    token_count,
):
    items, tile_rows, flat = x.shape
    half = flat // 2
    items = items // PARTS
    step_items = block_of(items, 16)
    steps = items // step_items
    is_first, is_last = part == 0, part == PARTS - 1

    def rows(n):
        return pl.BlockSpec((step_items, n, half), lambda i: (i, 0, 0))

    smem = pl.BlockSpec(memory_space=pltpu.SMEM)
    field = pl.BlockSpec((step_items, tile_rows, half), lambda i: (part * steps + i, 0, 1))
    out_rows = (12, 12, 24, 8, 8)
    slots = stats.shape[0]
    slot_rows = -(-PAYLOAD // slots)
    slot_rows = -(-(slot_rows + 2) // 8) * 8
    totals = [jax.ShapeDtypeStruct(s, f32) for s in totals_shapes]
    totals[4] = jax.ShapeDtypeStruct((16, LANES), f32)
    scratch = [pltpu.VMEM((2, WIDTH, LANES), f32)]
    if is_last:
        tail = [
            jax.ShapeDtypeStruct((slots // 2, slot_rows, LANES), f32),
            jax.ShapeDtypeStruct((slots // 2, slot_rows, LANES), f32),
            jax.ShapeDtypeStruct((8, LANES), f32),
        ]
        scratch.append(pltpu.VMEM((slots * (slot_rows - 2), LANES), f32))
        scratch += [pltpu.VMEM(s, f32) for s in totals_shapes]
    else:
        tail = totals
        scratch.append(pltpu.VMEM(totals_shapes[4], f32))
    scratch += [
        pltpu.VMEM((3 * WIDTH, 3 * WIDTH), bf16),
        pltpu.VMEM((WIDTH, 3 * WIDTH), bf16),
        pltpu.VMEM((HIDDEN, 3 * WIDTH), bf16),
        pltpu.VMEM((WIDTH, 3 * HIDDEN), bf16),
        pltpu.VMEM((HIDDEN, 3 * WIDTH), bf16),
        pltpu.VMEM((WIDTH, 3 * HIDDEN), bf16),
        pltpu.VMEM((WIDTH, 3 * WIDTH), bf16),
        pltpu.VMEM((WIDTH, 9 * WIDTH), bf16),
        pltpu.VMEM((12, WIDTH, LANES), f32),
        pltpu.VMEM((HIDDEN, LANES), f32),
        pltpu.VMEM((4, HEADS, PLACES, LANES), f32),
    ]
    constants = (stats, *weights, *prepared, *(bias_net_parts if is_last else ()), *so_far)
    return pl.pallas_call(
        partial(block_kernel, step_items, part * items, float(token_count), is_first, is_last),
        grid=(steps,),
        in_specs=[smem, smem, smem, field, rows(24), rows(8), rows(8), field]
        + [whole(a) for a in constants],
        out_specs=[rows(n) for n in out_rows] + [whole(a) for a in tail],
        out_shape=[jax.ShapeDtypeStruct((items, n, half), f32) for n in out_rows] + tail,
        scratch_shapes=scratch,
        cost_estimate=about(40),
        compiler_params=pltpu.CompilerParams(
            dimension_semantics=("arbitrary",), vmem_limit_bytes=65024 * 1024
        ),
    )(flags, lead, side, x, *halo, ct, *constants)


def place(ref_out, m, keep, right, down, corner, part, fn):
    half = keep.shape[2]
    at, low = 12 * part, 4 * part
    for rows, left, own in (
        (slice(0, SHIFT), corner[m, low : low + SHIFT, :], down[m, low : low + SHIFT, :]),
        (slice(SHIFT, 16), right[m, at : at + 12, :], keep[m]),
    ):
        for lanes, value in ((slice(0, half), left), (slice(half, 2 * half), own)):
            ref_out[m, rows, lanes] = fn(value, rows, lanes)


def final_kernel(token_count, part_steps, x_ref, norm_ref, sums_ref, *refs):
    cols = x_ref.shape[2] // WIDTH
    out_ref, grad_ref = refs[-2:]

    def wide(row):
        return jnp.concatenate([row[:, :WIDTH]] * cols, 1)

    mean, inv_std = norm_ref[0:1], norm_ref[1:2]
    at = sums_ref.shape[1] - 2
    mean_grad = sums_ref[0, at : at + 1] * (1.0 / token_count)
    mean_cross = sums_ref[0, at + 1 : at + 2] * (1.0 / token_count)
    factor, centre = wide(inv_std), wide(mean)
    offset, slope = wide(inv_std * mean_grad), wide(inv_std * inv_std * mean_cross)

    def work(out_keep, dn_keep, *halo):
        for m in range(x_ref.shape[0]):

            def grad(v, rows, lanes):
                x = x_ref[m, rows, lanes] - centre[:, lanes]
                return factor[:, lanes] * v - offset[:, lanes] - x * slope[:, lanes]

            place(out_ref, m, out_keep, *halo, 0, lambda v, rows, lanes: v)
            place(grad_ref, m, dn_keep, *halo, 1, grad)

    for n in range(PARTS):
        pl.when(pl.program_id(0) // part_steps == n)(partial(work, *refs[5 * n : 5 * n + 5]))


def finish_fields(x, parts, norm, sums, token_count):
    items, rows, flat = x.shape
    step_items = block_of(items // PARTS, 16)
    part_steps = items // PARTS // step_items

    def spec(part, n):
        return pl.BlockSpec(
            (step_items, n, flat // 2),
            lambda i: (jnp.clip(i - part * part_steps, 0, part_steps - 1), 0, 0),
        )

    field = pl.BlockSpec((step_items, rows, flat), lambda i: (i, 0, 0))
    return pl.pallas_call(
        partial(final_kernel, float(token_count), part_steps),
        grid=(items // step_items,),
        in_specs=[
            field,
            whole(norm),
            pl.BlockSpec((1,) + sums.shape[1:], lambda i: (0, 0, 0)),
        ]
        + [spec(part, n) for part in range(PARTS) for n in (12, 12, 24, 8, 8)],
        out_specs=[field] * 2,
        out_shape=[jax.ShapeDtypeStruct(x.shape, f32)] * 2,
        cost_estimate=about(60),
        compiler_params=in_order,
    )(x, norm, sums, *[a for part in parts for a in part])


def sum_slots_kernel(slots_ref, all_ref):
    total = slots_ref[0]
    for j in range(1, slots_ref.shape[0]):
        total = total + slots_ref[j]
    all_ref[...] = jnp.broadcast_to(total[None], all_ref.shape)


def sum_slots(slots):
    return pl.pallas_call(
        sum_slots_kernel,
        grid=(1,),
        in_specs=[whole(slots)],
        out_specs=whole(slots),
        out_shape=jax.ShapeDtypeStruct(slots.shape, f32),
        compiler_params=pltpu.CompilerParams(vmem_limit_bytes=16 * 1024 * 1024),
    )(slots)


def unpack_kernel(
    side_ref,
    mine_ref,
    other_ref,
    qkv_ref,
    qv_ref,
    scale_ref,
    w1_ref,
    b1_ref,
    w2_ref,
    out_ref,
    b_out_ref,
    up_ref,
    b_up_ref,
    down_ref,
    b_down_ref,
    norm_ref,
    flat_ref,
):
    slots, slot_rows, _ = mine_ref.shape
    share = slot_rows - 2
    first_side = side_ref[0] == 0
    for j in range(slots):
        mine, other = mine_ref[j, 0:share, :], other_ref[j, 0:share, :]
        flat_ref[share * j : share * (j + 1), :] = jnp.where(first_side, mine, other)
        flat_ref[share * (slots + j) : share * (slots + j + 1), :] = jnp.where(
            first_side, other, mine
        )
    qkv_ref[:, 0:LANES] = flat_ref[0:96, :]
    qkv_ref[:, LANES : 2 * LANES] = flat_ref[96:192, :]
    qkv_ref[:, 2 * LANES :] = flat_ref[192:288, WIDTH:]
    out_ref[...] = flat_ref[192:288, :WIDTH]
    for k in range(3):
        lanes = slice(k * LANES, (k + 1) * LANES)
        up_ref[:, lanes] = flat_ref[288 + 96 * k : 384 + 96 * k, :]
        down_ref[:, lanes] = flat_ref[576 + 96 * k : 672 + 96 * k, :]
        b_up_ref[k : k + 1, :] = flat_ref[876 + k : 877 + k, :]
    norm_ref[...] = flat_ref[864:872, :WIDTH]
    scale_ref[...] = flat_ref[864:865, WIDTH : WIDTH + HEADS]
    b_down_ref[...] = flat_ref[872:873, :WIDTH]
    b_out_ref[...] = flat_ref[873:874, :WIDTH]
    qv_ref[...] = flat_ref[874:876, :WIDTH]
    for k in range(4):
        lanes = slice(k * LANES, (k + 1) * LANES)
        for i in range(2):
            w1_ref[i : i + 1, lanes] = flat_ref[879 + 4 * i + k : 880 + 4 * i + k, :]
        b1_ref[:, lanes] = flat_ref[887 + k : 888 + k, :]
        for i in range(3):
            w2_ref[i : i + 1, lanes] = flat_ref[891 + 4 * i + k : 892 + 4 * i + k, :]


def unpack(side, mine, other):
    slots, slot_rows, _ = mine.shape
    shapes = [
        (WIDTH, 3 * WIDTH),
        (2, WIDTH),
        (1, HEADS),
        (2, 512),
        (1, 512),
        (HEADS, 512),
        (WIDTH, WIDTH),
        (1, WIDTH),
        (WIDTH, HIDDEN),
        (3, LANES),
        (WIDTH, HIDDEN),
        (1, WIDTH),
        (8, WIDTH),
    ]
    shapes = [jax.ShapeDtypeStruct(s, f32) for s in shapes]
    return pl.pallas_call(
        unpack_kernel,
        grid=(1,),
        in_specs=[pl.BlockSpec(memory_space=pltpu.SMEM), whole(mine), whole(other)],
        out_specs=[whole(a) for a in shapes],
        out_shape=shapes,
        compiler_params=pltpu.CompilerParams(vmem_limit_bytes=16 * 1024 * 1024),
        scratch_shapes=[pltpu.VMEM((2 * slots * (slot_rows - 2), LANES), f32)],
    )(side, mine, other)


def take_from(block, dy, dx):
    rows, cols = lax.axis_size("ty"), lax.axis_size(("th", "tl"))
    route = []
    for i in range(rows * cols):
        y, x = divmod(i, cols)
        route.append((((y + dy) % rows) * cols + (x + dx) % cols, i))
    return lax.ppermute(block, axes_tiles, route)


def exchange(slots, axes):
    return lax.all_to_all(slots, axes, 0, 0, tiled=True)


def swap(block):
    return lax.ppermute(block, "tl", [(0, 1), (1, 0)])


def shards(
    inputs,
    regions,
    lead_step_index,
    running_channel_mean,
    running_channel_variance,
    query_key_value_weight,
    query_value_bias,
    log_cosine_scale,
    bias_net_weight1,
    bias_net_bias1,
    bias_net_weight2,
    output_weight,
    projection_bias,
    up_weight,
    up_bias,
    down_weight,
    down_bias,
    conditioned_norm_values,
    cotangent,
):
    items, tile_rows, flat = inputs.shape
    devices = lax.axis_size(axes_all)
    token_count = items * tile_rows * (flat // WIDTH) * devices

    stats, sent = pack(inputs, cotangent, devices)
    stats = exchange(stats, axes_all)
    side = lax.axis_index("tl").astype(jnp.int32).reshape(1)

    vectors = (
        query_value_bias,
        projection_bias,
        down_bias,
        conditioned_norm_values,
        up_bias,
        running_channel_mean,
        running_channel_variance,
        bias_net_weight1,
        bias_net_bias1,
        bias_net_weight2.T,
    )
    coords, target = offset_constants()
    weights = (query_key_value_weight, output_weight, up_weight, down_weight)
    corners = regions.transpose(1, 2, 0)
    (flags, *prepared, gate), sent_later = prepare(
        inputs, cotangent, log_cosine_scale, corners, vectors, coords, target
    )
    halos = []
    for right, down, corner in (sent, *sent_later):
        if halos:
            (right, down, corner), halos[-1] = lax.optimization_barrier(
                ((right, down, corner), halos[-1])
            )
        halos.append((take_from(right, 0, 1), take_from(down, 1, 0), take_from(corner, 1, 1)))
    bias_net_parts = (gate, coords, target)
    totals, out_parts, dn_parts, home = [], [], [], []
    for part in range(PARTS):
        out_keep, dn_keep, right, down, corner, *totals = run_block(
            part,
            flags,
            lead_step_index,
            side,
            inputs,
            cotangent,
            halos[part],
            stats,
            weights,
            prepared,
            bias_net_parts,
            totals,
            token_count,
        )
        home.append((take_from(right, 0, -1), take_from(down, -1, 0), take_from(corner, -1, -1)))
        out_parts.append(out_keep)
        dn_parts.append(dn_keep)
    own, give, norm = totals
    give, home[:-1] = lax.optimization_barrier((give, home[:-1]))
    shares = sum_slots(exchange(own + swap(give), axes_far))
    outputs, grad_inputs = finish_fields(
        inputs,
        [(o, d, *h) for o, d, h in zip(out_parts, dn_parts, home)],
        norm,
        shares,
        token_count,
    )
    mine = exchange(shares, axes_far)
    mine, outputs, grad_inputs = lax.optimization_barrier((mine, outputs, grad_inputs))
    other = swap(mine)
    (
        g_qkv,
        g_qv,
        g_scale,
        g_w1,
        g_b1,
        g_w2,
        g_out,
        g_b_out,
        g_up,
        g_b_up,
        g_down,
        g_b_down,
        g_norm,
    ) = unpack(side, mine, other)
    return (
        outputs,
        grad_inputs,
        g_qkv,
        g_qv,
        g_scale.reshape(-1),
        g_w1,
        g_b1.reshape(-1),
        g_w2.T,
        g_out,
        g_b_out.reshape(-1),
        g_up,
        g_b_up.reshape(-1),
        g_down,
        g_b_down.reshape(-1),
        g_norm.reshape(2, 4, WIDTH),
        norm[2, :WIDTH],
        norm[3, :WIDTH],
    )


def solution(mesh):
    rows, cols, depth = (mesh.shape[a] for a in ("ty", "tx", "items"))
    split_mesh = jax.sharding.Mesh(mesh.devices.reshape(rows, cols // 2, 2, depth), axes_all)
    tiled = P("items", "ty", ("th", "tl"))
    placed = (tiled, tiled, P("items")) + (P(),) * 15 + (tiled,)
    return jax.shard_map(
        shards,
        mesh=split_mesh,
        in_specs=placed,
        out_specs=(tiled, tiled) + (P(),) * 15,
        check_vma=False,
    )
```
